32 devices in a mesh: dp: 4 (over z), ctx: 2 (over core), tensor: 4 (over y, x).
Axes of the slice: x: 2, y: 2, z: 4, core: 2. Of those that a mesh axis runs over, the one named last changes fastest.
Arguments:
- inputs: bfloat16 [8192, 2048], P(('dp', 'ctx'), 'tensor'), may hold values from -6 to 6
- cotangent: bfloat16 [8192, 2048], P(('dp', 'ctx'), 'tensor'), may hold values from -6 to 6
- doc_lengths: int32 [4, 7], P('dp'), may hold values from 0 to 1024, as said below
- attn_weights: float32 [4, 2048, 2048], P(None, ('dp', 'ctx'), 'tensor'), may hold values from -0.125 to 0.125
- mlp_weights: float32 [3, 2048, 8192], P(None, ('dp', 'ctx'), 'tensor'), may hold values from -0.125 to 0.125
- norm_gains: float32 [4, 2048], P(None, ('tensor', 'dp', 'ctx')), may hold values from 0.25 to 2.6
- attn_first: float32 [4, 2048, 2048], P(None, ('dp', 'ctx'), 'tensor'), may hold values from -128 to 128
- attn_second: float32 [4, 2048, 2048], P(None, ('dp', 'ctx'), 'tensor'), may hold values from 1720.32 to 6881.28
- mlp_first: float32 [3, 2048, 8192], P(None, ('dp', 'ctx'), 'tensor'), may hold values from -48 to 48
- mlp_second: float32 [3, 2048, 8192], P(None, ('dp', 'ctx'), 'tensor'), may hold values from 245.76 to 983.04
- gain_first: float32 [4, 2048], P(None, ('tensor', 'dp', 'ctx')), may hold values from -64 to 64
- gain_second: float32 [4, 2048], P(None, ('tensor', 'dp', 'ctx')), may hold values from 622.592 to 2457.6
Outputs:
- block_out: bfloat16 [8192, 2048], P(('dp', 'ctx'), 'tensor')
- grad_inputs: float32 [8192, 2048], P(('dp', 'ctx'), 'tensor')
- new_attn: float32 [4, 2048, 2048], P(None, ('dp', 'ctx'), 'tensor')
- attn_one: float32 [4, 2048, 2048], P(None, ('dp', 'ctx'), 'tensor')
- attn_two: float32 [4, 2048, 2048], P(None, ('dp', 'ctx'), 'tensor')
- new_mlp: float32 [3, 2048, 8192], P(None, ('dp', 'ctx'), 'tensor')
- mlp_one: float32 [3, 2048, 8192], P(None, ('dp', 'ctx'), 'tensor')
- mlp_two: float32 [3, 2048, 8192], P(None, ('dp', 'ctx'), 'tensor')
- new_gains: float32 [4, 2048], P(None, ('tensor', 'dp', 'ctx'))
- gain_one: float32 [4, 2048], P(None, ('tensor', 'dp', 'ctx'))
- gain_two: float32 [4, 2048], P(None, ('tensor', 'dp', 'ctx'))
The draws below stay inside these ranges and needn't reach their ends.
Inputs may be any that keep to these rules, and one draw needn't show every extreme that they name: `doc_lengths`: each row sums to 2048; its fourth entry is 1024, a document with tokens on both devices of ctx.
All inputs are finite; a program needn't handle non-finite values.
Results may differ from the reference program's by a relative error of at most 0.025.
The reference program's roundings to bfloat16 on the way count: a program that leaves them out, or rounds other values in their place, can miss the bound.
Values may be sent and summed in bfloat16 or wider, within the bound.
No kernel may reach another device: no remote copies, remote signals or barrier semaphores. Data moves between devices by JAX's collectives and lax.ppermute only.
A program may use at most 320 MiB of HBM per device.

```python
import math
import jax
import jax.numpy as jnp
from jax import lax

D = 2048
HEADS = 16
HEAD_DIM = 128
FF = 8192
ROWS = 1024
STEP = 10
TOKENS = 8192
N_DP = 4
N_CTX = 2


def draw_doc_lengths(key, part):
    key = jax.random.fold_in(key, 11)
    start_key, left_key, right_key = jax.random.split(key, 3)
    cross_start = jax.random.randint(start_key, (N_DP, 1), 1, ROWS)
    right_len = ROWS - cross_start
    left_cuts = jnp.sort(jax.random.randint(left_key, (N_DP, 2), 0, cross_start + 1), axis=1)
    right_cuts = jnp.sort(jax.random.randint(right_key, (N_DP, 2), 0, right_len + 1), axis=1)
    longest = jnp.full((N_DP, 1), ROWS, dtype=jnp.int32)
    pieces = [left_cuts[:, :1], left_cuts[:, 1:] - left_cuts[:, :1], cross_start - left_cuts[:, 1:], longest, right_cuts[:, :1], right_cuts[:, 1:] - right_cuts[:, :1], right_len - right_cuts[:, 1:]]
    return jnp.concatenate(pieces, axis=1).astype(jnp.int32)


def draw_norm_gains(key, part):
    key = jax.random.fold_in(key, 5)
    fraction = jnp.arange(D, dtype=jnp.float32) / D
    ramp = 0.5 + fraction
    factor = jax.random.uniform(key, (4, D), jnp.float32, 0.8, 1.2)
    return ramp[None, :] * factor


def levels(rng, shape, cuts, least, largest):
    gain, own = 1.0, jax.random.fold_in(rng, 6)
    for dim, blocks in cuts:
        heights = jnp.exp(jax.random.uniform(jax.random.fold_in(own, dim), (blocks,), jnp.float32, least / len(cuts), largest / len(cuts)))
        gain = gain * jnp.repeat(heights, shape[dim] // blocks).reshape([-1 if axis == dim else 1 for axis in range(len(shape))])
    return gain


def scatter_about(rng, dims, scale, most, shards=(), kind=jnp.bfloat16):
    values = jax.random.normal(rng, dims, jnp.float32) * scale
    if len(shards) > 0:
        values = levels(rng, dims, shards, -0.22, 0.18) * values
    return jnp.clip(values, min=-most, max=most).astype(kind)


def setup_inputs(seed: int = 0) -> dict:
    keys = jax.random.split(jax.random.key(seed), 13)
    return {
        "inputs": scatter_about(keys[0], (TOKENS, D), 1.0, 6.0, ((0, 8), (1, 4))),
        "cotangent": scatter_about(keys[1], (TOKENS, D), 1.0, 6.0, ((0, 8), (1, 4))),
        "doc_lengths": draw_doc_lengths(jax.random.fold_in(keys[12], 71), 0),
        "attn_weights": scatter_about(keys[3], (4, D, D), D ** -0.5, 0.125, ((1, 8), (2, 4)), jnp.float32),
        "mlp_weights": scatter_about(keys[4], (3, D, FF), D ** -0.5, 0.125, ((1, 8), (2, 4)), jnp.float32),
        "norm_gains": draw_norm_gains(jax.random.fold_in(keys[12], 71), 0),
        "attn_first": scatter_about(keys[6], (4, D, D), (0.22 * TOKENS ** 0.5), 128.0, ((1, 8), (2, 4)), jnp.float32),
        "attn_second": jnp.clip(jnp.exp(math.log(6881.28) - 1.3862944 * jax.random.uniform(keys[7], (4, D, D), jnp.float32) ** levels(keys[7], (4, D, D), ((1, 8), (2, 4)), -0.2, 0.2)), 1720.32, 6881.28),
        "mlp_first": scatter_about(keys[8], (3, D, FF), (0.083 * TOKENS ** 0.5), 48.0, ((1, 8), (2, 4)), jnp.float32),
        "mlp_second": jnp.clip(jnp.exp(math.log(983.04) - 1.3862944 * jax.random.uniform(keys[9], (3, D, FF), jnp.float32) ** levels(keys[9], (3, D, FF), ((1, 8), (2, 4)), -0.2, 0.2)), 245.76, 983.04),
        "gain_first": scatter_about(keys[10], (4, D), (0.13 * TOKENS ** 0.5), 64.0, ((1, 32),), jnp.float32),
        "gain_second": jnp.clip(jnp.exp(math.log(2457.6) - 1.3730492 * jax.random.uniform(keys[11], (4, D), jnp.float32) ** levels(keys[11], (4, D), ((1, 32),), -0.2, 0.2)), 622.592, 2457.6),
    }


@jax.custom_vjp
def low(v):
    return lax.optimization_barrier(v.astype(jnp.bfloat16)).astype(jnp.float32)

@jax.custom_vjp
def low_back(v):
    return v

def low_keep(v):
    return (low(v), None)

def low_pass(kept, grad):
    return (grad,)

def back_keep(v):
    return (v, None)

def back_low(kept, grad):
    return (low(grad),)
low.defvjp(low_keep, low_pass)
low_back.defvjp(back_keep, back_low)
NORM_EPS = 1e-06
ROPE_THETA = 500000.0
BETA_ONE = 0.9
BETA_TWO = 0.95
ADAM_EPS = 1e-08
WEIGHT_DECAY = 0.1
LEARN_RATE = 0.02
GAIN_RATE = 1.0
PRECISE = lax.Precision.HIGHEST

def doc_layout(doc_row, token_place):
    doc_ends = jnp.cumsum(doc_row).astype(jnp.int32)
    passed = token_place[:, None] >= doc_ends[None, :]
    segment = lax.optimization_barrier(jnp.sum(passed.astype(jnp.int32), axis=1)).astype(jnp.int32)
    doc_begin = lax.optimization_barrier(jnp.max(jnp.where(passed, doc_ends[None, :], jnp.zeros_like(doc_ends)[None, :]), axis=1))
    return (segment, (token_place - doc_begin).astype(jnp.int32))

def rotate(values, position, turn):
    half_dim = values.shape[-1] // 2
    frequency = ROPE_THETA ** (-2.0 * jnp.arange(half_dim, dtype=jnp.float32) / values.shape[-1])
    angles = position.astype(jnp.float32)[:, None] * frequency[None, :]
    cosine = jnp.cos(angles)[:, None, :]
    sine = turn * jnp.sin(angles)[:, None, :]
    front = values[..., :half_dim]
    back_half = values[..., half_dim:]
    return jnp.concatenate([front * cosine - back_half * sine, back_half * cosine + front * sine], axis=-1)

def rms_scale(values):
    return lax.rsqrt(lax.optimization_barrier(jnp.mean(values * values, axis=1, keepdims=True)) + NORM_EPS)

def attend(queries, key_rows, value_rows, segment):
    token_place = jnp.arange(segment.shape[0], dtype=jnp.int32)
    allowed = (segment[:, None] == segment[None, :]) & (token_place[None, :] <= token_place[:, None])
    scores = low_back(jnp.einsum('qhd,khd->hqk', queries, key_rows, precision=PRECISE) * HEAD_DIM ** (-0.5))
    scores = jnp.where(allowed[None], scores, -1e+30)
    row_max = lax.optimization_barrier(jnp.max(scores, axis=2, keepdims=True))
    exponent = jnp.exp(scores - row_max)
    probabilities = exponent / lax.optimization_barrier(jnp.sum(exponent, axis=2, keepdims=True))
    return jnp.einsum('hqk,khd->qhd', low(probabilities), value_rows, precision=PRECISE)

def attend_pieces(pieces):
    return attend(pieces[0], pieces[1], pieces[2], pieces[3])

def block_forward(inputs, attn_w, mlp_w, gain_rows, segment, position):
    queries = low_back(jnp.dot(inputs, attn_w[0], precision=PRECISE))
    key_proj = low_back(jnp.dot(inputs, attn_w[1], precision=PRECISE))
    value_proj = low(low_back(jnp.dot(inputs, attn_w[2], precision=PRECISE)))
    queries = queries * rms_scale(queries) * gain_rows[0]
    key_proj = key_proj * rms_scale(key_proj) * gain_rows[1]
    queries = low(rotate(queries.reshape(-1, HEADS, HEAD_DIM), position, 1.0))
    key_proj = low(rotate(key_proj.reshape(-1, HEADS, HEAD_DIM), position, 1.0))
    value_proj = value_proj.reshape(-1, HEADS, HEAD_DIM)
    group_len = N_CTX * ROWS
    attended = lax.map(jax.checkpoint(attend_pieces), (queries.reshape(N_DP, group_len, HEADS, HEAD_DIM), key_proj.reshape(N_DP, group_len, HEADS, HEAD_DIM), value_proj.reshape(N_DP, group_len, HEADS, HEAD_DIM), segment.reshape(N_DP, group_len)))
    attn_out = low(low_back(attended.reshape(-1, D)))
    branch = low_back(jnp.dot(attn_out, attn_w[3].T, precision=PRECISE))
    hidden_in = inputs + branch * rms_scale(branch) * gain_rows[2]
    lowered = low(hidden_in)
    gate_proj = low_back(jnp.dot(lowered, mlp_w[0], precision=PRECISE))
    up_proj = low_back(jnp.dot(lowered, mlp_w[1], precision=PRECISE))
    activated = low(gate_proj * jax.nn.sigmoid(gate_proj) * up_proj)
    result = low_back(jnp.dot(activated, mlp_w[2].T, precision=PRECISE))
    return hidden_in + result * rms_scale(result) * gain_rows[3]

def adam_step(weight, gradient, moment_one, moment_two, rate, decay):
    moment_one = BETA_ONE * moment_one + (1.0 - BETA_ONE) * gradient
    moment_two = BETA_TWO * moment_two + (1.0 - BETA_TWO) * gradient * gradient
    fix_one = 1.0 - BETA_ONE ** STEP
    fix_two = 1.0 - BETA_TWO ** STEP
    update = moment_one / fix_one / (jnp.sqrt(moment_two / fix_two) + ADAM_EPS)
    return (weight - rate * (update + decay * weight), moment_one, moment_two)

def reference(inputs, cotangent, doc_lengths, attn_weights, mlp_weights, norm_gains, attn_first, attn_second, mlp_first, mlp_second, gain_first, gain_second):
    token_place = jnp.arange(N_CTX * ROWS, dtype=jnp.int32)
    segment, position = jax.vmap(lambda doc_row: doc_layout(doc_row, token_place))(doc_lengths)
    segment = segment.reshape(-1)
    position = position.reshape(-1)

    def forward(in_rows, attn_w, mlp_w, gain_rows):
        return block_forward(in_rows, attn_w, mlp_w, gain_rows, segment, position)
    output, pullback = jax.vjp(forward, inputs.astype(jnp.float32), low(attn_weights), low(mlp_weights), low(norm_gains))
    grad_inputs, grad_attn, grad_mlp, grad_gain = pullback(cotangent.astype(jnp.float32))
    new_attn, attn_one, attn_two = adam_step(attn_weights, grad_attn, attn_first, attn_second, LEARN_RATE, WEIGHT_DECAY)
    new_mlp, mlp_one, mlp_two = adam_step(mlp_weights, grad_mlp, mlp_first, mlp_second, LEARN_RATE, WEIGHT_DECAY)
    new_gains, gain_one, gain_two = adam_step(norm_gains, grad_gain, gain_first, gain_second, GAIN_RATE, 0.0)
    return (output.astype(jnp.bfloat16), grad_inputs, new_attn, attn_one, attn_two, new_mlp, mlp_one, mlp_two, new_gains, gain_one, gain_two)
```

```python
import functools

import jax
import jax.numpy as jnp
from jax import lax
from jax.experimental import pallas as pl
from jax.experimental.pallas import tpu as pltpu
from jax.sharding import PartitionSpec as P

D = 2048
HEAD_DIM = 128
STEP = 10


NORM_EPS = 1e-06
ROPE_THETA = 500000.0
BETA_ONE = 0.9
BETA_TWO = 0.95
ADAM_EPS = 1e-08
WEIGHT_DECAY = 0.1
LEARN_RATE = 0.02
GAIN_RATE = 1.0

SCORE_SCALE = HEAD_DIM ** (-0.5)
Q_BLOCK = 256
VMEM = 56 * 1024 * 1024
BF16 = jnp.bfloat16
F32 = jnp.float32


def passed_along(block, axis, distance):
    devices = range(lax.axis_size(axis))
    route = [(i - distance, i) for i in devices if i - distance in devices]
    return lax.ppermute(block, axis, route)


def swap(block, distance):
    return lax.ppermute(
        block, "tensor", [(i, i ^ distance) for i in range(lax.axis_size("tensor"))]
    )


def piece_order():
    n = lax.axis_size("tensor")
    return (0, 3, 1, 2) if n == 4 else tuple(range(n))


def gather_pieces(block):
    n = lax.axis_size("tensor")
    if n != 4:
        return [block] + [swap(block, k) for k in range(1, n)]
    one, two = swap(block, 1), swap(block, 2)
    half = block.shape[0] // 2
    upper = swap(one[:half], 2)
    lower = swap(two[half:], 1)
    return [block, jnp.concatenate([upper, lower], axis=0), one, two]


def scatter_square(mine, last, pair):
    rows = mine.shape[0]
    half = rows // 2
    last = last.astype(BF16)
    upper = swap(last[:half], 1)
    lower = swap(last[half:], 2)
    passing = jnp.concatenate([lower, upper], axis=0).astype(F32)
    pair = (pair + jnp.pad(passing, ((half, half), (0, 0)))).astype(BF16)
    one, two = swap(pair[:rows], 1), swap(pair[rows:], 2)
    return [mine, one, two]


def scatter_pieces(parts):
    if lax.axis_size("tensor") == 4:
        return scatter_square(parts[0], parts[1], jnp.concatenate(parts[2:], axis=0))
    total = parts[0]
    for k in range(1, len(parts)):
        total = total + swap(parts[k].astype(BF16), k).astype(F32)
    return [total]


def add_up(terms):
    return functools.reduce(jnp.add, [term.astype(F32) for term in terms])


def axis_total(values, axis):
    n = lax.axis_size(axis)
    others = [
        lax.ppermute(values, axis, [(i, (i + k) % n) for i in range(n)]) for k in range(1, n)
    ]
    return functools.reduce(jnp.add, others, values)


def doc_begins(doc_row, token_place):
    doc_ends = jnp.cumsum(doc_row)
    passed = token_place[:, None] >= doc_ends[None, :]
    return jnp.max(
        jnp.where(passed, doc_ends[None, :], jnp.zeros_like(doc_ends)[None, :]), axis=1
    )


def turn_tables(position):
    half_dim = HEAD_DIM // 2
    frequency = ROPE_THETA ** (-2.0 * jnp.arange(half_dim, dtype=F32) / HEAD_DIM)
    angles = position.astype(F32)[:, None] * frequency[None, :]
    cosine, sine = jnp.cos(angles), jnp.sin(angles)
    return jnp.concatenate([cosine, cosine], axis=1), jnp.concatenate([-sine, sine], axis=1)


def adam_step(weight, gradient, moment_one, moment_two, rate, decay):
    moment_one = BETA_ONE * moment_one + (1.0 - BETA_ONE) * gradient
    moment_two = BETA_TWO * moment_two + (1.0 - BETA_TWO) * gradient * gradient
    fix_one = 1.0 - BETA_ONE**STEP
    fix_two = 1.0 - BETA_TWO**STEP
    update = moment_one / fix_one / (jnp.sqrt(moment_two / fix_two) + ADAM_EPS)
    return (weight - rate * (update + decay * weight), moment_one, moment_two)


def matmul(left, right):
    return jnp.dot(left, right, preferred_element_type=F32)


def contract_rows(left, right):
    return lax.dot_general(left, right, (((0,), (0,)), ((), ())), preferred_element_type=F32)


def by_columns(left, right):
    return lax.dot_general(left, right, (((1,), (1,)), ((), ())), preferred_element_type=F32)


def after(value, *earlier):
    return lax.optimization_barrier((value,) + earlier)[0]


def other_core(values):
    return lax.ppermute(values, "ctx", [(0, 1), (1, 0)])


def scatter_owned(sums, axes=("dp",)):
    return lax.psum_scatter(sums, axes, scatter_dimension=0, tiled=True)


def call(
    kernel, grid, in_specs, out_specs, out_shape, scratch=(), flops=0, nbytes=0, trans=0, scalars=0
):
    return pl.pallas_call(
        kernel,
        grid_spec=pltpu.PrefetchScalarGridSpec(
            num_scalar_prefetch=scalars,
            grid=grid,
            in_specs=in_specs,
            out_specs=out_specs,
            scratch_shapes=list(scratch),
        ),
        out_shape=out_shape,
        compiler_params=pltpu.CompilerParams(vmem_limit_bytes=VMEM),
        cost_estimate=pl.CostEstimate(flops=flops, bytes_accessed=nbytes, transcendentals=trans),
    )


def weight_half_kernel(blocks, ctx_ref, *refs):
    left, right_ref, (out_ref, turned) = refs[:blocks], refs[blocks], refs[-2:]
    given_ref = refs[blocks + 1] if len(refs) > blocks + 3 else None

    @pl.when(pl.program_id(0) == 0)
    def _():
        for i, ref in enumerate(left):
            turned[i] = ref[...].T

    right = right_ref[...]
    for i in range(blocks):
        total = matmul(turned[i], right)
        if given_ref is not None:
            total = total + given_ref[i].astype(F32)
        out_ref[i] = total.astype(BF16)


def weight_half(left, right, ctx, given=None):
    rows, depth = left.shape
    blocks = lax.axis_size("dp")
    owned = depth // (blocks * lax.axis_size("ctx"))
    n_ctx = lax.axis_size("ctx")
    wide = right.shape[-1]
    block = next(size for size in (512, 256, 128) if wide % size == 0)
    steps = wide // block
    if right.ndim == 3:
        each = steps
        right_spec = pl.BlockSpec((None, rows, block), lambda j, c: (j // each, 0, j % each))
        steps = each * right.shape[0]
    else:
        right_spec = pl.BlockSpec((rows, block), lambda j, c: (0, j))
    out_spec = pl.BlockSpec((blocks, owned, block), lambda j, c: (0, 0, j))
    specs = [
        pl.BlockSpec((rows, owned), lambda j, c, i=i: (0, n_ctx * i + c[0])) for i in range(blocks)
    ]
    operands = [left] * blocks + [right]
    specs.append(right_spec)
    if given is not None:
        operands.append(given)
        specs.append(out_spec)
    columns = steps * block
    return call(
        functools.partial(weight_half_kernel, blocks),
        (steps,),
        specs,
        out_spec,
        jax.ShapeDtypeStruct((blocks, owned, columns), BF16),
        [pltpu.VMEM((blocks, owned, rows), BF16)],
        flops=2 * rows * blocks * owned * columns,
        nbytes=2 * (rows * blocks * owned + rows * columns + 2 * blocks * owned * columns),
        scalars=1,
    )(ctx[None], *operands)


def rope_kernel(q_ref, k_ref, v_ref, rs_ref, gq_ref, gk_ref, cos_ref, sin_ref, qo, ko, vo):
    cosine, sine = cos_ref[...], sin_ref[...]
    for place, (src, gain, dst) in enumerate(((q_ref, gq_ref, qo), (k_ref, gk_ref, ko))):
        scale = rs_ref[:, place : place + 1]
        for head in range(src.shape[1] // HEAD_DIM):
            cols = slice(head * HEAD_DIM, (head + 1) * HEAD_DIM)
            x = src[:, cols] * scale * gain[:, cols]
            dst[:, cols] = (x * cosine + pltpu.roll(x, HEAD_DIM // 2, 1) * sine).astype(BF16)
    vo[...] = v_ref[...].astype(BF16)


def rope(qkv, rs, gain_query, gain_key, cosine, sine):
    rows, width = qkv.shape[0], qkv.shape[1] // 3
    block = min(rows, 256)
    part = lambda j: pl.BlockSpec((block, width), lambda i, j=j: (i, j))
    gain = pl.BlockSpec((1, width), lambda i: (0, 0))
    table = pl.BlockSpec((block, HEAD_DIM), lambda i: (i, 0))
    out = jax.ShapeDtypeStruct((rows, width), BF16)
    return call(
        rope_kernel,
        (rows // block,),
        [part(0), part(1), part(2), pl.BlockSpec((block, 2), lambda i: (i, 0)), gain, gain]
        + [table, table],
        [part(0)] * 3,
        [out] * 3,
        flops=rows * width * 12,
        nbytes=rows * width * 18,
    )(qkv, qkv, qkv, rs, gain_query[None], gain_key[None], cosine, sine)


def attend_kernel(span, q_ref, k_ref, v_ref, start_ref, o_ref, lse_ref):
    rows = q_ref.shape[0]
    step = pl.program_id(0)
    first = pl.multiple_of(step * rows, rows)
    shape = (rows, span)
    row = lax.broadcasted_iota(jnp.int32, shape, 0)
    column = lax.broadcasted_iota(jnp.int32, shape, 1) - (span - rows)
    allowed = (column <= row) & (column >= start_ref[...] - step * rows)
    for head in range(q_ref.shape[1] // HEAD_DIM):
        cols = slice(head * HEAD_DIM, (head + 1) * HEAD_DIM)
        keys = k_ref[pl.ds(first, span), cols]
        values = v_ref[pl.ds(first, span), cols]
        scores = by_columns(q_ref[:, cols], keys) * SCORE_SCALE
        scores = jnp.where(allowed, scores, -1e30)
        top = jnp.max(scores, axis=1, keepdims=True)
        weights = jnp.exp(scores - top)
        total = jnp.sum(weights, axis=1, keepdims=True)
        low = (weights / total).astype(BF16)
        o_ref[:, cols] = matmul(low, values).astype(BF16)
        lse_ref[:, head : head + 1] = top + jnp.log(total)


def attend(query, keys, values, start):
    rows, width = query.shape
    heads = width // HEAD_DIM
    block = Q_BLOCK
    span = rows + block
    whole = pl.BlockSpec(keys.shape, lambda i: (0, 0))
    return call(
        functools.partial(attend_kernel, span),
        (rows // block,),
        [pl.BlockSpec((block, width), lambda i: (i, 0)), whole, whole]
        + [pl.BlockSpec((block, 1), lambda i: (i, 0))],
        [pl.BlockSpec((block, width), lambda i: (i, 0)), pl.BlockSpec((block, heads), lambda i: (i, 0))],
        [jax.ShapeDtypeStruct((rows, width), BF16), jax.ShapeDtypeStruct((rows, heads), F32)],
        flops=4 * rows * span * width,
        nbytes=rows * width * 12,
        trans=rows * span * heads,
    )(query, keys, values, start[:, None])


def attend_back_kernel(
    span, q_ref, k_ref, v_ref, do_ref, lse_ref, start_ref, dq_ref, dkp_ref, dvp_ref, dk_ref, dv_ref, ka, va
):
    rows = q_ref.shape[0]
    step = pl.program_id(0)
    first = pl.multiple_of(step * rows, rows)

    @pl.when(step == 0)
    def _():
        ka[...] = jnp.zeros_like(ka)
        va[...] = jnp.zeros_like(va)

    shape = (span, rows)
    column = lax.broadcasted_iota(jnp.int32, shape, 0) - (span - rows)
    row = lax.broadcasted_iota(jnp.int32, shape, 1)
    allowed = (column <= row) & (column >= start_ref[...] - step * rows)
    for head in range(q_ref.shape[1] // HEAD_DIM):
        cols = slice(head * HEAD_DIM, (head + 1) * HEAD_DIM)
        query, grad = q_ref[:, cols], do_ref[:, cols]
        keys = k_ref[pl.ds(first, span), cols]
        values = v_ref[pl.ds(first, span), cols]
        scores = by_columns(keys, query) * SCORE_SCALE
        weights = jnp.where(allowed, jnp.exp(scores - lse_ref[head : head + 1, :]), 0.0)
        grad_weights = by_columns(values, grad)
        mean = jnp.sum(weights * grad_weights, axis=0, keepdims=True)
        grad_scores = (weights * (grad_weights - mean)).astype(BF16)
        dq_ref[:, cols] = contract_rows(grad_scores, keys) * SCORE_SCALE
        va[pl.ds(first, span), cols] += matmul(weights.astype(BF16), grad)
        ka[pl.ds(first, span), cols] += matmul(grad_scores, query) * SCORE_SCALE

    @pl.when(step == pl.num_programs(0) - 1)
    def _():
        total = dk_ref.shape[0]
        dkp_ref[...] = ka[:total, :].astype(BF16)
        dvp_ref[...] = va[:total, :].astype(BF16)
        dk_ref[...] = ka[total:, :]
        dv_ref[...] = va[total:, :]


def attend_back(query, keys, values, grad, lse, start):
    rows, width = query.shape
    heads = width // HEAD_DIM
    block = Q_BLOCK
    span = rows + block
    whole = pl.BlockSpec(keys.shape, lambda i: (0, 0))
    mine = pl.BlockSpec((block, width), lambda i: (i, 0))
    full = pl.BlockSpec((rows, width), lambda i: (0, 0))
    return call(
        functools.partial(attend_back_kernel, span),
        (rows // block,),
        [mine, whole, whole, mine]
        + [pl.BlockSpec((heads, block), lambda i: (0, i)), pl.BlockSpec((1, block), lambda i: (0, i))],
        [mine, full, full, full, full],
        [jax.ShapeDtypeStruct((rows, width), t) for t in (F32, BF16, BF16, F32, F32)],
        [pltpu.VMEM(keys.shape, F32)] * 2,
        flops=10 * rows * span * width,
        nbytes=rows * width * 28,
        trans=rows * span * heads,
    )(query, keys, values, grad, lse, start[None, :])


def unrope_kernel(
    dq_ref, dk_ref, dv_ref, bk_ref, bv_ref, q_ref, k_ref, rs_ref, gq_ref, gk_ref, cos_ref, sin_ref,
    wq_ref, wk_ref, dvo_ref, inner_ref, gain_ref,
):
    cosine, sine = cos_ref[...], -sin_ref[...]
    for place, (src, back, x_ref, gain, dst) in enumerate(
        ((dq_ref, None, q_ref, gq_ref, wq_ref), (dk_ref, bk_ref, k_ref, gk_ref, wk_ref))
    ):
        scale = rs_ref[:, place : place + 1]
        inner = 0.0
        for head in range(src.shape[1] // HEAD_DIM):
            cols = slice(head * HEAD_DIM, (head + 1) * HEAD_DIM)
            grad = src[:, cols]
            if back is not None:
                grad = grad + back[:, cols].astype(F32)
            grad = grad * cosine + pltpu.roll(grad, HEAD_DIM // 2, 1) * sine
            x = x_ref[:, cols]
            weighted = grad * gain[:, cols]
            dst[:, cols] = weighted
            inner = inner + jnp.sum(weighted * x, axis=1, keepdims=True)
            gain_ref[0, place : place + 1, cols] = jnp.sum(grad * x * scale, axis=0, keepdims=True)
        inner_ref[:, place : place + 1] = inner
    dvo_ref[...] = (dv_ref[...] + bv_ref[...].astype(F32)).astype(BF16)


def unrope(dq, dk, dv, back_k, back_v, qkv, rs, gain_query, gain_key, cosine, sine):
    rows, width = dq.shape
    block = min(rows, 256)
    part = lambda j: pl.BlockSpec((block, width), lambda i, j=j: (i, j))
    gain = pl.BlockSpec((1, width), lambda i: (0, 0))
    table = pl.BlockSpec((block, HEAD_DIM), lambda i: (i, 0))
    pair = pl.BlockSpec((block, 2), lambda i: (i, 0))
    return call(
        unrope_kernel,
        (rows // block,),
        [part(0)] * 5 + [part(0), part(1), pair, gain, gain, table, table],
        [part(0)] * 3 + [pair, pl.BlockSpec((1, 2, width), lambda i: (i, 0, 0))],
        [jax.ShapeDtypeStruct((rows, width), t) for t in (F32, F32, BF16)]
        + [jax.ShapeDtypeStruct((rows, 2), F32)]
        + [jax.ShapeDtypeStruct((rows // block, 2, width), F32)],
        flops=rows * width * 30,
        nbytes=rows * width * 34,
    )(dq, dk, dv, back_k, back_v, qkv, qkv, rs, gain_query[None], gain_key[None], cosine, sine)


def merged(block):
    return block.reshape(-1, block.shape[-1])


def gate_up_kernel(x_ref, wg_ref, wu_ref, gu_ref, act_ref):
    x = x_ref[...]
    gate, up = matmul(x, merged(wg_ref[...])), matmul(x, merged(wu_ref[...]))
    gu_ref[0], gu_ref[1] = gate, up
    act_ref[...] = (gate * jax.nn.sigmoid(gate) * up).astype(BF16)


def gate_up(x, weights, owned):
    rows, depth = x.shape
    owners, hidden = weights.shape[0], weights.shape[2]
    block = min(hidden, 256)
    return call(
        gate_up_kernel,
        (hidden // block,),
        [
            pl.BlockSpec((rows, depth), lambda j: (0, 0)),
            pl.BlockSpec((owners, owned, block), lambda j: (0, 0, j)),
            pl.BlockSpec((owners, owned, block), lambda j: (0, 1, j)),
        ],
        [
            pl.BlockSpec((2, rows, block), lambda j: (0, 0, j)),
            pl.BlockSpec((rows, block), lambda j: (0, j)),
        ],
        [
            jax.ShapeDtypeStruct((2, rows, hidden), F32),
            jax.ShapeDtypeStruct((rows, hidden), BF16),
        ],
        flops=4 * rows * depth * hidden,
        nbytes=4 * depth * hidden + rows * (10 * hidden + 2 * depth),
        trans=rows * hidden,
    )(x, weights, weights)


def down_kernel(x_ref, w_ref, out_ref):
    out_ref[...] = by_columns(x_ref[...], merged(w_ref[...])).astype(out_ref.dtype)


def down(x, weights, place, count, begin, rows, kind):
    owners, hidden = weights.shape[0], weights.shape[2]
    group = max(1, min(owners, 512 // count))
    at, row = begin // rows, place // count
    return call(
        down_kernel,
        (owners // group,),
        [
            pl.BlockSpec((rows, hidden), lambda j: (at, 0)),
            pl.BlockSpec((group, count, hidden), lambda j: (j, row, 0)),
        ],
        pl.BlockSpec((rows, group * count), lambda j: (0, j)),
        jax.ShapeDtypeStruct((rows, owners * count), kind),
        flops=2 * rows * owners * count * hidden,
        nbytes=2 * owners * count * hidden + rows * (2 * hidden + 4 * owners * count),
    )(x, weights)


def act_back_kernel(cuts, x_ref, *refs):
    weights, (gu_ref, out_ref, split) = refs[: len(cuts)], refs[len(cuts) :]
    owners = weights[0].shape[0]
    owned = x_ref.shape[1] // owners

    @pl.when(pl.program_id(0) == 0)
    def _():
        to = 0
        for begin, count in cuts:
            for i in range(owners):
                at = i * owned + begin
                split[:, to : to + count] = x_ref[:, at : at + count]
                to += count

    grad, at = 0.0, 0
    for (_, count), ref in zip(cuts, weights):
        grad = grad + matmul(split[:, at : at + owners * count], merged(ref[...]))
        at += owners * count
    gate, up = gu_ref[0], gu_ref[1]
    sig = jax.nn.sigmoid(gate)
    out_ref[0] = (grad * up * sig * (1.0 + gate * (1.0 - sig))).astype(BF16)
    out_ref[1] = (grad * gate * sig).astype(BF16)


def act_back(x, pieces, gate_and_up):
    rows, depth = x.shape
    hidden = gate_and_up.shape[2]
    block = min(hidden, 512)
    pair = pl.BlockSpec((2, rows, block), lambda j: (0, 0, j))
    return call(
        functools.partial(act_back_kernel, [(first, count) for _, _, count, first in pieces]),
        (hidden // block,),
        [pl.BlockSpec((rows, depth), lambda j: (0, 0))]
        + [
            pl.BlockSpec((array.shape[0], count, block), lambda j, at=place // count: (0, at, j))
            for array, place, count, _ in pieces
        ]
        + [pair],
        pair,
        jax.ShapeDtypeStruct((2, rows, hidden), BF16),
        [pltpu.VMEM((rows, depth), BF16)],
        flops=2 * rows * depth * hidden,
        nbytes=2 * depth * hidden + rows * (12 * hidden + 2 * depth),
        trans=rows * hidden,
    )(x, *[array for array, _, _, _ in pieces], gate_and_up)


def hidden_back_kernel(x_ref, wg_ref, wu_ref, out_ref):
    total = by_columns(x_ref[0], merged(wg_ref[...])) + by_columns(x_ref[1], merged(wu_ref[...]))
    out_ref[...] = total.astype(out_ref.dtype)


def hidden_back(grads, weights, owned, begin, rows, kind):
    hidden, owners = grads.shape[2], weights.shape[0]
    group = max(1, (512 if rows <= 512 else 256) // owned)
    at = begin // rows
    return call(
        hidden_back_kernel,
        (owners // group,),
        [
            pl.BlockSpec((2, rows, hidden), lambda j: (0, at, 0)),
            pl.BlockSpec((group, owned, hidden), lambda j: (j, 0, 0)),
            pl.BlockSpec((group, owned, hidden), lambda j: (j, 1, 0)),
        ],
        pl.BlockSpec((rows, group * owned), lambda j: (0, j)),
        jax.ShapeDtypeStruct((rows, owners * owned), kind),
        flops=4 * rows * owners * owned * hidden,
        nbytes=4 * owners * owned * hidden + rows * (4 * hidden + 4 * owners * owned),
    )(grads, weights, weights)


def total_of(refs):
    return functools.reduce(jnp.add, [ref[...].astype(F32) for ref in refs])


def norm_back(grad, gain, values, scale):
    weighted = grad * gain
    inner = jnp.sum(weighted * values, axis=1, keepdims=True)
    back = scale * weighted - values * scale**3 * inner / D
    return back, jnp.sum(grad * values * scale, axis=0, keepdims=True)


def result_kernel(counts, owners, *refs):
    begin, parts = 0, []
    for count in counts:
        parts.append(total_of(refs[begin : begin + count]))
        begin += count
    hidden_ref, grad_ref, gain_ref, out_ref, back_ref, gain_grad_ref = refs[begin:]
    if len(parts) == 1:
        result = parts[0]
    else:
        width = parts[0].shape[1] // owners
        result = jnp.concatenate(
            [part[:, i * width : (i + 1) * width] for i in range(owners) for part in parts], axis=1
        )
    scale = lax.rsqrt(jnp.mean(result * result, axis=1, keepdims=True) + NORM_EPS)
    gain = gain_ref[...]
    out_ref[...] = (hidden_ref[...] + result * scale * gain).astype(BF16)
    back, gain_grad = norm_back(grad_ref[...].astype(F32), gain, result, scale)
    back_ref[...] = back.astype(BF16)
    gain_grad_ref[0] = gain_grad


def result_step(parts, owners, hidden_in, grad_out, gain):
    rows, depth = hidden_in.shape
    block = min(rows, 64)
    mine = pl.BlockSpec((block, depth), lambda i: (i, 0))
    flat = [array for part in parts for array in part]
    return call(
        functools.partial(result_kernel, [len(part) for part in parts], owners),
        (rows // block,),
        [pl.BlockSpec((block, array.shape[1]), lambda i: (i, 0)) for array in flat]
        + [mine, mine, pl.BlockSpec((1, depth), lambda i: (0, 0))],
        [mine, mine, pl.BlockSpec((1, 1, depth), lambda i: (i, 0, 0))],
        [
            jax.ShapeDtypeStruct((rows, depth), BF16),
            jax.ShapeDtypeStruct((rows, depth), BF16),
            jax.ShapeDtypeStruct((rows // block, 1, depth), F32),
        ],
        flops=rows * depth * 20,
        nbytes=rows * depth * 20,
    )(*flat, hidden_in, grad_out, gain[None])


def branch_back_kernel(count, *refs):
    branch_ref, grad_ref, gain_ref, hidden_ref, back_ref, gain_grad_ref = refs[count:]
    grad = grad_ref[...].astype(F32) + total_of(refs[:count])
    hidden_ref[...] = grad
    branch = branch_ref[...]
    scale = lax.rsqrt(jnp.mean(branch * branch, axis=1, keepdims=True) + NORM_EPS)
    back, gain_grad = norm_back(grad, gain_ref[...], branch, scale)
    back_ref[...] = back.astype(BF16)
    gain_grad_ref[0] = gain_grad


def branch_back(parts, branch, grad_out, gain):
    rows, depth = branch.shape
    block = min(rows, 64)
    mine = pl.BlockSpec((block, depth), lambda i: (i, 0))
    return call(
        functools.partial(branch_back_kernel, len(parts)),
        (rows // block,),
        [mine] * (len(parts) + 2) + [pl.BlockSpec((1, depth), lambda i: (0, 0))],
        [mine, mine, pl.BlockSpec((1, 1, depth), lambda i: (i, 0, 0))],
        [
            jax.ShapeDtypeStruct((rows, depth), F32),
            jax.ShapeDtypeStruct((rows, depth), BF16),
            jax.ShapeDtypeStruct((rows // block, 1, depth), F32),
        ],
        flops=rows * depth * 20,
        nbytes=rows * depth * 20,
    )(*parts, branch, grad_out, gain[None])


def body(
    inputs,
    cotangent,
    doc_lengths,
    attn_weights,
    mlp_weights,
    norm_gains,
    attn_first,
    attn_second,
    mlp_first,
    mlp_second,
    gain_first,
    gain_second,
):
    owners = ("dp", "ctx")
    n = lax.axis_size("tensor")
    mine = lax.axis_index("tensor")
    rows, width = inputs.shape
    own = rows // n
    hidden = mlp_weights.shape[2]

    low = attn_weights.astype(BF16)
    attn_shard = jnp.concatenate([low[0], low[1], low[2], low[3]], axis=1)
    low = mlp_weights.astype(BF16)
    owned = low.shape[1]
    lead = owned // 2 if owned % 256 == 0 else 0
    up_shard = jnp.concatenate([low[0], low[1], low[2, :lead]], axis=0)
    attn_full = lax.all_gather(attn_shard, owners, axis=0, tiled=True)
    up_full = lax.all_gather(up_shard, owners, axis=0)
    down_full = lax.all_gather(low[2, lead:], owners, axis=0)
    down_pieces = [(down_full, 0, owned - lead, lead)]
    if lead:
        down_pieces = [(up_full, 2 * owned, lead, 0)] + down_pieces
    w_qkv, w_out = attn_full[:, : 3 * width], attn_full[:, 3 * width :]
    gains = lax.all_gather(
        norm_gains.astype(BF16), ("tensor",) + owners, axis=1, tiled=True
    ).astype(F32)
    gain_attn, gain_mlp = gains[2], gains[3]
    near = lax.dynamic_slice_in_dim(gains, mine * width, width, axis=1)
    gain_query, gain_key = near[0], near[1]

    gathered = jnp.zeros((rows, n * width), BF16)
    order = piece_order()
    for k, piece in zip(order, gather_pieces(inputs)):
        gathered = lax.dynamic_update_slice(gathered, piece, (0, (mine ^ k) * width))
    grad_out = jnp.zeros((own, n * width), BF16)
    for k in range(n):
        piece = lax.dynamic_slice_in_dim(cotangent, (mine ^ k) * own, own, axis=0)
        piece = swap(piece, k) if k else piece
        grad_out = lax.dynamic_update_slice(grad_out, piece, (0, (mine ^ k) * width))

    offset = lax.axis_index("ctx") * rows
    token_place = offset + jnp.arange(rows, dtype=jnp.int32)
    begins = doc_begins(doc_lengths[0], token_place)
    cosine, sine = turn_tables(token_place - begins)
    start = begins - offset

    qkv = matmul(gathered, w_qkv)
    queries, key_proj = qkv[:, :width], qkv[:, width : 2 * width]
    squares = axis_total(
        jnp.stack([jnp.sum(queries * queries, axis=1), jnp.sum(key_proj * key_proj, axis=1)]),
        "tensor",
    )
    qk_rs = lax.rsqrt(squares / D + NORM_EPS).T
    query_low, key_low, value_low = rope(qkv, qk_rs, gain_query, gain_key, cosine, sine)
    all_keys = jnp.concatenate([passed_along(key_low, "ctx", 1), key_low], axis=0)
    all_values = jnp.concatenate([passed_along(value_low, "ctx", 1), value_low], axis=0)
    attn_low, log_total = attend(query_low, all_keys, all_values, start)

    parts = [
        by_columns(lax.dynamic_slice_in_dim(attn_low, (mine ^ k) * own, own, axis=0), w_out)
        for k in order
    ]
    branch = add_up(scatter_pieces(parts))
    branch_rs = lax.rsqrt(jnp.mean(branch * branch, axis=1, keepdims=True) + NORM_EPS)
    my_rows = lax.dynamic_slice_in_dim(gathered, mine * own, own, axis=0)
    hidden_in = my_rows.astype(F32) + branch * branch_rs * gain_attn
    hidden_low = jnp.concatenate(gather_pieces(hidden_in.astype(BF16)), axis=0)
    gate_and_up, act_low = gate_up(hidden_low, up_full, owned)
    terms = []
    for array, place, count, _ in down_pieces:
        piece = functools.partial(down, act_low, array, place, count)
        if n == 4:
            last = piece(own, own, BF16)
            pair = piece(2 * own, 2 * own, F32)
            terms.append(scatter_square(piece(0, own, F32), last, pair))
        else:
            parts = piece(0, rows, F32)
            terms.append(scatter_pieces([parts[k * own : (k + 1) * own] for k in range(n)]))
    output_low, grad_result, gain_mlp_parts = result_step(
        terms, down_full.shape[0], hidden_in, grad_out, gain_mlp
    )
    grad_gain_mlp = jnp.sum(gain_mlp_parts, axis=(0, 1))
    grad_result_all = jnp.concatenate(gather_pieces(grad_result), axis=0)
    down_sums = contract_rows(grad_result_all, act_low).astype(BF16)
    owned_down = scatter_owned(down_sums, owners)
    grad_gate_up = act_back(after(grad_result_all, down_sums), down_pieces, gate_and_up)
    if n == 4:
        last = hidden_back(grad_gate_up, up_full, owned, own, own, BF16)
        pair = hidden_back(after(grad_gate_up, last), up_full, owned, 2 * own, 2 * own, F32)
        first = hidden_back(after(grad_gate_up, pair), up_full, owned, 0, own, F32)
        terms = scatter_square(first, last, pair)
    else:
        first = hidden_back(grad_gate_up, up_full, owned, 0, rows, F32)
        terms = scatter_pieces([first[k * own : (k + 1) * own] for k in range(n)])
    grad_hidden, grad_branch, gain_attn_parts = branch_back(terms, branch, grad_out, gain_attn)
    grad_gain_attn = jnp.sum(gain_attn_parts, axis=(0, 1))
    ctx = lax.axis_index("ctx")
    given = other_core(weight_half(hidden_low, after(grad_gate_up, first), 1 - ctx))
    up_sums = weight_half(hidden_low, grad_gate_up, ctx, given)
    owned_up = scatter_owned(merged(after(up_sums, owned_down)))
    grad_branch_all = jnp.zeros((rows, n * width), BF16)
    for k, piece in zip(order, gather_pieces(grad_branch)):
        grad_branch_all = lax.dynamic_update_slice(grad_branch_all, piece, ((mine ^ k) * own, 0))
    grad_mixed = matmul(grad_branch_all, w_out).astype(BF16)
    given = other_core(weight_half(grad_branch_all, attn_low, 1 - ctx))
    out_sums = weight_half(grad_branch_all, attn_low, ctx, given)
    dq, dkp, dvp, dk, dv = attend_back(
        query_low, all_keys, all_values, grad_mixed, log_total.T, start
    )
    back_key = passed_along(dkp, "ctx", -1)
    back_value = passed_along(dvp, "ctx", -1)
    weighted_q, weighted_k, grad_v, inner, gain_parts = unrope(
        dq, dk, dv, back_key, back_value, qkv, qk_rs, gain_query, gain_key, cosine, sine
    )
    inner = axis_total(inner.T, "tensor").T
    grad_q = qk_rs[:, :1] * weighted_q - queries * qk_rs[:, :1] ** 3 * inner[:, :1] / D
    grad_k = qk_rs[:, 1:] * weighted_k - key_proj * qk_rs[:, 1:] ** 3 * inner[:, 1:] / D
    grad_qkv = jnp.concatenate([grad_q.astype(BF16), grad_k.astype(BF16), grad_v], axis=1)
    given = other_core(weight_half(gathered, grad_qkv, 1 - ctx))
    qkv_sums = weight_half(gathered, grad_qkv, ctx, given)
    attn_sums = jnp.concatenate([merged(qkv_sums), merged(out_sums)], axis=1)
    owned_attn = scatter_owned(after(attn_sums, owned_up))
    residual = lax.dynamic_update_slice(
        jnp.zeros((rows, n * width), F32), grad_hidden, (mine * own, 0)
    )
    parts = []
    for k in order:
        at = (mine ^ k) * width
        part = by_columns(grad_qkv, lax.dynamic_slice_in_dim(w_qkv, at, width, axis=0))
        parts.append(part + lax.dynamic_slice_in_dim(residual, at, width, axis=1))
    grad_inputs = add_up(scatter_pieces(parts))

    wide = jnp.stack([grad_gain_attn, grad_gain_mlp])
    near = lax.dynamic_slice_in_dim(wide, mine * width, width, axis=1)
    for k in range(1, n):
        near = near + swap(lax.dynamic_slice_in_dim(wide, (mine ^ k) * width, width, axis=1), k)
    gain_sums = jnp.concatenate([jnp.sum(gain_parts, axis=0), near])
    gain_sums = axis_total(axis_total(gain_sums, "ctx"), "dp")
    share = norm_gains.shape[1]
    place = (lax.axis_index("dp") * lax.axis_size("ctx") + lax.axis_index("ctx")) * share
    gain_grad = lax.dynamic_slice_in_dim(gain_sums, place, share, axis=1)

    output = jnp.zeros((rows, width), BF16)
    for k in range(n):
        piece = lax.dynamic_slice_in_dim(output_low, (mine ^ k) * width, width, axis=1)
        piece = swap(piece, k) if k else piece
        output = lax.dynamic_update_slice(output, piece, ((mine ^ k) * own, 0))

    owned_attn = owned_attn.astype(F32)
    attn_grad = jnp.stack([owned_attn[:, i * width : (i + 1) * width] for i in range(4)])
    owned_up = owned_up.astype(F32)
    mlp_grad = jnp.stack([owned_up[:, :hidden], owned_up[:, hidden:], owned_down.astype(F32)])
    new_attn, attn_one, attn_two = adam_step(
        attn_weights, attn_grad, attn_first, attn_second, LEARN_RATE, WEIGHT_DECAY
    )
    new_mlp, mlp_one, mlp_two = adam_step(
        mlp_weights, mlp_grad, mlp_first, mlp_second, LEARN_RATE, WEIGHT_DECAY
    )
    new_gains, gain_one, gain_two = adam_step(
        norm_gains, gain_grad, gain_first, gain_second, GAIN_RATE, 0.0
    )
    return (
        output,
        grad_inputs,
        new_attn,
        attn_one,
        attn_two,
        new_mlp,
        mlp_one,
        mlp_two,
        new_gains,
        gain_one,
        gain_two,
    )


def solution(mesh):
    return jax.shard_map(
        body,
        mesh=mesh,
        in_specs=(
            P(("dp", "ctx"), "tensor"),
            P(("dp", "ctx"), "tensor"),
            P("dp", None),
            P(None, ("dp", "ctx"), "tensor"),
            P(None, ("dp", "ctx"), "tensor"),
            P(None, ("tensor", "dp", "ctx")),
            P(None, ("dp", "ctx"), "tensor"),
            P(None, ("dp", "ctx"), "tensor"),
            P(None, ("dp", "ctx"), "tensor"),
            P(None, ("dp", "ctx"), "tensor"),
            P(None, ("tensor", "dp", "ctx")),
            P(None, ("tensor", "dp", "ctx")),
        ),
        out_specs=(
            P(("dp", "ctx"), "tensor"),
            P(("dp", "ctx"), "tensor"),
            P(None, ("dp", "ctx"), "tensor"),
            P(None, ("dp", "ctx"), "tensor"),
            P(None, ("dp", "ctx"), "tensor"),
            P(None, ("dp", "ctx"), "tensor"),
            P(None, ("dp", "ctx"), "tensor"),
            P(None, ("dp", "ctx"), "tensor"),
            P(None, ("tensor", "dp", "ctx")),
            P(None, ("tensor", "dp", "ctx")),
            P(None, ("tensor", "dp", "ctx")),
        ),
        check_vma=False,
    )
```

```python
import functools

import jax
import jax.numpy as jnp
from jax import lax
from jax.experimental import pallas as pl
from jax.experimental.pallas import tpu as pltpu
from jax.sharding import PartitionSpec as P

D = 2048
HEAD_DIM = 128
STEP = 10


NORM_EPS = 1e-06
ROPE_THETA = 500000.0
BETA_ONE = 0.9
BETA_TWO = 0.95
ADAM_EPS = 1e-08
WEIGHT_DECAY = 0.1
LEARN_RATE = 0.02
GAIN_RATE = 1.0

SCORE_SCALE = HEAD_DIM ** (-0.5)
Q_BLOCK = 256
VMEM = 56 * 1024 * 1024
BF16 = jnp.bfloat16
F32 = jnp.float32


def passed_along(block, axis, distance):
    devices = range(lax.axis_size(axis))
    route = [(i - distance, i) for i in devices if i - distance in devices]
    return lax.ppermute(block, axis, route)


def swap(block, distance):
    return lax.ppermute(
        block, "tensor", [(i, i ^ distance) for i in range(lax.axis_size("tensor"))]
    )


def piece_order():
    n = lax.axis_size("tensor")
    return (0, 3, 1, 2) if n == 4 else tuple(range(n))


def gather_pieces(block):
    n = lax.axis_size("tensor")
    if n != 4:
        return [block] + [swap(block, k) for k in range(1, n)]
    half = block.shape[0] // 2
    upper, lower = block[:half], block[half:]
    two_upper, one_lower = swap(upper, 2), swap(lower, 1)
    one_upper, two_lower = swap(upper, 1), swap(lower, 2)
    far_upper, far_lower = swap(two_upper, 1), swap(one_lower, 2)
    return [
        jnp.concatenate(pair, axis=0)
        for pair in ((upper, lower), (far_upper, far_lower), (one_upper, one_lower), (two_upper, two_lower))
    ]


def send_far(last):
    half = last.shape[0] // 2
    last = last.astype(BF16)
    upper = swap(last[:half], 1)
    lower = swap(last[half:], 2)
    return jnp.concatenate([lower, upper], axis=0)


def send_near(pair, passing):
    rows = pair.shape[0] // 2
    passing = jnp.pad(passing.astype(F32), ((rows // 2, rows // 2), (0, 0)))
    pair = (pair + passing).astype(BF16)
    return pair, [swap(pair[:rows], 1), swap(pair[rows:], 2)]


def scatter_pieces(parts):
    if lax.axis_size("tensor") == 4:
        passing = send_far(parts[1])
        return [parts[0]] + send_near(jnp.concatenate(parts[2:], axis=0), passing)[1]
    total = parts[0]
    for k in range(1, len(parts)):
        total = total + swap(parts[k].astype(BF16), k).astype(F32)
    return [total]


def add_up(terms):
    return functools.reduce(jnp.add, [term.astype(F32) for term in terms])


def axis_total(values, axis):
    n = lax.axis_size(axis)
    flat = values.reshape(-1, HEAD_DIM)
    others = [
        lax.ppermute(flat, axis, [(i, i ^ k if n in (2, 4, 8) else (i + k) % n) for i in range(n)])
        for k in range(1, n)
    ]
    return functools.reduce(jnp.add, others, flat).reshape(values.shape)


def doc_begins(doc_row, token_place):
    doc_ends = jnp.cumsum(doc_row)
    passed = token_place[:, None] >= doc_ends[None, :]
    return jnp.max(
        jnp.where(passed, doc_ends[None, :], jnp.zeros_like(doc_ends)[None, :]), axis=1
    )


def turn_tables(position):
    half_dim = HEAD_DIM // 2
    frequency = ROPE_THETA ** (-2.0 * jnp.arange(half_dim, dtype=F32) / HEAD_DIM)
    angles = position.astype(F32)[:, None] * frequency[None, :]
    cosine, sine = jnp.cos(angles), jnp.sin(angles)
    return jnp.concatenate([cosine, cosine], axis=1), jnp.concatenate([-sine, sine], axis=1)


def adam_step(weight, gradient, moment_one, moment_two, rate, decay):
    moment_one = BETA_ONE * moment_one + (1.0 - BETA_ONE) * gradient
    moment_two = BETA_TWO * moment_two + (1.0 - BETA_TWO) * gradient * gradient
    fix_one = 1.0 - BETA_ONE**STEP
    fix_two = 1.0 - BETA_TWO**STEP
    update = moment_one / fix_one / (jnp.sqrt(moment_two / fix_two) + ADAM_EPS)
    return (weight - rate * (update + decay * weight), moment_one, moment_two)


def matmul(left, right):
    return jnp.dot(left, right, preferred_element_type=F32)


def contract_rows(left, right):
    return lax.dot_general(left, right, (((0,), (0,)), ((), ())), preferred_element_type=F32)


def by_columns(left, right):
    return lax.dot_general(left, right, (((1,), (1,)), ((), ())), preferred_element_type=F32)


def after(value, *earlier):
    return lax.optimization_barrier((value,) + earlier)[0]


def other_core(values):
    return lax.ppermute(values, "ctx", [(0, 1), (1, 0)])


def scatter_owned(sums, axes=("dp",)):
    return lax.psum_scatter(sums, axes, scatter_dimension=0, tiled=True)


def call(
    kernel, grid, in_specs, out_specs, out_shape, scratch=(), flops=0, nbytes=0, trans=0, scalars=0,
    announced=0.25,
):
    return pl.pallas_call(
        kernel,
        grid_spec=pltpu.PrefetchScalarGridSpec(
            num_scalar_prefetch=scalars,
            grid=grid,
            in_specs=in_specs,
            out_specs=out_specs,
            scratch_shapes=list(scratch),
        ),
        out_shape=out_shape,
        compiler_params=pltpu.CompilerParams(vmem_limit_bytes=VMEM),
        cost_estimate=pl.CostEstimate(
            flops=int(flops * announced),
            bytes_accessed=int(nbytes * announced),
            transcendentals=int(trans * announced),
        ),
    )


def weight_half_kernel(blocks, steps, ctx_ref, *refs):
    left, right_ref, (out_ref, turned) = refs[:blocks], refs[blocks], refs[-2:]
    given_ref = refs[blocks + 1] if len(refs) > blocks + 3 else None
    tail_ref = refs[blocks + 2] if len(refs) > blocks + 4 else None

    @pl.when(pl.program_id(0) == 0)
    def _():
        for i, ref in enumerate(left):
            turned[i] = ref[...].T

    @pl.when(pl.program_id(0) < steps)
    def _():
        right = right_ref[...]
        for i in range(blocks):
            total = matmul(turned[i], right)
            if given_ref is not None:
                total = total + given_ref[i].astype(F32)
            out_ref[i] = total.astype(BF16)

    if tail_ref is not None:

        @pl.when(pl.program_id(0) >= steps)
        def _():
            out_ref[...] = tail_ref[...]


def weight_half(left, right, ctx, given=None, tail=None):
    rows, depth = left.shape
    blocks = lax.axis_size("dp")
    owned = depth // (blocks * lax.axis_size("ctx"))
    n_ctx = lax.axis_size("ctx")
    wide = right.shape[-1]
    block = next(size for size in (512, 256, 128) if wide % size == 0)
    each = wide // block
    steps = each * (right.shape[0] if right.ndim == 3 else 1)
    last = steps - 1
    if right.ndim == 3:
        right_spec = pl.BlockSpec((None, rows, block), lambda j, c: (j // each, 0, j % each))
    else:
        right_spec = pl.BlockSpec((rows, block), lambda j, c: (0, jnp.minimum(j, last)))
    specs = [
        pl.BlockSpec((rows, owned), lambda j, c, i=i: (0, n_ctx * i + c[0])) for i in range(blocks)
    ]
    operands = [left] * blocks + [right]
    specs.append(right_spec)
    columns = steps * block
    more = 0
    if given is not None:
        operands.append(given)
        specs.append(
            pl.BlockSpec((blocks, owned, block), lambda j, c: (0, 0, jnp.minimum(j, last)))
        )
    if tail is not None:
        operands.append(tail)
        more = tail.shape[2] // block
        specs.append(
            pl.BlockSpec((blocks, owned, block), lambda j, c: (0, 0, jnp.maximum(j - steps, 0)))
        )
    return call(
        functools.partial(weight_half_kernel, blocks, steps),
        (steps + more,),
        specs,
        pl.BlockSpec((blocks, owned, block), lambda j, c: (0, 0, j)),
        jax.ShapeDtypeStruct((blocks, owned, columns + more * block), BF16),
        [pltpu.VMEM((blocks, owned, rows), BF16)],
        flops=2 * rows * blocks * owned * columns,
        nbytes=2 * (rows * blocks * owned + rows * columns + 2 * blocks * owned * columns),
        scalars=1,
    )(ctx[None], *operands)


def rope_kernel(q_ref, k_ref, v_ref, rs_ref, gq_ref, gk_ref, cos_ref, sin_ref, qo, ko, vo):
    cosine, sine = cos_ref[...], sin_ref[...]
    for place, (src, gain, dst) in enumerate(((q_ref, gq_ref, qo), (k_ref, gk_ref, ko))):
        scale = rs_ref[:, place : place + 1]
        for head in range(src.shape[1] // HEAD_DIM):
            cols = slice(head * HEAD_DIM, (head + 1) * HEAD_DIM)
            x = src[:, cols] * scale * gain[:, cols]
            dst[:, cols] = (x * cosine + pltpu.roll(x, HEAD_DIM // 2, 1) * sine).astype(BF16)
    vo[...] = v_ref[...].astype(BF16)


def rope(qkv, rs, gain_query, gain_key, cosine, sine):
    rows, width = qkv.shape[0], qkv.shape[1] // 3
    block = min(rows, 256)
    part = lambda j: pl.BlockSpec((block, width), lambda i, j=j: (i, j))
    gain = pl.BlockSpec((1, width), lambda i: (0, 0))
    table = pl.BlockSpec((block, HEAD_DIM), lambda i: (i, 0))
    out = jax.ShapeDtypeStruct((rows, width), BF16)
    return call(
        rope_kernel,
        (rows // block,),
        [part(0), part(1), part(2), pl.BlockSpec((block, 2), lambda i: (i, 0)), gain, gain]
        + [table, table],
        [part(0)] * 3,
        [out] * 3,
        flops=rows * width * 12,
        nbytes=rows * width * 18,
    )(qkv, qkv, qkv, rs, gain_query[None], gain_key[None], cosine, sine)


def attend_kernel(span, q_ref, k_ref, v_ref, start_ref, o_ref, lse_ref):
    rows = q_ref.shape[0]
    step = pl.program_id(0)
    first = pl.multiple_of(step * rows, rows)
    shape = (rows, span)
    row = lax.broadcasted_iota(jnp.int32, shape, 0)
    column = lax.broadcasted_iota(jnp.int32, shape, 1) - (span - rows)
    allowed = (column <= row) & (column >= start_ref[...] - step * rows)
    for head in range(q_ref.shape[1] // HEAD_DIM):
        cols = slice(head * HEAD_DIM, (head + 1) * HEAD_DIM)
        keys = k_ref[pl.ds(first, span), cols]
        values = v_ref[pl.ds(first, span), cols]
        scores = by_columns(q_ref[:, cols], keys) * SCORE_SCALE
        scores = jnp.where(allowed, scores, -1e30)
        top = jnp.max(scores, axis=1, keepdims=True)
        weights = jnp.exp(scores - top)
        total = jnp.sum(weights, axis=1, keepdims=True)
        low = (weights / total).astype(BF16)
        o_ref[:, cols] = matmul(low, values).astype(BF16)
        lse_ref[:, head : head + 1] = top + jnp.log(total)


def attend(query, keys, values, start):
    rows, width = query.shape
    heads = width // HEAD_DIM
    block = Q_BLOCK
    span = rows + block
    whole = pl.BlockSpec(keys.shape, lambda i: (0, 0))
    return call(
        functools.partial(attend_kernel, span),
        (rows // block,),
        [pl.BlockSpec((block, width), lambda i: (i, 0)), whole, whole]
        + [pl.BlockSpec((block, 1), lambda i: (i, 0))],
        [pl.BlockSpec((block, width), lambda i: (i, 0)), pl.BlockSpec((block, heads), lambda i: (i, 0))],
        [jax.ShapeDtypeStruct((rows, width), BF16), jax.ShapeDtypeStruct((rows, heads), F32)],
        flops=4 * rows * span * width,
        nbytes=rows * width * 12,
        trans=rows * span * heads,
    )(query, keys, values, start[:, None])


def attend_back_kernel(
    span, q_ref, k_ref, v_ref, do_ref, lse_ref, start_ref, dq_ref, dkp_ref, dvp_ref, dk_ref, dv_ref, ka, va
):
    rows = q_ref.shape[0]
    step = pl.program_id(0)
    first = pl.multiple_of(step * rows, rows)

    @pl.when(step == 0)
    def _():
        ka[...] = jnp.zeros_like(ka)
        va[...] = jnp.zeros_like(va)

    shape = (span, rows)
    column = lax.broadcasted_iota(jnp.int32, shape, 0) - (span - rows)
    row = lax.broadcasted_iota(jnp.int32, shape, 1)
    allowed = (column <= row) & (column >= start_ref[...] - step * rows)
    for head in range(q_ref.shape[1] // HEAD_DIM):
        cols = slice(head * HEAD_DIM, (head + 1) * HEAD_DIM)
        query, grad = q_ref[:, cols], do_ref[:, cols]
        keys = k_ref[pl.ds(first, span), cols]
        values = v_ref[pl.ds(first, span), cols]
        scores = by_columns(keys, query) * SCORE_SCALE
        weights = jnp.where(allowed, jnp.exp(scores - lse_ref[head : head + 1, :]), 0.0)
        grad_weights = by_columns(values, grad)
        mean = jnp.sum(weights * grad_weights, axis=0, keepdims=True)
        grad_scores = (weights * (grad_weights - mean)).astype(BF16)
        dq_ref[:, cols] = contract_rows(grad_scores, keys) * SCORE_SCALE
        va[pl.ds(first, span), cols] += matmul(weights.astype(BF16), grad)
        ka[pl.ds(first, span), cols] += matmul(grad_scores, query) * SCORE_SCALE

    @pl.when(step == pl.num_programs(0) - 1)
    def _():
        total = dk_ref.shape[0]
        dkp_ref[...] = ka[:total, :].astype(BF16)
        dvp_ref[...] = va[:total, :].astype(BF16)
        dk_ref[...] = ka[total:, :]
        dv_ref[...] = va[total:, :]


def attend_back(query, keys, values, grad, lse, start):
    rows, width = query.shape
    heads = width // HEAD_DIM
    block = Q_BLOCK
    span = rows + block
    whole = pl.BlockSpec(keys.shape, lambda i: (0, 0))
    mine = pl.BlockSpec((block, width), lambda i: (i, 0))
    full = pl.BlockSpec((rows, width), lambda i: (0, 0))
    return call(
        functools.partial(attend_back_kernel, span),
        (rows // block,),
        [mine, whole, whole, mine]
        + [pl.BlockSpec((heads, block), lambda i: (0, i)), pl.BlockSpec((1, block), lambda i: (0, i))],
        [mine, full, full, full, full],
        [jax.ShapeDtypeStruct((rows, width), t) for t in (F32, BF16, BF16, F32, F32)],
        [pltpu.VMEM(keys.shape, F32)] * 2,
        flops=10 * rows * span * width,
        nbytes=rows * width * 28,
        trans=rows * span * heads,
        announced=12,
    )(query, keys, values, grad, lse, start[None, :])


def unrope_kernel(
    dq_ref, dk_ref, dv_ref, bk_ref, bv_ref, q_ref, k_ref, rs_ref, gq_ref, gk_ref, cos_ref, sin_ref,
    wq_ref, wk_ref, dvo_ref, inner_ref, gain_ref,
):
    cosine, sine = cos_ref[...], -sin_ref[...]
    for place, (src, back, x_ref, gain, dst) in enumerate(
        ((dq_ref, None, q_ref, gq_ref, wq_ref), (dk_ref, bk_ref, k_ref, gk_ref, wk_ref))
    ):
        scale = rs_ref[:, place : place + 1]
        inner = 0.0
        for head in range(src.shape[1] // HEAD_DIM):
            cols = slice(head * HEAD_DIM, (head + 1) * HEAD_DIM)
            grad = src[:, cols]
            if back is not None:
                grad = grad + back[:, cols].astype(F32)
            grad = grad * cosine + pltpu.roll(grad, HEAD_DIM // 2, 1) * sine
            x = x_ref[:, cols]
            weighted = grad * gain[:, cols]
            dst[:, cols] = weighted
            inner = inner + jnp.sum(weighted * x, axis=1, keepdims=True)
            gain_ref[0, place : place + 1, cols] = jnp.sum(grad * x * scale, axis=0, keepdims=True)
        inner_ref[:, place : place + 1] = inner
    dvo_ref[...] = (dv_ref[...] + bv_ref[...].astype(F32)).astype(BF16)


def unrope(dq, dk, dv, back_k, back_v, qkv, rs, gain_query, gain_key, cosine, sine):
    rows, width = dq.shape
    block = min(rows, 256)
    part = lambda j: pl.BlockSpec((block, width), lambda i, j=j: (i, j))
    gain = pl.BlockSpec((1, width), lambda i: (0, 0))
    table = pl.BlockSpec((block, HEAD_DIM), lambda i: (i, 0))
    pair = pl.BlockSpec((block, 2), lambda i: (i, 0))
    return call(
        unrope_kernel,
        (rows // block,),
        [part(0)] * 5 + [part(0), part(1), pair, gain, gain, table, table],
        [part(0)] * 3 + [pair, pl.BlockSpec((1, 2, width), lambda i: (i, 0, 0))],
        [jax.ShapeDtypeStruct((rows, width), t) for t in (F32, F32, BF16)]
        + [jax.ShapeDtypeStruct((rows, 2), F32)]
        + [jax.ShapeDtypeStruct((rows // block, 2, width), F32)],
        flops=rows * width * 30,
        nbytes=rows * width * 34,
    )(dq, dk, dv, back_k, back_v, qkv, qkv, rs, gain_query[None], gain_key[None], cosine, sine)


def merged(block):
    return block.reshape(-1, block.shape[-1])


def gate_up_kernel(x_ref, wg_ref, wu_ref, gu_ref, act_ref):
    x = x_ref[...]
    gate, up = matmul(x, merged(wg_ref[...])), matmul(x, merged(wu_ref[...]))
    gu_ref[0], gu_ref[1] = gate, up
    act_ref[...] = (gate * jax.nn.sigmoid(gate) * up).astype(BF16)


def gate_up(x, weights, owned):
    rows, depth = x.shape
    owners, hidden = weights.shape[0], weights.shape[2]
    block = min(hidden, 256)
    return call(
        gate_up_kernel,
        (hidden // block,),
        [
            pl.BlockSpec((rows, depth), lambda j: (0, 0)),
            pl.BlockSpec((owners, owned, block), lambda j: (0, 0, j)),
            pl.BlockSpec((owners, owned, block), lambda j: (0, 1, j)),
        ],
        [
            pl.BlockSpec((2, rows, block), lambda j: (0, 0, j)),
            pl.BlockSpec((rows, block), lambda j: (0, j)),
        ],
        [
            jax.ShapeDtypeStruct((2, rows, hidden), F32),
            jax.ShapeDtypeStruct((rows, hidden), BF16),
        ],
        flops=4 * rows * depth * hidden,
        nbytes=4 * depth * hidden + rows * (10 * hidden + 2 * depth),
        trans=rows * hidden,
    )(x, weights, weights)


def down_kernel(x_ref, w_ref, out_ref):
    out_ref[...] = by_columns(x_ref[...], merged(w_ref[...])).astype(out_ref.dtype)


def down(x, weights, place, count, begin, rows, kind):
    owners, hidden = weights.shape[0], weights.shape[2]
    group = max(1, min(owners, 512 // count))
    at, row = begin // rows, place // count
    return call(
        down_kernel,
        (owners // group,),
        [
            pl.BlockSpec((rows, hidden), lambda j: (at, 0)),
            pl.BlockSpec((group, count, hidden), lambda j: (j, row, 0)),
        ],
        pl.BlockSpec((rows, group * count), lambda j: (0, j)),
        jax.ShapeDtypeStruct((rows, owners * count), kind),
        flops=2 * rows * owners * count * hidden,
        nbytes=2 * owners * count * hidden + rows * (2 * hidden + 4 * owners * count),
    )(x, weights)


def act_back_kernel(cuts, x_ref, *refs):
    weights, (gu_ref, out_ref, split) = refs[: len(cuts)], refs[len(cuts) :]
    owners = weights[0].shape[0]
    owned = x_ref.shape[1] // owners

    @pl.when(pl.program_id(0) == 0)
    def _():
        to = 0
        for begin, count in cuts:
            for i in range(owners):
                at = i * owned + begin
                split[:, to : to + count] = x_ref[:, at : at + count]
                to += count

    grad, at = 0.0, 0
    for (_, count), ref in zip(cuts, weights):
        grad = grad + matmul(split[:, at : at + owners * count], merged(ref[...]))
        at += owners * count
    gate, up = gu_ref[0], gu_ref[1]
    sig = jax.nn.sigmoid(gate)
    out_ref[0] = (grad * up * sig * (1.0 + gate * (1.0 - sig))).astype(BF16)
    out_ref[1] = (grad * gate * sig).astype(BF16)


def act_back(x, pieces, gate_and_up):
    rows, depth = x.shape
    hidden = gate_and_up.shape[2]
    block = min(hidden, 512)
    pair = pl.BlockSpec((2, rows, block), lambda j: (0, 0, j))
    return call(
        functools.partial(act_back_kernel, [(first, count) for _, _, count, first in pieces]),
        (hidden // block,),
        [pl.BlockSpec((rows, depth), lambda j: (0, 0))]
        + [
            pl.BlockSpec((array.shape[0], count, block), lambda j, at=place // count: (0, at, j))
            for array, place, count, _ in pieces
        ]
        + [pair],
        pair,
        jax.ShapeDtypeStruct((2, rows, hidden), BF16),
        [pltpu.VMEM((rows, depth), BF16)],
        flops=2 * rows * depth * hidden,
        nbytes=2 * depth * hidden + rows * (12 * hidden + 2 * depth),
        trans=rows * hidden,
    )(x, *[array for array, _, _, _ in pieces], gate_and_up)


def hidden_back_kernel(x_ref, wg_ref, wu_ref, out_ref):
    total = by_columns(x_ref[0], merged(wg_ref[...])) + by_columns(x_ref[1], merged(wu_ref[...]))
    out_ref[...] = total.astype(out_ref.dtype)


def hidden_back(grads, weights, owned, begin, rows, kind):
    hidden, owners = grads.shape[2], weights.shape[0]
    group = max(1, (512 if rows <= 512 else 256) // owned)
    at = begin // rows
    return call(
        hidden_back_kernel,
        (owners // group,),
        [
            pl.BlockSpec((2, rows, hidden), lambda j: (0, at, 0)),
            pl.BlockSpec((group, owned, hidden), lambda j: (j, 0, 0)),
            pl.BlockSpec((group, owned, hidden), lambda j: (j, 1, 0)),
        ],
        pl.BlockSpec((rows, group * owned), lambda j: (0, j)),
        jax.ShapeDtypeStruct((rows, owners * owned), kind),
        flops=4 * rows * owners * owned * hidden,
        nbytes=4 * owners * owned * hidden + rows * (4 * hidden + 4 * owners * owned),
    )(grads, weights, weights)


def total_of(refs):
    return functools.reduce(jnp.add, [ref[...].astype(F32) for ref in refs])


def norm_back(grad, gain, values, scale):
    weighted = grad * gain
    inner = jnp.sum(weighted * values, axis=1, keepdims=True)
    back = scale * weighted - values * scale**3 * inner / D
    return back, jnp.sum(grad * values * scale, axis=0, keepdims=True)


def result_kernel(counts, owners, *refs):
    begin, parts = 0, []
    for count in counts:
        parts.append(total_of(refs[begin : begin + count]))
        begin += count
    hidden_ref, grad_ref, gain_ref, out_ref, back_ref, gain_grad_ref = refs[begin:]
    if len(parts) == 1:
        result = parts[0]
    else:
        width = parts[0].shape[1] // owners
        result = jnp.concatenate(
            [part[:, i * width : (i + 1) * width] for i in range(owners) for part in parts], axis=1
        )
    scale = lax.rsqrt(jnp.mean(result * result, axis=1, keepdims=True) + NORM_EPS)
    gain = gain_ref[...]
    out_ref[...] = (hidden_ref[...] + result * scale * gain).astype(BF16)
    back, gain_grad = norm_back(grad_ref[...].astype(F32), gain, result, scale)
    back_ref[...] = back.astype(BF16)
    gain_grad_ref[0] = gain_grad


def result_step(parts, owners, hidden_in, grad_out, gain):
    rows, depth = hidden_in.shape
    block = min(rows, 64)
    mine = pl.BlockSpec((block, depth), lambda i: (i, 0))
    flat = [array for part in parts for array in part]
    return call(
        functools.partial(result_kernel, [len(part) for part in parts], owners),
        (rows // block,),
        [pl.BlockSpec((block, array.shape[1]), lambda i: (i, 0)) for array in flat]
        + [mine, mine, pl.BlockSpec((1, depth), lambda i: (0, 0))],
        [mine, mine, pl.BlockSpec((1, 1, depth), lambda i: (i, 0, 0))],
        [
            jax.ShapeDtypeStruct((rows, depth), BF16),
            jax.ShapeDtypeStruct((rows, depth), BF16),
            jax.ShapeDtypeStruct((rows // block, 1, depth), F32),
        ],
        flops=rows * depth * 20,
        nbytes=rows * depth * 20,
    )(*flat, hidden_in, grad_out, gain[None])


def branch_back_kernel(count, *refs):
    branch_ref, grad_ref, gain_ref, hidden_ref, back_ref, gain_grad_ref = refs[count:]
    grad = grad_ref[...].astype(F32) + total_of(refs[:count])
    hidden_ref[...] = grad
    branch = branch_ref[...]
    scale = lax.rsqrt(jnp.mean(branch * branch, axis=1, keepdims=True) + NORM_EPS)
    back, gain_grad = norm_back(grad, gain_ref[...], branch, scale)
    back_ref[...] = back.astype(BF16)
    gain_grad_ref[0] = gain_grad


def branch_back(parts, branch, grad_out, gain):
    rows, depth = branch.shape
    block = min(rows, 64)
    mine = pl.BlockSpec((block, depth), lambda i: (i, 0))
    return call(
        functools.partial(branch_back_kernel, len(parts)),
        (rows // block,),
        [mine] * (len(parts) + 2) + [pl.BlockSpec((1, depth), lambda i: (0, 0))],
        [mine, mine, pl.BlockSpec((1, 1, depth), lambda i: (i, 0, 0))],
        [
            jax.ShapeDtypeStruct((rows, depth), F32),
            jax.ShapeDtypeStruct((rows, depth), BF16),
            jax.ShapeDtypeStruct((rows // block, 1, depth), F32),
        ],
        flops=rows * depth * 20,
        nbytes=rows * depth * 20,
    )(*parts, branch, grad_out, gain[None])


def input_back_kernel(places_ref, x_ref, w_ref, residual_ref, out_ref):
    out_ref[...] = by_columns(x_ref[...], w_ref[...]).astype(out_ref.dtype)

    @pl.when(pl.program_id(1) == places_ref[0])
    def _():
        total = by_columns(x_ref[...], w_ref[...]) + residual_ref[...]
        out_ref[...] = total.astype(out_ref.dtype)


def input_back(grads, weights, residual, mine, distances, kind):
    rows, deep = grads.shape
    own = residual.shape[0]
    width = deep // 3
    blocks = rows // own
    places = jnp.stack([mine] + [mine ^ k for k in distances])
    return call(
        input_back_kernel,
        (len(distances), blocks),
        [
            pl.BlockSpec((own, deep), lambda a, i, p: (i, 0)),
            pl.BlockSpec((width, deep), lambda a, i, p: (p[1 + a], 0)),
            pl.BlockSpec((own, width), lambda a, i, p: (0, p[1 + a])),
        ],
        pl.BlockSpec((own, width), lambda a, i, p: (a * blocks + i, 0)),
        jax.ShapeDtypeStruct((len(distances) * rows, width), kind),
        flops=2 * rows * deep * width * len(distances),
        nbytes=rows * deep * 2 * (len(distances) + 1),
        scalars=1,
    )(places, grads, weights, residual)


def body(
    inputs,
    cotangent,
    doc_lengths,
    attn_weights,
    mlp_weights,
    norm_gains,
    attn_first,
    attn_second,
    mlp_first,
    mlp_second,
    gain_first,
    gain_second,
):
    owners = ("dp", "ctx")
    n = lax.axis_size("tensor")
    mine = lax.axis_index("tensor")
    rows, width = inputs.shape
    own = rows // n
    hidden = mlp_weights.shape[2]

    low = attn_weights.astype(BF16)
    attn_shard = jnp.concatenate([low[0], low[1], low[2], low[3]], axis=1)
    low = mlp_weights.astype(BF16)
    owned = low.shape[1]
    lead = owned // 2 if owned % 256 == 0 else 0
    up_shard = jnp.concatenate([low[0], low[1], low[2, :lead]], axis=0)
    attn_full = lax.all_gather(attn_shard, owners, axis=0, tiled=True)
    up_full = lax.all_gather(up_shard, owners, axis=0)
    down_full = lax.all_gather(low[2, lead:], owners, axis=0)
    down_pieces = [(down_full, 0, owned - lead, lead)]
    if lead:
        down_pieces = [(up_full, 2 * owned, lead, 0)] + down_pieces
    w_qkv, w_out = attn_full[:, : 3 * width], attn_full[:, 3 * width :]
    gains = lax.all_gather(
        norm_gains.astype(BF16), ("tensor",) + owners, axis=1, tiled=True
    ).astype(F32)
    gain_attn, gain_mlp = gains[2], gains[3]
    near = lax.dynamic_slice_in_dim(gains, mine * width, width, axis=1)
    gain_query, gain_key = near[0], near[1]

    gathered = jnp.zeros((rows, n * width), BF16)
    order = piece_order()
    for k, piece in zip(order, gather_pieces(inputs)):
        gathered = lax.dynamic_update_slice(gathered, piece, (0, (mine ^ k) * width))
    grad_out = jnp.zeros((own, n * width), BF16)
    for k in range(n):
        piece = lax.dynamic_slice_in_dim(cotangent, (mine ^ k) * own, own, axis=0)
        piece = swap(piece, k) if k else piece
        grad_out = lax.dynamic_update_slice(grad_out, piece, (0, (mine ^ k) * width))

    offset = lax.axis_index("ctx") * rows
    token_place = offset + jnp.arange(rows, dtype=jnp.int32)
    begins = doc_begins(doc_lengths[0], token_place)
    cosine, sine = turn_tables(token_place - begins)
    start = begins - offset

    qkv = matmul(after(gathered, grad_out), w_qkv)
    queries, key_proj = qkv[:, :width], qkv[:, width : 2 * width]
    squares = axis_total(
        jnp.stack([jnp.sum(queries * queries, axis=1), jnp.sum(key_proj * key_proj, axis=1)]),
        "tensor",
    )
    qk_rs = lax.rsqrt(squares / D + NORM_EPS).T
    query_low, key_low, value_low = rope(qkv, qk_rs, gain_query, gain_key, cosine, sine)
    all_keys = jnp.concatenate([passed_along(key_low, "ctx", 1), key_low], axis=0)
    all_values = jnp.concatenate([passed_along(value_low, "ctx", 1), value_low], axis=0)
    attn_low, log_total = attend(query_low, all_keys, all_values, start)

    parts = [
        by_columns(lax.dynamic_slice_in_dim(attn_low, (mine ^ k) * own, own, axis=0), w_out)
        for k in order
    ]
    branch = add_up(scatter_pieces(parts))
    branch_rs = lax.rsqrt(jnp.mean(branch * branch, axis=1, keepdims=True) + NORM_EPS)
    my_rows = lax.dynamic_slice_in_dim(gathered, mine * own, own, axis=0)
    hidden_in = my_rows.astype(F32) + branch * branch_rs * gain_attn
    hidden_low = jnp.concatenate(gather_pieces(hidden_in.astype(BF16)), axis=0)
    gate_and_up, act_low = gate_up(hidden_low, up_full, owned)
    terms, done, near = [], (), []
    for array, place, count, _ in down_pieces:
        array = after(array, *done)
        piece = lambda x, begin, size, kind: down(x, array, place, count, begin, size, kind)
        if n == 4:
            last = piece(act_low, own, own, BF16)
            passing = send_far(last)
            pair = piece(after(act_low, last, *near), 2 * own, 2 * own, F32)
            first = piece(after(act_low, pair), 0, own, F32)
            sent, near = send_near(pair, passing)
            terms.append([first] + near)
            done = (first, sent)
        else:
            parts = piece(act_low, 0, rows, F32)
            terms.append(scatter_pieces([parts[k * own : (k + 1) * own] for k in range(n)]))
    output_low, grad_result, gain_mlp_parts = result_step(
        terms, down_full.shape[0], hidden_in, grad_out, gain_mlp
    )
    grad_gain_mlp = jnp.sum(gain_mlp_parts, axis=(0, 1))
    grad_result_all = jnp.concatenate(gather_pieces(grad_result), axis=0)
    down_sums = contract_rows(grad_result_all, act_low).astype(BF16)
    owned_down = scatter_owned(down_sums, owners)
    grad_gate_up = act_back(after(grad_result_all, down_sums), down_pieces, gate_and_up)
    ctx = lax.axis_index("ctx")
    if n == 4:
        last = hidden_back(grad_gate_up, up_full, owned, own, own, BF16)
        passing = send_far(last)
        given = weight_half(hidden_low, after(grad_gate_up, last), 1 - ctx)
        pair = hidden_back(after(grad_gate_up, given), up_full, owned, 2 * own, 2 * own, F32)
        sent, near = send_near(pair, passing)
        first = hidden_back(after(grad_gate_up, sent), up_full, owned, 0, own, F32)
        terms = [first] + near
    else:
        first = hidden_back(grad_gate_up, up_full, owned, 0, rows, F32)
        given = weight_half(hidden_low, after(grad_gate_up, first), 1 - ctx)
        terms = scatter_pieces([first[k * own : (k + 1) * own] for k in range(n)])
    up_sums = weight_half(hidden_low, grad_gate_up, ctx, other_core(given))
    grad_hidden, grad_branch, gain_attn_parts = branch_back(
        terms, after(branch, up_sums), grad_out, gain_attn
    )
    grad_gain_attn = jnp.sum(gain_attn_parts, axis=(0, 1))
    owned_up = scatter_owned(merged(after(up_sums, owned_down)))
    grad_branch_all = jnp.zeros((rows, n * width), BF16)
    for k, piece in zip(order, gather_pieces(grad_branch)):
        grad_branch_all = lax.dynamic_update_slice(grad_branch_all, piece, ((mine ^ k) * own, 0))
    grad_mixed = matmul(grad_branch_all, w_out).astype(BF16)
    dq, dkp, dvp, dk, dv = attend_back(
        query_low, all_keys, all_values, grad_mixed, log_total.T, start
    )
    back_key = passed_along(dkp, "ctx", -1)
    back_value = passed_along(dvp, "ctx", -1)
    given = other_core(weight_half(after(grad_branch_all, dkp), attn_low, 1 - ctx))
    weighted_q, weighted_k, grad_v, inner, gain_parts = unrope(
        dq, dk, dv, back_key, back_value, qkv, qk_rs, gain_query, gain_key, cosine, sine
    )
    out_sums = weight_half(after(grad_branch_all, inner), attn_low, ctx, given)
    inner = after(axis_total(inner.T, "tensor").T, out_sums)
    grad_q = qk_rs[:, :1] * weighted_q - queries * qk_rs[:, :1] ** 3 * inner[:, :1] / D
    grad_k = qk_rs[:, 1:] * weighted_k - key_proj * qk_rs[:, 1:] ** 3 * inner[:, 1:] / D
    grad_qkv = jnp.concatenate([grad_q.astype(BF16), grad_k.astype(BF16), grad_v], axis=1)
    given = weight_half(gathered, grad_qkv, 1 - ctx)
    near_inputs = lambda source, distances, kind: input_back(
        source, attn_full, grad_hidden, mine, distances, kind
    )
    if n == 4:
        last = near_inputs(after(grad_qkv, given), order[1:2], BF16)
        passing = send_far(last)
        attn_sums = weight_half(
            gathered, after(grad_qkv, last), ctx, other_core(given), out_sums
        )
        pair = near_inputs(after(grad_qkv, attn_sums), order[2:], F32)
        sent, near = send_near(pair, passing)
    else:
        attn_sums = weight_half(gathered, grad_qkv, ctx, other_core(given), out_sums)
        parts = near_inputs(grad_qkv, order, F32)
        sent = parts
    owned_attn = scatter_owned(merged(after(attn_sums, owned_up)))
    owned_up = after(owned_up, sent).astype(F32)
    mlp_grad = jnp.stack([owned_up[:, :hidden], owned_up[:, hidden:], owned_down.astype(F32)])
    new_mlp, mlp_one, mlp_two = adam_step(
        mlp_weights, mlp_grad, mlp_first, mlp_second, LEARN_RATE, WEIGHT_DECAY
    )
    if n == 4:
        grad_inputs = add_up([near_inputs(after(grad_qkv, new_mlp), order[:1], F32)] + near)
    else:
        grad_inputs = add_up(scatter_pieces([parts[k * rows : (k + 1) * rows] for k in range(n)]))

    wide = jnp.stack([grad_gain_attn, grad_gain_mlp])
    near = lax.dynamic_slice_in_dim(wide, mine * width, width, axis=1)
    for k in range(1, n):
        near = near + swap(lax.dynamic_slice_in_dim(wide, (mine ^ k) * width, width, axis=1), k)
    gain_sums = jnp.concatenate([jnp.sum(gain_parts, axis=0), near])
    gain_sums = axis_total(axis_total(gain_sums, "ctx"), "dp")
    share = norm_gains.shape[1]
    place = (lax.axis_index("dp") * lax.axis_size("ctx") + lax.axis_index("ctx")) * share
    gain_grad = lax.dynamic_slice_in_dim(gain_sums, place, share, axis=1)

    output = jnp.zeros((rows, width), BF16)
    for k in range(n):
        piece = lax.dynamic_slice_in_dim(output_low, (mine ^ k) * width, width, axis=1)
        piece = swap(piece, k) if k else piece
        output = lax.dynamic_update_slice(output, piece, ((mine ^ k) * own, 0))

    owned_attn = owned_attn.astype(F32)
    attn_grad = jnp.stack([owned_attn[:, i * width : (i + 1) * width] for i in range(4)])
    new_attn, attn_one, attn_two = adam_step(
        attn_weights, attn_grad, attn_first, attn_second, LEARN_RATE, WEIGHT_DECAY
    )
    new_gains, gain_one, gain_two = adam_step(
        norm_gains, gain_grad, gain_first, gain_second, GAIN_RATE, 0.0
    )
    return (
        output,
        grad_inputs,
        new_attn,
        attn_one,
        attn_two,
        new_mlp,
        mlp_one,
        mlp_two,
        new_gains,
        gain_one,
        gain_two,
    )


def solution(mesh):
    return jax.shard_map(
        body,
        mesh=mesh,
        in_specs=(
            P(("dp", "ctx"), "tensor"),
            P(("dp", "ctx"), "tensor"),
            P("dp", None),
            P(None, ("dp", "ctx"), "tensor"),
            P(None, ("dp", "ctx"), "tensor"),
            P(None, ("tensor", "dp", "ctx")),
            P(None, ("dp", "ctx"), "tensor"),
            P(None, ("dp", "ctx"), "tensor"),
            P(None, ("dp", "ctx"), "tensor"),
            P(None, ("dp", "ctx"), "tensor"),
            P(None, ("tensor", "dp", "ctx")),
            P(None, ("tensor", "dp", "ctx")),
        ),
        out_specs=(
            P(("dp", "ctx"), "tensor"),
            P(("dp", "ctx"), "tensor"),
            P(None, ("dp", "ctx"), "tensor"),
            P(None, ("dp", "ctx"), "tensor"),
            P(None, ("dp", "ctx"), "tensor"),
            P(None, ("dp", "ctx"), "tensor"),
            P(None, ("dp", "ctx"), "tensor"),
            P(None, ("dp", "ctx"), "tensor"),
            P(None, ("tensor", "dp", "ctx")),
            P(None, ("tensor", "dp", "ctx")),
            P(None, ("tensor", "dp", "ctx")),
        ),
        check_vma=False,
    )
```

```python
import functools

import jax
import jax.numpy as jnp
from jax import lax
from jax.experimental import pallas as pl
from jax.experimental.pallas import tpu as pltpu
from jax.sharding import PartitionSpec as P

D = 2048
HEAD_DIM = 128
STEP = 10


NORM_EPS = 1e-06
ROPE_THETA = 500000.0
BETA_ONE = 0.9
BETA_TWO = 0.95
ADAM_EPS = 1e-08
WEIGHT_DECAY = 0.1
LEARN_RATE = 0.02
GAIN_RATE = 1.0

SCORE_SCALE = HEAD_DIM ** (-0.5)
Q_BLOCK = 256
VMEM = 32
BF16 = jnp.bfloat16
F32 = jnp.float32


def passed_along(block, axis, distance):
    devices = range(lax.axis_size(axis))
    route = [(i - distance, i) for i in devices if i - distance in devices]
    return lax.ppermute(block, axis, route)


def swap(block, distance):
    return lax.ppermute(
        block, "tensor", [(i, i ^ distance) for i in range(lax.axis_size("tensor"))]
    )


def piece_order():
    n = lax.axis_size("tensor")
    return (0, 3, 1, 2) if n == 4 else tuple(range(n))


def gather_pieces(block, finely=False):
    n = lax.axis_size("tensor")
    if n != 4:
        return [block] + [swap(block, k) for k in range(1, n)]
    half = block.shape[0] // 2
    if not finely:
        one, two = swap(block, 1), swap(block, 2)
        return [block, swap(two[:half], 1), swap(one[half:], 2), one, two]
    upper, lower = block[:half], block[half:]
    two_upper, one_lower = swap(upper, 2), swap(lower, 1)
    one_upper, two_lower = swap(upper, 1), swap(lower, 2)
    far_upper, far_lower = swap(two_upper, 1), swap(one_lower, 2)
    return [
        jnp.concatenate(pair, axis=0)
        for pair in ((upper, lower), (far_upper, far_lower), (one_upper, one_lower), (two_upper, two_lower))
    ]


def send_far(last):
    half = last.shape[0] // 2
    last = last.astype(BF16)
    upper = swap(last[:half], 1)
    lower = swap(last[half:], 2)
    return jnp.concatenate([lower, upper], axis=0)


def near_blocks(pair, passing):
    rows = pair.shape[0] // 2
    passing = jnp.pad(passing.astype(F32), ((rows // 2, rows // 2), (0, 0)))
    return (pair + passing).astype(BF16)


def send_near(pair, passing):
    rows = pair.shape[0] // 2
    pair = near_blocks(pair, passing)
    return pair, [swap(pair[:rows], 1), swap(pair[rows:], 2)]


def scatter_pieces(parts):
    if lax.axis_size("tensor") == 4:
        passing = send_far(parts[1])
        return [parts[0]] + send_near(jnp.concatenate(parts[2:], axis=0), passing)[1]
    total = parts[0]
    for k in range(1, len(parts)):
        total = total + swap(parts[k].astype(BF16), k).astype(F32)
    return [total]


def add_up(terms):
    return functools.reduce(jnp.add, [term.astype(F32) for term in terms])


def axis_total(values, axis):
    n = lax.axis_size(axis)
    flat = values.reshape(-1, HEAD_DIM)
    others = [
        lax.ppermute(flat, axis, [(i, i ^ k if n in (2, 4, 8) else (i + k) % n) for i in range(n)])
        for k in range(1, n)
    ]
    return functools.reduce(jnp.add, others, flat).reshape(values.shape)


def doc_begins(doc_row, token_place):
    doc_ends = jnp.cumsum(doc_row)
    passed = token_place[:, None] >= doc_ends[None, :]
    return jnp.max(
        jnp.where(passed, doc_ends[None, :], jnp.zeros_like(doc_ends)[None, :]), axis=1
    )


def turn_tables(position):
    half_dim = HEAD_DIM // 2
    frequency = ROPE_THETA ** (-2.0 * jnp.arange(half_dim, dtype=F32) / HEAD_DIM)
    angles = position.astype(F32)[:, None] * frequency[None, :]
    cosine, sine = jnp.cos(angles), jnp.sin(angles)
    return jnp.concatenate([cosine, cosine], axis=1), jnp.concatenate([-sine, sine], axis=1)


def adam_step(weight, gradient, moment_one, moment_two, rate, decay):
    moment_one = BETA_ONE * moment_one + (1.0 - BETA_ONE) * gradient
    moment_two = BETA_TWO * moment_two + (1.0 - BETA_TWO) * gradient * gradient
    fix_one = 1.0 - BETA_ONE**STEP
    fix_two = 1.0 - BETA_TWO**STEP
    update = moment_one / fix_one / (jnp.sqrt(moment_two / fix_two) + ADAM_EPS)
    return (weight - rate * (update + decay * weight), moment_one, moment_two)


def adam_kernel(grad_ref, weight_ref, first_ref, second_ref, *rest):
    wide = weight_ref.shape[2]
    for i in range(weight_ref.shape[0]):
        grad = grad_ref[:, i * wide : (i + 1) * wide].astype(F32)
        new = adam_step(
            weight_ref[i], grad, first_ref[i], second_ref[i], LEARN_RATE, WEIGHT_DECAY
        )
        for ref, value in zip(rest[-3:], new):
            ref[i] = value


def adam(grad, weights, first, second, begin, count, earlier=()):
    _, rows, wide = weights.shape
    block = min(wide, 1024)
    group = max(1, min(count, 1024 // block))
    steps, at = wide // block, begin // group
    spec = pl.BlockSpec((group, rows, block), lambda k, j: (at + k, 0, j))
    return pl.pallas_call(
        adam_kernel,
        grid=(count // group, steps),
        in_specs=[
            pl.BlockSpec((rows, group * block), lambda k, j: (0, k * steps + j)), spec, spec, spec
        ]
        + [pl.BlockSpec(memory_space=pl.ANY)] * len(earlier),
        out_specs=[spec] * 3,
        out_shape=[jax.ShapeDtypeStruct(weights.shape, F32)] * 3,
        input_output_aliases={4 + i: i for i in range(len(earlier))},
        compiler_params=pltpu.CompilerParams(vmem_limit_bytes=60 * 1024 * 1024),
        cost_estimate=pl.CostEstimate(
            flops=0, bytes_accessed=count * rows * wide * 26, transcendentals=0
        ),
    )(grad, weights, first, second, *earlier)


def matmul(left, right):
    return jnp.dot(left, right, preferred_element_type=F32)


def contract_rows(left, right):
    return lax.dot_general(left, right, (((0,), (0,)), ((), ())), preferred_element_type=F32)


def by_columns(left, right):
    return lax.dot_general(left, right, (((1,), (1,)), ((), ())), preferred_element_type=F32)


def after(value, *earlier):
    return lax.optimization_barrier((value,) + earlier)[0]


def other_core(values):
    return lax.ppermute(values, "ctx", [(0, 1), (1, 0)])


def scatter_owned(sums, axes=("dp",)):
    return lax.psum_scatter(sums, axes, scatter_dimension=0, tiled=True)


def call(
    kernel, grid, in_specs, out_specs, out_shape, scratch=(), flops=0, nbytes=0, trans=0, scalars=0,
    announced=0.25, vmem=VMEM,
):
    return pl.pallas_call(
        kernel,
        grid_spec=pltpu.PrefetchScalarGridSpec(
            num_scalar_prefetch=scalars,
            grid=grid,
            in_specs=in_specs,
            out_specs=out_specs,
            scratch_shapes=list(scratch),
        ),
        out_shape=out_shape,
        compiler_params=pltpu.CompilerParams(vmem_limit_bytes=vmem * 1024 * 1024),
        cost_estimate=pl.CostEstimate(
            flops=int(flops * announced),
            bytes_accessed=int(nbytes * announced),
            transcendentals=int(trans * announced),
        ),
    )


def weight_half_kernel(blocks, steps, ctx_ref, *refs):
    left, right_ref, (out_ref, turned) = refs[:blocks], refs[blocks], refs[-2:]
    given_ref = refs[blocks + 1] if len(refs) > blocks + 3 else None
    tail_ref = refs[blocks + 2] if len(refs) > blocks + 4 else None

    @pl.when(pl.program_id(0) == 0)
    def _():
        for i, ref in enumerate(left):
            turned[i] = ref[...].T

    @pl.when(pl.program_id(0) < steps)
    def _():
        right = right_ref[...]
        for i in range(blocks):
            total = matmul(turned[i], right)
            if given_ref is not None:
                total = total + given_ref[i].astype(F32)
            out_ref[i] = total.astype(BF16)

    if tail_ref is not None:

        @pl.when(pl.program_id(0) >= steps)
        def _():
            out_ref[...] = tail_ref[...]


def weight_half(left, right, ctx, given=None, tail=None):
    rows, depth = left.shape
    blocks = lax.axis_size("dp")
    owned = depth // (blocks * lax.axis_size("ctx"))
    n_ctx = lax.axis_size("ctx")
    wide = right.shape[-1]
    block = next(size for size in (512, 256, 128) if wide % size == 0)
    each = wide // block
    steps = each * (right.shape[0] if right.ndim == 3 else 1)
    last = steps - 1
    if right.ndim == 3:
        right_spec = pl.BlockSpec((None, rows, block), lambda j, c: (j // each, 0, j % each))
    else:
        right_spec = pl.BlockSpec((rows, block), lambda j, c: (0, jnp.minimum(j, last)))
    specs = [
        pl.BlockSpec((rows, owned), lambda j, c, i=i: (0, n_ctx * i + c[0])) for i in range(blocks)
    ]
    operands = [left] * blocks + [right]
    specs.append(right_spec)
    columns = steps * block
    more = 0
    if given is not None:
        operands.append(given)
        specs.append(
            pl.BlockSpec((blocks, owned, block), lambda j, c: (0, 0, jnp.minimum(j, last)))
        )
    if tail is not None:
        operands.append(tail)
        more = tail.shape[2] // block
        specs.append(
            pl.BlockSpec((blocks, owned, block), lambda j, c: (0, 0, jnp.maximum(j - steps, 0)))
        )
    return call(
        functools.partial(weight_half_kernel, blocks, steps),
        (steps + more,),
        specs,
        pl.BlockSpec((blocks, owned, block), lambda j, c: (0, 0, j)),
        jax.ShapeDtypeStruct((blocks, owned, columns + more * block), BF16),
        [pltpu.VMEM((blocks, owned, rows), BF16)],
        flops=2 * rows * blocks * owned * columns,
        nbytes=2 * (rows * blocks * owned + rows * columns + 2 * blocks * owned * columns),
        scalars=1,
    )(ctx[None], *operands)


def rope_kernel(q_ref, k_ref, v_ref, rs_ref, gq_ref, gk_ref, cos_ref, sin_ref, qo, ko, vo):
    cosine, sine = cos_ref[...], sin_ref[...]
    for place, (src, gain, dst) in enumerate(((q_ref, gq_ref, qo), (k_ref, gk_ref, ko))):
        scale = rs_ref[:, place : place + 1]
        for head in range(src.shape[1] // HEAD_DIM):
            cols = slice(head * HEAD_DIM, (head + 1) * HEAD_DIM)
            x = src[:, cols] * scale * gain[:, cols]
            dst[:, cols] = (x * cosine + pltpu.roll(x, HEAD_DIM // 2, 1) * sine).astype(BF16)
    vo[...] = v_ref[...].astype(BF16)


def rope(qkv, rs, gain_query, gain_key, cosine, sine):
    rows, width = qkv.shape[0], qkv.shape[1] // 3
    block = min(rows, 256)
    part = lambda j: pl.BlockSpec((block, width), lambda i, j=j: (i, j))
    gain = pl.BlockSpec((1, width), lambda i: (0, 0))
    table = pl.BlockSpec((block, HEAD_DIM), lambda i: (i, 0))
    out = jax.ShapeDtypeStruct((rows, width), BF16)
    return call(
        rope_kernel,
        (rows // block,),
        [part(0), part(1), part(2), pl.BlockSpec((block, 2), lambda i: (i, 0)), gain, gain]
        + [table, table],
        [part(0)] * 3,
        [out] * 3,
        flops=rows * width * 12,
        nbytes=rows * width * 18,
    )(qkv, qkv, qkv, rs, gain_query[None], gain_key[None], cosine, sine)


def attend_kernel(span, q_ref, k_ref, v_ref, start_ref, o_ref, lse_ref):
    rows = q_ref.shape[0]
    step = pl.program_id(0)
    first = pl.multiple_of(step * rows, rows)
    shape = (rows, span)
    row = lax.broadcasted_iota(jnp.int32, shape, 0)
    column = lax.broadcasted_iota(jnp.int32, shape, 1) - (span - rows)
    allowed = (column <= row) & (column >= start_ref[...] - step * rows)
    for head in range(q_ref.shape[1] // HEAD_DIM):
        cols = slice(head * HEAD_DIM, (head + 1) * HEAD_DIM)
        keys = k_ref[pl.ds(first, span), cols]
        values = v_ref[pl.ds(first, span), cols]
        scores = by_columns(q_ref[:, cols], keys) * SCORE_SCALE
        scores = jnp.where(allowed, scores, -1e30)
        top = jnp.max(scores, axis=1, keepdims=True)
        weights = jnp.exp(scores - top)
        total = jnp.sum(weights, axis=1, keepdims=True)
        low = (weights / total).astype(BF16)
        o_ref[:, cols] = matmul(low, values).astype(BF16)
        lse_ref[:, head : head + 1] = top + jnp.log(total)


def attend(query, keys, values, start):
    rows, width = query.shape
    heads = width // HEAD_DIM
    block = Q_BLOCK
    span = rows + block
    whole = pl.BlockSpec(keys.shape, lambda i: (0, 0))
    return call(
        functools.partial(attend_kernel, span),
        (rows // block,),
        [pl.BlockSpec((block, width), lambda i: (i, 0)), whole, whole]
        + [pl.BlockSpec((block, 1), lambda i: (i, 0))],
        [pl.BlockSpec((block, width), lambda i: (i, 0)), pl.BlockSpec((block, heads), lambda i: (i, 0))],
        [jax.ShapeDtypeStruct((rows, width), BF16), jax.ShapeDtypeStruct((rows, heads), F32)],
        flops=4 * rows * span * width,
        nbytes=rows * width * 12,
        trans=rows * span * heads,
    )(query, keys, values, start[:, None])


def attend_back_kernel(
    span, q_ref, k_ref, v_ref, do_ref, lse_ref, start_ref, dq_ref, dkp_ref, dvp_ref, dk_ref, dv_ref, ka, va
):
    rows = q_ref.shape[0]
    step = pl.program_id(0)
    first = pl.multiple_of(step * rows, rows)

    @pl.when(step == 0)
    def _():
        ka[...] = jnp.zeros_like(ka)
        va[...] = jnp.zeros_like(va)

    shape = (span, rows)
    column = lax.broadcasted_iota(jnp.int32, shape, 0) - (span - rows)
    row = lax.broadcasted_iota(jnp.int32, shape, 1)
    allowed = (column <= row) & (column >= start_ref[...] - step * rows)
    for head in range(q_ref.shape[1] // HEAD_DIM):
        cols = slice(head * HEAD_DIM, (head + 1) * HEAD_DIM)
        query, grad = q_ref[:, cols], do_ref[:, cols]
        keys = k_ref[pl.ds(first, span), cols]
        values = v_ref[pl.ds(first, span), cols]
        scores = by_columns(keys, query) * SCORE_SCALE
        weights = jnp.where(allowed, jnp.exp(scores - lse_ref[head : head + 1, :]), 0.0)
        grad_weights = by_columns(values, grad)
        mean = jnp.sum(weights * grad_weights, axis=0, keepdims=True)
        grad_scores = (weights * (grad_weights - mean)).astype(BF16)
        dq_ref[:, cols] = contract_rows(grad_scores, keys) * SCORE_SCALE
        va[pl.ds(first, span), cols] += matmul(weights.astype(BF16), grad)
        ka[pl.ds(first, span), cols] += matmul(grad_scores, query) * SCORE_SCALE

    @pl.when(step == pl.num_programs(0) - 1)
    def _():
        total = dk_ref.shape[0]
        dkp_ref[...] = ka[:total, :].astype(BF16)
        dvp_ref[...] = va[:total, :].astype(BF16)
        dk_ref[...] = ka[total:, :]
        dv_ref[...] = va[total:, :]


def attend_back(query, keys, values, grad, lse, start):
    rows, width = query.shape
    heads = width // HEAD_DIM
    block = Q_BLOCK
    span = rows + block
    whole = pl.BlockSpec(keys.shape, lambda i: (0, 0))
    mine = pl.BlockSpec((block, width), lambda i: (i, 0))
    full = pl.BlockSpec((rows, width), lambda i: (0, 0))
    return call(
        functools.partial(attend_back_kernel, span),
        (rows // block,),
        [mine, whole, whole, mine]
        + [pl.BlockSpec((heads, block), lambda i: (0, i)), pl.BlockSpec((1, block), lambda i: (0, i))],
        [mine, full, full, full, full],
        [jax.ShapeDtypeStruct((rows, width), t) for t in (F32, BF16, BF16, F32, F32)],
        [pltpu.VMEM(keys.shape, F32)] * 2,
        flops=10 * rows * span * width,
        nbytes=rows * width * 28,
        trans=rows * span * heads,
        announced=12,
    )(query, keys, values, grad, lse, start[None, :])


def unrope_kernel(
    dq_ref, dk_ref, dv_ref, bk_ref, bv_ref, q_ref, k_ref, rs_ref, gq_ref, gk_ref, cos_ref, sin_ref,
    wq_ref, wk_ref, dvo_ref, inner_ref, gain_ref,
):
    cosine, sine = cos_ref[...], -sin_ref[...]
    for place, (src, back, x_ref, gain, dst) in enumerate(
        ((dq_ref, None, q_ref, gq_ref, wq_ref), (dk_ref, bk_ref, k_ref, gk_ref, wk_ref))
    ):
        scale = rs_ref[:, place : place + 1]
        inner = 0.0
        for head in range(src.shape[1] // HEAD_DIM):
            cols = slice(head * HEAD_DIM, (head + 1) * HEAD_DIM)
            grad = src[:, cols]
            if back is not None:
                grad = grad + back[:, cols].astype(F32)
            grad = grad * cosine + pltpu.roll(grad, HEAD_DIM // 2, 1) * sine
            x = x_ref[:, cols]
            weighted = grad * gain[:, cols]
            dst[:, cols] = weighted
            inner = inner + jnp.sum(weighted * x, axis=1, keepdims=True)
            gain_ref[0, place : place + 1, cols] = jnp.sum(grad * x * scale, axis=0, keepdims=True)
        inner_ref[:, place : place + 1] = inner
    dvo_ref[...] = (dv_ref[...] + bv_ref[...].astype(F32)).astype(BF16)


def unrope(dq, dk, dv, back_k, back_v, qkv, rs, gain_query, gain_key, cosine, sine):
    rows, width = dq.shape
    block = min(rows, 256)
    part = lambda j: pl.BlockSpec((block, width), lambda i, j=j: (i, j))
    gain = pl.BlockSpec((1, width), lambda i: (0, 0))
    table = pl.BlockSpec((block, HEAD_DIM), lambda i: (i, 0))
    pair = pl.BlockSpec((block, 2), lambda i: (i, 0))
    return call(
        unrope_kernel,
        (rows // block,),
        [part(0)] * 5 + [part(0), part(1), pair, gain, gain, table, table],
        [part(0)] * 3 + [pair, pl.BlockSpec((1, 2, width), lambda i: (i, 0, 0))],
        [jax.ShapeDtypeStruct((rows, width), t) for t in (F32, F32, BF16)]
        + [jax.ShapeDtypeStruct((rows, 2), F32)]
        + [jax.ShapeDtypeStruct((rows // block, 2, width), F32)],
        flops=rows * width * 30,
        nbytes=rows * width * 34,
    )(dq, dk, dv, back_k, back_v, qkv, qkv, rs, gain_query[None], gain_key[None], cosine, sine)


def merged(block):
    return block.reshape(-1, block.shape[-1])


def gate_up_kernel(x_ref, wg_ref, wu_ref, gu_ref, act_ref):
    x = x_ref[...]
    gate, up = matmul(x, merged(wg_ref[...])), matmul(x, merged(wu_ref[...]))
    gu_ref[0], gu_ref[1] = gate, up
    act_ref[...] = (gate * jax.nn.sigmoid(gate) * up).astype(BF16)


def gate_up(x, weights, owned):
    rows, depth = x.shape
    owners, hidden = weights.shape[0], weights.shape[2]
    block = min(hidden, 256)
    return call(
        gate_up_kernel,
        (hidden // block,),
        [
            pl.BlockSpec((rows, depth), lambda j: (0, 0)),
            pl.BlockSpec((owners, owned, block), lambda j: (0, 0, j)),
            pl.BlockSpec((owners, owned, block), lambda j: (0, 1, j)),
        ],
        [
            pl.BlockSpec((2, rows, block), lambda j: (0, 0, j)),
            pl.BlockSpec((rows, block), lambda j: (0, j)),
        ],
        [
            jax.ShapeDtypeStruct((2, rows, hidden), F32),
            jax.ShapeDtypeStruct((rows, hidden), BF16),
        ],
        flops=4 * rows * depth * hidden,
        nbytes=4 * depth * hidden + rows * (10 * hidden + 2 * depth),
        trans=rows * hidden,
    )(x, weights, weights)


def down_kernel(x_ref, w_ref, out_ref):
    out_ref[...] = by_columns(x_ref[...], merged(w_ref[...])).astype(out_ref.dtype)


def down(x, weights, place, count, begin, rows, kind):
    owners, hidden = weights.shape[0], weights.shape[2]
    group = max(1, min(owners, 512 // count))
    at, row = begin // rows, place // count
    return call(
        down_kernel,
        (owners // group,),
        [
            pl.BlockSpec((rows, hidden), lambda j: (at, 0)),
            pl.BlockSpec((group, count, hidden), lambda j: (j, row, 0)),
        ],
        pl.BlockSpec((rows, group * count), lambda j: (0, j)),
        jax.ShapeDtypeStruct((rows, owners * count), kind),
        flops=2 * rows * owners * count * hidden,
        nbytes=2 * owners * count * hidden + rows * (2 * hidden + 4 * owners * count),
    )(x, weights)


def act_back_kernel(cuts, count_x, *refs):
    blocks, weights = refs[:count_x], refs[count_x : count_x + len(cuts)]
    gu_ref, out_ref, split = refs[count_x + len(cuts) :]
    owners = weights[0].shape[0]
    owned = split.shape[1] // owners

    @pl.when(pl.program_id(0) == 0)
    def _():
        row = 0
        for x_ref in blocks:
            rows, to = slice(row, row + x_ref.shape[0]), 0
            row += x_ref.shape[0]
            for begin, count in cuts:
                for i in range(owners):
                    at = i * owned + begin
                    split[rows, to : to + count] = x_ref[:, at : at + count]
                    to += count

    grad, at = 0.0, 0
    for (_, count), ref in zip(cuts, weights):
        grad = grad + matmul(split[:, at : at + owners * count], merged(ref[...]))
        at += owners * count
    gate, up = gu_ref[0], gu_ref[1]
    sig = jax.nn.sigmoid(gate)
    out_ref[0] = (grad * up * sig * (1.0 + gate * (1.0 - sig))).astype(BF16)
    out_ref[1] = (grad * gate * sig).astype(BF16)


def act_back(blocks, pieces, gate_and_up):
    _, rows, hidden = gate_and_up.shape
    depth = blocks[0].shape[1]
    block = min(hidden, 512)
    pair = pl.BlockSpec((2, rows, block), lambda j: (0, 0, j))
    return call(
        functools.partial(
            act_back_kernel, [(first, count) for _, _, count, first in pieces], len(blocks)
        ),
        (hidden // block,),
        [pl.BlockSpec(array.shape, lambda j: (0, 0)) for array in blocks]
        + [
            pl.BlockSpec((array.shape[0], count, block), lambda j, at=place // count: (0, at, j))
            for array, place, count, _ in pieces
        ]
        + [pair],
        pair,
        jax.ShapeDtypeStruct((2, rows, hidden), BF16),
        [pltpu.VMEM((rows, depth), BF16)],
        flops=2 * rows * depth * hidden,
        nbytes=2 * depth * hidden + rows * (12 * hidden + 2 * depth),
        trans=rows * hidden,
    )(*blocks, *[array for array, _, _, _ in pieces], gate_and_up)


def hidden_back_kernel(x_ref, wg_ref, wu_ref, out_ref):
    total = by_columns(x_ref[0], merged(wg_ref[...])) + by_columns(x_ref[1], merged(wu_ref[...]))
    out_ref[...] = total.astype(out_ref.dtype)


def hidden_back(grads, weights, owned, begin, rows, kind):
    hidden, owners = grads.shape[2], weights.shape[0]
    group = max(1, (512 if rows <= 512 else 256) // owned)
    at = begin // rows
    return call(
        hidden_back_kernel,
        (owners // group,),
        [
            pl.BlockSpec((2, rows, hidden), lambda j: (0, at, 0)),
            pl.BlockSpec((group, owned, hidden), lambda j: (j, 0, 0)),
            pl.BlockSpec((group, owned, hidden), lambda j: (j, 1, 0)),
        ],
        pl.BlockSpec((rows, group * owned), lambda j: (0, j)),
        jax.ShapeDtypeStruct((rows, owners * owned), kind),
        flops=4 * rows * owners * owned * hidden,
        nbytes=4 * owners * owned * hidden + rows * (4 * hidden + 4 * owners * owned),
    )(grads, weights, weights)


def total_of(refs):
    return functools.reduce(jnp.add, [ref[...].astype(F32) for ref in refs])


def norm_back(grad, gain, values, scale):
    weighted = grad * gain
    inner = jnp.sum(weighted * values, axis=1, keepdims=True)
    back = scale * weighted - values * scale**3 * inner / D
    return back, jnp.sum(grad * values * scale, axis=0, keepdims=True)


def result_of(counts, owners, refs):
    begin, parts = 0, []
    for count in counts:
        parts.append(total_of(refs[begin : begin + count]))
        begin += count
    result = parts[0]
    if len(parts) > 1:
        width = result.shape[1] // owners
        result = jnp.concatenate(
            [part[:, i * width : (i + 1) * width] for i in range(owners) for part in parts], axis=1
        )
    scale = lax.rsqrt(jnp.mean(result * result, axis=1, keepdims=True) + NORM_EPS)
    return result, scale, refs[begin:]


def result_kernel(counts, owners, *refs):
    result, scale, refs = result_of(counts, owners, refs)
    grad_ref, gain_ref, back_ref, gain_grad_ref = refs
    back, gain_grad = norm_back(grad_ref[...].astype(F32), gain_ref[...], result, scale)
    back_ref[...] = back.astype(BF16)
    gain_grad_ref[0] = gain_grad


def output_kernel(counts, owners, *refs):
    result, scale, (hidden_ref, gain_ref, out_ref) = result_of(counts, owners, refs)
    out_ref[...] = (hidden_ref[...] + result * scale * gain_ref[...]).astype(BF16)


def result_step(parts, owners, other, gain, begin, rows, forward):
    depth = other.shape[1]
    block = min(rows, 64)
    at = begin // block
    flat = [array for part in parts for array in part]
    back_specs = [pl.BlockSpec((1, 1, depth), lambda i: (i, 0, 0))]
    back_shapes = [jax.ShapeDtypeStruct((rows // block, 1, depth), F32)]
    return call(
        functools.partial(
            output_kernel if forward else result_kernel, [len(part) for part in parts], owners
        ),
        (rows // block,),
        [pl.BlockSpec((block, array.shape[1]), lambda i: (i + at, 0)) for array in flat + [other]]
        + [pl.BlockSpec((1, depth), lambda i: (0, 0))],
        [pl.BlockSpec((block, depth), lambda i: (i, 0))] + ([] if forward else back_specs),
        [jax.ShapeDtypeStruct((rows, depth), BF16)] + ([] if forward else back_shapes),
        flops=rows * depth * 20,
        nbytes=rows * depth * 20,
    )(*flat, other, gain[None])


def branch_back_kernel(count, *refs):
    branch_ref, grad_ref, gain_ref, hidden_ref, back_ref, gain_grad_ref = refs[count:]
    grad = grad_ref[...].astype(F32) + total_of(refs[:count])
    hidden_ref[...] = grad
    branch = branch_ref[...]
    scale = lax.rsqrt(jnp.mean(branch * branch, axis=1, keepdims=True) + NORM_EPS)
    back, gain_grad = norm_back(grad, gain_ref[...], branch, scale)
    back_ref[...] = back.astype(BF16)
    gain_grad_ref[0] = gain_grad


def branch_back(parts, branch, grad_out, gain):
    rows, depth = branch.shape
    block = min(rows, 64)
    mine = pl.BlockSpec((block, depth), lambda i: (i, 0))
    return call(
        functools.partial(branch_back_kernel, len(parts)),
        (rows // block,),
        [mine] * (len(parts) + 2) + [pl.BlockSpec((1, depth), lambda i: (0, 0))],
        [mine, mine, pl.BlockSpec((1, 1, depth), lambda i: (i, 0, 0))],
        [
            jax.ShapeDtypeStruct((rows, depth), F32),
            jax.ShapeDtypeStruct((rows, depth), BF16),
            jax.ShapeDtypeStruct((rows // block, 1, depth), F32),
        ],
        flops=rows * depth * 20,
        nbytes=rows * depth * 20,
    )(*parts, branch, grad_out, gain[None])


def input_back_kernel(places_ref, x_ref, w_ref, residual_ref, out_ref):
    out_ref[...] = by_columns(x_ref[...], w_ref[...]).astype(out_ref.dtype)

    @pl.when(pl.program_id(1) == places_ref[0])
    def _():
        total = by_columns(x_ref[...], w_ref[...]) + residual_ref[...]
        out_ref[...] = total.astype(out_ref.dtype)


def input_back(grads, weights, residual, mine, distances, kind):
    rows, deep = grads.shape
    own = residual.shape[0]
    width = deep // 3
    blocks = rows // own
    places = jnp.stack([mine] + [mine ^ k for k in distances])
    return call(
        input_back_kernel,
        (len(distances), blocks),
        [
            pl.BlockSpec((own, deep), lambda a, i, p: (i, 0)),
            pl.BlockSpec((width, deep), lambda a, i, p: (p[1 + a], 0)),
            pl.BlockSpec((own, width), lambda a, i, p: (0, p[1 + a])),
        ],
        pl.BlockSpec((own, width), lambda a, i, p: (a * blocks + i, 0)),
        jax.ShapeDtypeStruct((len(distances) * rows, width), kind),
        flops=2 * rows * deep * width * len(distances),
        nbytes=rows * deep * 2 * (len(distances) + 1),
        scalars=1,
    )(places, grads, weights, residual)


def body(
    inputs,
    cotangent,
    doc_lengths,
    attn_weights,
    mlp_weights,
    norm_gains,
    attn_first,
    attn_second,
    mlp_first,
    mlp_second,
    gain_first,
    gain_second,
):
    owners = ("dp", "ctx")
    n = lax.axis_size("tensor")
    mine = lax.axis_index("tensor")
    rows, width = inputs.shape
    own = rows // n
    hidden = mlp_weights.shape[2]

    low = attn_weights.astype(BF16)
    attn_shard = jnp.concatenate([low[0], low[1], low[2], low[3]], axis=1)
    low = mlp_weights.astype(BF16)
    owned = low.shape[1]
    lead = owned // 2 if owned % 256 == 0 else 0
    up_shard = jnp.concatenate([low[0], low[1], low[2, :lead]], axis=0)
    attn_full = lax.all_gather(attn_shard, owners, axis=0, tiled=True)
    up_full = lax.all_gather(up_shard, owners, axis=0)
    down_full = lax.all_gather(low[2, lead:], owners, axis=0)
    down_pieces = [(down_full, 0, owned - lead, lead)]
    if lead:
        down_pieces = [(up_full, 2 * owned, lead, 0)] + down_pieces
    w_qkv, w_out = attn_full[:, : 3 * width], attn_full[:, 3 * width :]
    gains = lax.all_gather(
        norm_gains.astype(BF16), ("tensor",) + owners, axis=1, tiled=True
    ).astype(F32)
    gain_attn, gain_mlp = gains[2], gains[3]
    near = lax.dynamic_slice_in_dim(gains, mine * width, width, axis=1)
    gain_query, gain_key = near[0], near[1]

    gathered = jnp.zeros((rows, n * width), BF16)
    order = piece_order()
    for k, piece in zip(order, gather_pieces(inputs, True)):
        gathered = lax.dynamic_update_slice(gathered, piece, (0, (mine ^ k) * width))
    grad_out = jnp.zeros((own, n * width), BF16)
    for k in range(n):
        piece = lax.dynamic_slice_in_dim(cotangent, (mine ^ k) * own, own, axis=0)
        piece = swap(piece, k) if k else piece
        grad_out = lax.dynamic_update_slice(grad_out, piece, (0, (mine ^ k) * width))

    offset = lax.axis_index("ctx") * rows
    token_place = offset + jnp.arange(rows, dtype=jnp.int32)
    begins = doc_begins(doc_lengths[0], token_place)
    cosine, sine = turn_tables(token_place - begins)
    start = begins - offset

    qkv = matmul(after(gathered, grad_out), w_qkv)
    queries, key_proj = qkv[:, :width], qkv[:, width : 2 * width]
    squares = axis_total(
        jnp.stack([jnp.sum(queries * queries, axis=1), jnp.sum(key_proj * key_proj, axis=1)]),
        "tensor",
    )
    qk_rs = lax.rsqrt(squares / D + NORM_EPS).T
    query_low, key_low, value_low = rope(qkv, qk_rs, gain_query, gain_key, cosine, sine)
    all_keys = jnp.concatenate([passed_along(key_low, "ctx", 1), key_low], axis=0)
    all_values = jnp.concatenate([passed_along(value_low, "ctx", 1), value_low], axis=0)
    attn_low, log_total = attend(query_low, all_keys, all_values, start)

    parts = [
        by_columns(lax.dynamic_slice_in_dim(attn_low, (mine ^ k) * own, own, axis=0), w_out)
        for k in order
    ]
    branch = add_up(scatter_pieces(parts))
    branch_rs = lax.rsqrt(jnp.mean(branch * branch, axis=1, keepdims=True) + NORM_EPS)
    my_rows = lax.dynamic_slice_in_dim(gathered, mine * own, own, axis=0)
    hidden_in = my_rows.astype(F32) + branch * branch_rs * gain_attn
    hidden_low = jnp.concatenate(gather_pieces(hidden_in.astype(BF16), True), axis=0)
    gate_and_up, act_low = gate_up(hidden_low, up_full, owned)
    result = functools.partial(result_step, owners=down_full.shape[0], gain=gain_mlp)
    terms, done, near = [], (), []
    for array, place, count, _ in down_pieces:
        array = after(array, *done)
        piece = lambda x, begin, size, kind: down(x, array, place, count, begin, size, kind)
        if n != 4:
            parts = piece(act_low, 0, rows, F32)
            terms.append(scatter_pieces([parts[k * own : (k + 1) * own] for k in range(n)]))
            continue
        last = piece(act_low, own, own, BF16)
        passing = send_far(last)
        pair = piece(after(act_low, last, *near), 2 * own, 2 * own, F32)
        first = piece(after(act_low, pair), 0, own, F32)
        if len(terms) + 1 < len(down_pieces):
            sent, near = send_near(pair, passing)
            terms.append([first] + near)
            done = (first, sent)
    if n == 4:
        terms.append([first] + send_near(pair, passing)[1])
        half = own // 2
        steps = [
            result(terms, other=grad_out, begin=i * half, rows=half, forward=False) for i in range(2)
        ]
        halves = [gather_pieces(step[0]) for step in steps]
        result_blocks = [part[i] for group in ((0,), (1, 2), (3,), (4,)) for part in halves for i in group]
        gain_mlp_parts = steps[0][1] + steps[1][1]
    else:
        grad_result, gain_mlp_parts = result(
            terms, other=grad_out, begin=0, rows=own, forward=False
        )
        result_blocks = gather_pieces(grad_result)
    (output_low,) = result(terms, other=hidden_in, begin=0, rows=own, forward=True)
    grad_gain_mlp = jnp.sum(gain_mlp_parts, axis=(0, 1))
    grad_result_all = jnp.concatenate(result_blocks, axis=0)
    down_sums = contract_rows(grad_result_all, act_low).astype(BF16)
    owned_down = scatter_owned(down_sums, owners)
    grad_gate_up = act_back(
        [after(grad_result_all, down_sums)], down_pieces, gate_and_up
    )
    ctx = lax.axis_index("ctx")
    if n == 4:
        last = hidden_back(grad_gate_up, up_full, owned, own, own, BF16)
        passing = send_far(last)
        given = weight_half(hidden_low, after(grad_gate_up, last), 1 - ctx)
        pair = hidden_back(after(grad_gate_up, given), up_full, owned, 2 * own, 2 * own, F32)
        sent, near = send_near(pair, passing)
        first = hidden_back(after(grad_gate_up, sent), up_full, owned, 0, own, F32)
        terms = [first] + near
    else:
        first = hidden_back(grad_gate_up, up_full, owned, 0, rows, F32)
        given = weight_half(hidden_low, after(grad_gate_up, first), 1 - ctx)
        terms = scatter_pieces([first[k * own : (k + 1) * own] for k in range(n)])
    up_sums = weight_half(hidden_low, grad_gate_up, ctx, other_core(given))
    grad_hidden, grad_branch, gain_attn_parts = branch_back(
        terms, after(branch, up_sums), grad_out, gain_attn
    )
    grad_gain_attn = jnp.sum(gain_attn_parts, axis=(0, 1))
    owned_up = scatter_owned(merged(after(up_sums, owned_down)))
    grad_branch_all = jnp.zeros((rows, n * width), BF16)
    for k, piece in zip(order, gather_pieces(grad_branch, True)):
        grad_branch_all = lax.dynamic_update_slice(grad_branch_all, piece, ((mine ^ k) * own, 0))
    down_new = adam(owned_down, mlp_weights, mlp_first, mlp_second, 2, 1)
    grad_mixed = matmul(after(grad_branch_all, down_new[0], output_low), w_out).astype(BF16)
    dq, dkp, dvp, dk, dv = attend_back(
        query_low, all_keys, all_values, grad_mixed, log_total.T, start
    )
    back_key = passed_along(dkp, "ctx", -1)
    back_value = passed_along(dvp, "ctx", -1)
    given = other_core(weight_half(after(grad_branch_all, dkp), attn_low, 1 - ctx))
    output = jnp.zeros((rows, width), BF16)
    for k in range(n):
        piece = lax.dynamic_slice_in_dim(output_low, (mine ^ k) * width, width, axis=1)
        piece = swap(piece, k) if k else piece
        output = lax.dynamic_update_slice(output, piece, ((mine ^ k) * own, 0))

    weighted_q, weighted_k, grad_v, inner, gain_parts = unrope(
        dq, dk, dv, back_key, back_value, qkv, qk_rs, gain_query, gain_key, cosine, sine
    )
    out_sums = weight_half(after(grad_branch_all, inner), attn_low, ctx, given)
    inner = after(axis_total(inner.T, "tensor").T, out_sums)
    grad_q = qk_rs[:, :1] * weighted_q - queries * qk_rs[:, :1] ** 3 * inner[:, :1] / D
    grad_k = qk_rs[:, 1:] * weighted_k - key_proj * qk_rs[:, 1:] ** 3 * inner[:, 1:] / D
    grad_qkv = jnp.concatenate([grad_q.astype(BF16), grad_k.astype(BF16), grad_v], axis=1)
    given = weight_half(gathered, grad_qkv, 1 - ctx)
    near_inputs = lambda source, distances, kind: input_back(
        source, attn_full, grad_hidden, mine, distances, kind
    )
    if n == 4:
        last = near_inputs(after(grad_qkv, given), order[1:2], BF16)
        passing = send_far(last)
        attn_sums = weight_half(
            gathered, after(grad_qkv, last), ctx, other_core(given), out_sums
        )
        pair = near_inputs(after(grad_qkv, attn_sums), order[2:], F32)
        sent, near = send_near(pair, passing)
    else:
        attn_sums = weight_half(gathered, grad_qkv, ctx, other_core(given), out_sums)
        parts = near_inputs(grad_qkv, order, F32)
        sent = parts
    owned_attn = scatter_owned(merged(after(attn_sums, owned_up)))
    new_mlp, mlp_one, mlp_two = adam(
        after(owned_up, sent), mlp_weights, mlp_first, mlp_second, 0, 2, down_new
    )
    if n == 4:
        grad_inputs = add_up([near_inputs(after(grad_qkv, new_mlp), order[:1], F32)] + near)
    else:
        grad_inputs = add_up(scatter_pieces([parts[k * rows : (k + 1) * rows] for k in range(n)]))

    wide = jnp.stack([grad_gain_attn, grad_gain_mlp])
    near = lax.dynamic_slice_in_dim(wide, mine * width, width, axis=1)
    for k in range(1, n):
        near = near + swap(lax.dynamic_slice_in_dim(wide, (mine ^ k) * width, width, axis=1), k)
    gain_sums = jnp.concatenate([jnp.sum(gain_parts, axis=0), near])
    gain_sums = axis_total(axis_total(gain_sums, "ctx"), "dp")
    share = norm_gains.shape[1]
    place = (lax.axis_index("dp") * lax.axis_size("ctx") + lax.axis_index("ctx")) * share
    gain_grad = lax.dynamic_slice_in_dim(gain_sums, place, share, axis=1)

    new_attn, attn_one, attn_two = adam(owned_attn, attn_weights, attn_first, attn_second, 0, 4)
    new_gains, gain_one, gain_two = adam_step(
        norm_gains, gain_grad, gain_first, gain_second, GAIN_RATE, 0.0
    )
    return (
        output,
        grad_inputs,
        new_attn,
        attn_one,
        attn_two,
        new_mlp,
        mlp_one,
        mlp_two,
        new_gains,
        gain_one,
        gain_two,
    )


def solution(mesh):
    return jax.shard_map(
        body,
        mesh=mesh,
        in_specs=(
            P(("dp", "ctx"), "tensor"),
            P(("dp", "ctx"), "tensor"),
            P("dp", None),
            P(None, ("dp", "ctx"), "tensor"),
            P(None, ("dp", "ctx"), "tensor"),
            P(None, ("tensor", "dp", "ctx")),
            P(None, ("dp", "ctx"), "tensor"),
            P(None, ("dp", "ctx"), "tensor"),
            P(None, ("dp", "ctx"), "tensor"),
            P(None, ("dp", "ctx"), "tensor"),
            P(None, ("tensor", "dp", "ctx")),
            P(None, ("tensor", "dp", "ctx")),
        ),
        out_specs=(
            P(("dp", "ctx"), "tensor"),
            P(("dp", "ctx"), "tensor"),
            P(None, ("dp", "ctx"), "tensor"),
            P(None, ("dp", "ctx"), "tensor"),
            P(None, ("dp", "ctx"), "tensor"),
            P(None, ("dp", "ctx"), "tensor"),
            P(None, ("dp", "ctx"), "tensor"),
            P(None, ("dp", "ctx"), "tensor"),
            P(None, ("tensor", "dp", "ctx")),
            P(None, ("tensor", "dp", "ctx")),
            P(None, ("tensor", "dp", "ctx")),
        ),
        check_vma=False,
    )
```

```python
import functools

import jax
import jax.numpy as jnp
from jax import lax
from jax.experimental import pallas as pl
from jax.experimental.pallas import tpu as pltpu
from jax.sharding import PartitionSpec as P

D = 2048
HEAD_DIM = 128
STEP = 10


NORM_EPS = 1e-06
ROPE_THETA = 500000.0
BETA_ONE = 0.9
BETA_TWO = 0.95
ADAM_EPS = 1e-08
WEIGHT_DECAY = 0.1
LEARN_RATE = 0.02
GAIN_RATE = 1.0

SCORE_SCALE = HEAD_DIM ** (-0.5)
Q_BLOCK = 256
VMEM = 32
BF16 = jnp.bfloat16
F32 = jnp.float32


def passed_along(block, axis, distance):
    devices = range(lax.axis_size(axis))
    route = [(i - distance, i) for i in devices if i - distance in devices]
    return lax.ppermute(block, axis, route)


def swap(block, distance):
    return lax.ppermute(
        block, "tensor", [(i, i ^ distance) for i in range(lax.axis_size("tensor"))]
    )


def piece_order():
    n = lax.axis_size("tensor")
    return (0, 3, 1, 2) if n == 4 else tuple(range(n))


def gather_pieces(block, finely=False):
    n = lax.axis_size("tensor")
    if n != 4:
        return [block] + [swap(block, k) for k in range(1, n)]
    half = block.shape[0] // 2
    if not finely:
        one, two = swap(block, 1), swap(block, 2)
        return [block, swap(two[:half], 1), swap(one[half:], 2), one, two]
    upper, lower = block[:half], block[half:]
    two_upper, one_lower = swap(upper, 2), swap(lower, 1)
    one_upper, two_lower = swap(upper, 1), swap(lower, 2)
    far_upper, far_lower = swap(two_upper, 1), swap(one_lower, 2)
    return [
        jnp.concatenate(pair, axis=0)
        for pair in ((upper, lower), (far_upper, far_lower), (one_upper, one_lower), (two_upper, two_lower))
    ]


def send_far(last):
    upper, lower = last
    return jnp.concatenate([swap(lower, 2), swap(upper, 1)], axis=0)


def near_blocks(pair, passing):
    rows = pair.shape[0] // 2
    passing = jnp.pad(passing.astype(F32), ((rows // 2, rows // 2), (0, 0)))
    return (pair + passing).astype(BF16)


def send_near(pair, passing):
    rows = pair.shape[0] // 2
    pair = near_blocks(pair, passing)
    return pair, [swap(pair[:rows], 1), swap(pair[rows:], 2)]


def scatter_pieces(parts):
    if lax.axis_size("tensor") == 4:
        passing = send_far(jnp.split(parts[1].astype(BF16), 2, axis=0))
        return [parts[0]] + send_near(jnp.concatenate(parts[2:], axis=0), passing)[1]
    total = parts[0]
    for k in range(1, len(parts)):
        total = total + swap(parts[k].astype(BF16), k).astype(F32)
    return [total]


def add_up(terms):
    return functools.reduce(jnp.add, [term.astype(F32) for term in terms])


def axis_total(values, axis):
    n = lax.axis_size(axis)
    flat = values.reshape(-1, HEAD_DIM)
    others = [
        lax.ppermute(flat, axis, [(i, i ^ k if n in (2, 4, 8) else (i + k) % n) for i in range(n)])
        for k in range(1, n)
    ]
    return functools.reduce(jnp.add, others, flat).reshape(values.shape)


def doc_begins(doc_row, token_place):
    doc_ends = jnp.cumsum(doc_row)
    passed = token_place[:, None] >= doc_ends[None, :]
    return jnp.max(
        jnp.where(passed, doc_ends[None, :], jnp.zeros_like(doc_ends)[None, :]), axis=1
    )


def turn_tables(position):
    half_dim = HEAD_DIM // 2
    frequency = ROPE_THETA ** (-2.0 * jnp.arange(half_dim, dtype=F32) / HEAD_DIM)
    angles = position.astype(F32)[:, None] * frequency[None, :]
    cosine, sine = jnp.cos(angles), jnp.sin(angles)
    return jnp.concatenate([cosine, cosine], axis=1), jnp.concatenate([-sine, sine], axis=1)


def adam_step(weight, gradient, moment_one, moment_two, rate, decay):
    moment_one = BETA_ONE * moment_one + (1.0 - BETA_ONE) * gradient
    moment_two = BETA_TWO * moment_two + (1.0 - BETA_TWO) * gradient * gradient
    fix_one = 1.0 - BETA_ONE**STEP
    fix_two = 1.0 - BETA_TWO**STEP
    update = moment_one / fix_one / (jnp.sqrt(moment_two / fix_two) + ADAM_EPS)
    return (weight - rate * (update + decay * weight), moment_one, moment_two)


def adam_kernel(grad_ref, weight_ref, first_ref, second_ref, *rest):
    wide = weight_ref.shape[2]
    for i in range(weight_ref.shape[0]):
        grad = grad_ref[:, i * wide : (i + 1) * wide].astype(F32)
        new = adam_step(
            weight_ref[i], grad, first_ref[i], second_ref[i], LEARN_RATE, WEIGHT_DECAY
        )
        for ref, value in zip(rest[-3:], new):
            ref[i] = value


def adam(grad, weights, first, second, begin, count, earlier=()):
    _, rows, wide = weights.shape
    block = min(wide, 1024)
    group = max(1, min(count, 1024 // block))
    steps, at = wide // block, begin // group
    spec = pl.BlockSpec((group, rows, block), lambda k, j: (at + k, 0, j))
    return pl.pallas_call(
        adam_kernel,
        grid=(count // group, steps),
        in_specs=[
            pl.BlockSpec((rows, group * block), lambda k, j: (0, k * steps + j)), spec, spec, spec
        ]
        + [pl.BlockSpec(memory_space=pl.ANY)] * len(earlier),
        out_specs=[spec] * 3,
        out_shape=[jax.ShapeDtypeStruct(weights.shape, F32)] * 3,
        input_output_aliases={4 + i: i for i in range(len(earlier))},
        compiler_params=pltpu.CompilerParams(vmem_limit_bytes=60 * 1024 * 1024),
        cost_estimate=pl.CostEstimate(
            flops=0, bytes_accessed=count * rows * wide * 26, transcendentals=0
        ),
    )(grad, weights, first, second, *earlier)


def matmul(left, right):
    return jnp.dot(left, right, preferred_element_type=F32)


def contract_rows(left, right):
    return lax.dot_general(left, right, (((0,), (0,)), ((), ())), preferred_element_type=F32)


def by_columns(left, right):
    return lax.dot_general(left, right, (((1,), (1,)), ((), ())), preferred_element_type=F32)


def along_line(block, *hops):
    return lax.ppermute(block, "dp", list(hops))


def line_gather(block):
    place = lax.axis_index("dp")
    below = along_line(block, (0, 1), (1, 2), (2, 3))
    above = along_line(block, (1, 0), (2, 1), (3, 2))
    across = along_line(block, (0, 2), (1, 3), (2, 0), (3, 1))
    ends = along_line(across, (2, 3), (1, 0))
    found = [block, jnp.where(place == 3, ends, above), across, jnp.where(place == 0, ends, below)]
    whole = jnp.zeros((4,) + block.shape, block.dtype)
    for i, value in enumerate(found):
        at = (place + i) % 4
        whole = lax.dynamic_update_slice(whole, value[None], (at,) + (0,) * block.ndim)
    return whole


def line_scatter(blocks):
    place = lax.axis_index("dp")
    pick = lambda i: lax.dynamic_index_in_dim(blocks, i % 4, axis=0, keepdims=False)
    far = along_line(pick(jnp.where(place == 0, 3, 0)), (0, 1), (3, 2))
    above = along_line(pick(place + 1), (0, 1), (1, 2), (2, 3))
    below = along_line(pick(place + 3), (1, 0), (2, 1), (3, 2))
    across = (pick(place + 2).astype(F32) + far.astype(F32)).astype(BF16)
    across = along_line(across, (0, 2), (1, 3), (2, 0), (3, 1))
    return add_up([pick(place), above, below, across]).astype(BF16)


def after(value, *earlier):
    return lax.optimization_barrier((value,) + earlier)[0]


def other_core(values):
    return lax.ppermute(values, "ctx", [(0, 1), (1, 0)])


def scatter_owned(sums, axes=("dp",)):
    return lax.psum_scatter(sums, axes, scatter_dimension=0, tiled=True)


def call(
    kernel, grid, in_specs, out_specs, out_shape, scratch=(), flops=0, nbytes=0, trans=0, scalars=0,
    announced=0.25, vmem=VMEM,
):
    return pl.pallas_call(
        kernel,
        grid_spec=pltpu.PrefetchScalarGridSpec(
            num_scalar_prefetch=scalars,
            grid=grid,
            in_specs=in_specs,
            out_specs=out_specs,
            scratch_shapes=list(scratch),
        ),
        out_shape=out_shape,
        compiler_params=pltpu.CompilerParams(vmem_limit_bytes=vmem * 1024 * 1024),
        cost_estimate=pl.CostEstimate(
            flops=int(flops * announced),
            bytes_accessed=int(nbytes * announced),
            transcendentals=int(trans * announced),
        ),
    )


def weight_half_kernel(blocks, steps, ctx_ref, *refs):
    left, right_ref, (out_ref, turned) = refs[:blocks], refs[blocks], refs[-2:]
    given_ref = refs[blocks + 1] if len(refs) > blocks + 3 else None
    tail_ref = refs[blocks + 2] if len(refs) > blocks + 4 else None

    @pl.when(pl.program_id(0) == 0)
    def _():
        for i, ref in enumerate(left):
            turned[i] = ref[...].T

    @pl.when(pl.program_id(0) < steps)
    def _():
        right = right_ref[...]
        for i in range(blocks):
            total = matmul(turned[i], right)
            if given_ref is not None:
                total = total + given_ref[i].astype(F32)
            out_ref[i] = total.astype(BF16)

    if tail_ref is not None:

        @pl.when(pl.program_id(0) >= steps)
        def _():
            out_ref[...] = tail_ref[...]


def weight_half(left, right, ctx, given=None, tail=None):
    rows, depth = left.shape
    blocks = lax.axis_size("dp")
    owned = depth // (blocks * lax.axis_size("ctx"))
    n_ctx = lax.axis_size("ctx")
    wide = right.shape[-1]
    block = next(size for size in (512, 256, 128) if wide % size == 0)
    each = wide // block
    steps = each * (right.shape[0] if right.ndim == 3 else 1)
    last = steps - 1
    if right.ndim == 3:
        right_spec = pl.BlockSpec((None, rows, block), lambda j, c: (j // each, 0, j % each))
    else:
        right_spec = pl.BlockSpec((rows, block), lambda j, c: (0, jnp.minimum(j, last)))
    specs = [
        pl.BlockSpec((rows, owned), lambda j, c, i=i: (0, n_ctx * i + c[0])) for i in range(blocks)
    ]
    operands = [left] * blocks + [right]
    specs.append(right_spec)
    columns = steps * block
    more = 0
    if given is not None:
        operands.append(given)
        specs.append(
            pl.BlockSpec((blocks, owned, block), lambda j, c: (0, 0, jnp.minimum(j, last)))
        )
    if tail is not None:
        operands.append(tail)
        more = tail.shape[2] // block
        specs.append(
            pl.BlockSpec((blocks, owned, block), lambda j, c: (0, 0, jnp.maximum(j - steps, 0)))
        )
    return call(
        functools.partial(weight_half_kernel, blocks, steps),
        (steps + more,),
        specs,
        pl.BlockSpec((blocks, owned, block), lambda j, c: (0, 0, j)),
        jax.ShapeDtypeStruct((blocks, owned, columns + more * block), BF16),
        [pltpu.VMEM((blocks, owned, rows), BF16)],
        flops=2 * rows * blocks * owned * columns,
        nbytes=2 * (rows * blocks * owned + rows * columns + 2 * blocks * owned * columns),
        scalars=1,
    )(ctx[None], *operands)


def rope_kernel(q_ref, k_ref, v_ref, rs_ref, gq_ref, gk_ref, cos_ref, sin_ref, qo, ko, vo):
    cosine, sine = cos_ref[...], sin_ref[...]
    for place, (src, gain, dst) in enumerate(((q_ref, gq_ref, qo), (k_ref, gk_ref, ko))):
        scale = rs_ref[:, place : place + 1]
        for head in range(src.shape[1] // HEAD_DIM):
            cols = slice(head * HEAD_DIM, (head + 1) * HEAD_DIM)
            x = src[:, cols] * scale * gain[:, cols]
            dst[:, cols] = (x * cosine + pltpu.roll(x, HEAD_DIM // 2, 1) * sine).astype(BF16)
    vo[...] = v_ref[...].astype(BF16)


def rope(qkv, rs, gain_query, gain_key, cosine, sine):
    rows, width = qkv.shape[0], qkv.shape[1] // 3
    block = min(rows, 256)
    part = lambda j: pl.BlockSpec((block, width), lambda i, j=j: (i, j))
    gain = pl.BlockSpec((1, width), lambda i: (0, 0))
    table = pl.BlockSpec((block, HEAD_DIM), lambda i: (i, 0))
    out = jax.ShapeDtypeStruct((rows, width), BF16)
    return call(
        rope_kernel,
        (rows // block,),
        [part(0), part(1), part(2), pl.BlockSpec((block, 2), lambda i: (i, 0)), gain, gain]
        + [table, table],
        [part(0)] * 3,
        [out] * 3,
        flops=rows * width * 12,
        nbytes=rows * width * 18,
    )(qkv, qkv, qkv, rs, gain_query[None], gain_key[None], cosine, sine)


def attend_kernel(span, q_ref, k_ref, v_ref, start_ref, o_ref, lse_ref):
    rows = q_ref.shape[0]
    step = pl.program_id(0)
    first = pl.multiple_of(step * rows, rows)
    shape = (rows, span)
    row = lax.broadcasted_iota(jnp.int32, shape, 0)
    column = lax.broadcasted_iota(jnp.int32, shape, 1) - (span - rows)
    allowed = (column <= row) & (column >= start_ref[...] - step * rows)
    for head in range(q_ref.shape[1] // HEAD_DIM):
        cols = slice(head * HEAD_DIM, (head + 1) * HEAD_DIM)
        keys = k_ref[pl.ds(first, span), cols]
        values = v_ref[pl.ds(first, span), cols]
        scores = by_columns(q_ref[:, cols], keys) * SCORE_SCALE
        scores = jnp.where(allowed, scores, -1e30)
        top = jnp.max(scores, axis=1, keepdims=True)
        weights = jnp.exp(scores - top)
        total = jnp.sum(weights, axis=1, keepdims=True)
        low = (weights / total).astype(BF16)
        o_ref[:, cols] = matmul(low, values).astype(BF16)
        lse_ref[:, head : head + 1] = top + jnp.log(total)


def attend(query, keys, values, start):
    rows, width = query.shape
    heads = width // HEAD_DIM
    block = Q_BLOCK
    span = rows + block
    whole = pl.BlockSpec(keys.shape, lambda i: (0, 0))
    return call(
        functools.partial(attend_kernel, span),
        (rows // block,),
        [pl.BlockSpec((block, width), lambda i: (i, 0)), whole, whole]
        + [pl.BlockSpec((block, 1), lambda i: (i, 0))],
        [pl.BlockSpec((block, width), lambda i: (i, 0)), pl.BlockSpec((block, heads), lambda i: (i, 0))],
        [jax.ShapeDtypeStruct((rows, width), BF16), jax.ShapeDtypeStruct((rows, heads), F32)],
        flops=4 * rows * span * width,
        nbytes=rows * width * 12,
        trans=rows * span * heads,
    )(query, keys, values, start[:, None])


def attend_back_kernel(
    span, q_ref, k_ref, v_ref, do_ref, lse_ref, start_ref, dq_ref, dkp_ref, dvp_ref, dk_ref, dv_ref, ka, va
):
    rows = q_ref.shape[0]
    step = pl.program_id(0)
    first = pl.multiple_of(step * rows, rows)

    @pl.when(step == 0)
    def _():
        ka[...] = jnp.zeros_like(ka)
        va[...] = jnp.zeros_like(va)

    shape = (span, rows)
    column = lax.broadcasted_iota(jnp.int32, shape, 0) - (span - rows)
    row = lax.broadcasted_iota(jnp.int32, shape, 1)
    allowed = (column <= row) & (column >= start_ref[...] - step * rows)
    for head in range(q_ref.shape[1] // HEAD_DIM):
        cols = slice(head * HEAD_DIM, (head + 1) * HEAD_DIM)
        query, grad = q_ref[:, cols], do_ref[:, cols]
        keys = k_ref[pl.ds(first, span), cols]
        values = v_ref[pl.ds(first, span), cols]
        scores = by_columns(keys, query) * SCORE_SCALE
        weights = jnp.where(allowed, jnp.exp(scores - lse_ref[head : head + 1, :]), 0.0)
        grad_weights = by_columns(values, grad)
        mean = jnp.sum(weights * grad_weights, axis=0, keepdims=True)
        grad_scores = (weights * (grad_weights - mean)).astype(BF16)
        dq_ref[:, cols] = contract_rows(grad_scores, keys) * SCORE_SCALE
        va[pl.ds(first, span), cols] += matmul(weights.astype(BF16), grad)
        ka[pl.ds(first, span), cols] += matmul(grad_scores, query) * SCORE_SCALE

    @pl.when(step == pl.num_programs(0) - 1)
    def _():
        total = dk_ref.shape[0]
        dkp_ref[...] = ka[:total, :].astype(BF16)
        dvp_ref[...] = va[:total, :].astype(BF16)
        dk_ref[...] = ka[total:, :]
        dv_ref[...] = va[total:, :]


def attend_back(query, keys, values, grad, lse, start):
    rows, width = query.shape
    heads = width // HEAD_DIM
    block = Q_BLOCK
    span = rows + block
    whole = pl.BlockSpec(keys.shape, lambda i: (0, 0))
    mine = pl.BlockSpec((block, width), lambda i: (i, 0))
    full = pl.BlockSpec((rows, width), lambda i: (0, 0))
    return call(
        functools.partial(attend_back_kernel, span),
        (rows // block,),
        [mine, whole, whole, mine]
        + [pl.BlockSpec((heads, block), lambda i: (0, i)), pl.BlockSpec((1, block), lambda i: (0, i))],
        [mine, full, full, full, full],
        [jax.ShapeDtypeStruct((rows, width), t) for t in (F32, BF16, BF16, F32, F32)],
        [pltpu.VMEM(keys.shape, F32)] * 2,
        flops=10 * rows * span * width,
        nbytes=rows * width * 28,
        trans=rows * span * heads,
        announced=12,
    )(query, keys, values, grad, lse, start[None, :])


def unrope_kernel(
    dq_ref, dk_ref, dv_ref, bk_ref, bv_ref, q_ref, k_ref, rs_ref, gq_ref, gk_ref, cos_ref, sin_ref,
    wq_ref, wk_ref, dvo_ref, inner_ref, gain_ref,
):
    cosine, sine = cos_ref[...], -sin_ref[...]
    for place, (src, back, x_ref, gain, dst) in enumerate(
        ((dq_ref, None, q_ref, gq_ref, wq_ref), (dk_ref, bk_ref, k_ref, gk_ref, wk_ref))
    ):
        scale = rs_ref[:, place : place + 1]
        inner = 0.0
        for head in range(src.shape[1] // HEAD_DIM):
            cols = slice(head * HEAD_DIM, (head + 1) * HEAD_DIM)
            grad = src[:, cols]
            if back is not None:
                grad = grad + back[:, cols].astype(F32)
            grad = grad * cosine + pltpu.roll(grad, HEAD_DIM // 2, 1) * sine
            x = x_ref[:, cols]
            weighted = grad * gain[:, cols]
            dst[:, cols] = weighted
            inner = inner + jnp.sum(weighted * x, axis=1, keepdims=True)
            gain_ref[0, place : place + 1, cols] = jnp.sum(grad * x * scale, axis=0, keepdims=True)
        inner_ref[:, place : place + 1] = inner
    dvo_ref[...] = (dv_ref[...] + bv_ref[...].astype(F32)).astype(BF16)


def unrope(dq, dk, dv, back_k, back_v, qkv, rs, gain_query, gain_key, cosine, sine):
    rows, width = dq.shape
    block = min(rows, 256)
    part = lambda j: pl.BlockSpec((block, width), lambda i, j=j: (i, j))
    gain = pl.BlockSpec((1, width), lambda i: (0, 0))
    table = pl.BlockSpec((block, HEAD_DIM), lambda i: (i, 0))
    pair = pl.BlockSpec((block, 2), lambda i: (i, 0))
    return call(
        unrope_kernel,
        (rows // block,),
        [part(0)] * 5 + [part(0), part(1), pair, gain, gain, table, table],
        [part(0)] * 3 + [pair, pl.BlockSpec((1, 2, width), lambda i: (i, 0, 0))],
        [jax.ShapeDtypeStruct((rows, width), t) for t in (F32, F32, BF16)]
        + [jax.ShapeDtypeStruct((rows, 2), F32)]
        + [jax.ShapeDtypeStruct((rows // block, 2, width), F32)],
        flops=rows * width * 30,
        nbytes=rows * width * 34,
    )(dq, dk, dv, back_k, back_v, qkv, qkv, rs, gain_query[None], gain_key[None], cosine, sine)


def merged(block):
    return block.reshape(-1, block.shape[-1])


def gate_up_kernel(x_ref, wg_ref, wu_ref, gu_ref, act_ref):
    x = x_ref[...]
    gate, up = matmul(x, merged(wg_ref[...])), matmul(x, merged(wu_ref[...]))
    gu_ref[0], gu_ref[1] = gate, up
    act_ref[...] = (gate * jax.nn.sigmoid(gate) * up).astype(BF16)


def gate_up(x, weights, owned):
    rows, depth = x.shape
    owners, hidden = weights.shape[0], weights.shape[2]
    block = min(hidden, 256)
    return call(
        gate_up_kernel,
        (hidden // block,),
        [
            pl.BlockSpec((rows, depth), lambda j: (0, 0)),
            pl.BlockSpec((owners, owned, block), lambda j: (0, 0, j)),
            pl.BlockSpec((owners, owned, block), lambda j: (0, 1, j)),
        ],
        [
            pl.BlockSpec((2, rows, block), lambda j: (0, 0, j)),
            pl.BlockSpec((rows, block), lambda j: (0, j)),
        ],
        [
            jax.ShapeDtypeStruct((2, rows, hidden), F32),
            jax.ShapeDtypeStruct((rows, hidden), BF16),
        ],
        flops=4 * rows * depth * hidden,
        nbytes=4 * depth * hidden + rows * (10 * hidden + 2 * depth),
        trans=rows * hidden,
    )(x, weights, weights)


def store_rows(total, outs):
    rows = total.shape[0] // len(outs)
    for i, ref in enumerate(outs):
        ref[...] = total[i * rows : (i + 1) * rows].astype(ref.dtype)


def row_outputs(rows, columns, block, kind, parts):
    return (
        [pl.BlockSpec((rows // parts, block), lambda j: (0, j))] * parts,
        [jax.ShapeDtypeStruct((rows // parts, columns), kind)] * parts,
    )


def down_kernel(x_ref, w_ref, *outs):
    store_rows(by_columns(x_ref[...], merged(w_ref[...])), outs)


def down(x, weights, place, count, begin, rows, kind, parts=1):
    owners, hidden = weights.shape[0], weights.shape[2]
    group = max(1, min(owners, 512 // count))
    at, row = begin // rows, place // count
    outs = call(
        down_kernel,
        (owners // group,),
        [
            pl.BlockSpec((rows, hidden), lambda j: (at, 0)),
            pl.BlockSpec((group, count, hidden), lambda j: (j, row, 0)),
        ],
        *row_outputs(rows, owners * count, group * count, kind, parts),
        flops=2 * rows * owners * count * hidden,
        nbytes=2 * owners * count * hidden + rows * (2 * hidden + 4 * owners * count),
    )(x, weights)
    return outs if parts > 1 else outs[0]


def act_back_kernel(cuts, count_x, *refs):
    blocks, weights = refs[:count_x], refs[count_x : count_x + len(cuts)]
    gu_ref, out_ref, split = refs[count_x + len(cuts) :]
    owners = weights[0].shape[0]
    owned = split.shape[1] // owners

    @pl.when(pl.program_id(0) == 0)
    def _():
        row = 0
        for x_ref in blocks:
            rows, to = slice(row, row + x_ref.shape[0]), 0
            row += x_ref.shape[0]
            for begin, count in cuts:
                for i in range(owners):
                    at = i * owned + begin
                    split[rows, to : to + count] = x_ref[:, at : at + count]
                    to += count

    grad, at = 0.0, 0
    for (_, count), ref in zip(cuts, weights):
        grad = grad + matmul(split[:, at : at + owners * count], merged(ref[...]))
        at += owners * count
    gate, up = gu_ref[0], gu_ref[1]
    sig = jax.nn.sigmoid(gate)
    out_ref[0] = (grad * up * sig * (1.0 + gate * (1.0 - sig))).astype(BF16)
    out_ref[1] = (grad * gate * sig).astype(BF16)


def act_back(blocks, pieces, gate_and_up):
    _, rows, hidden = gate_and_up.shape
    depth = blocks[0].shape[1]
    block = min(hidden, 512)
    pair = pl.BlockSpec((2, rows, block), lambda j: (0, 0, j))
    return call(
        functools.partial(
            act_back_kernel, [(first, count) for _, _, count, first in pieces], len(blocks)
        ),
        (hidden // block,),
        [pl.BlockSpec(array.shape, lambda j: (0, 0)) for array in blocks]
        + [
            pl.BlockSpec((array.shape[0], count, block), lambda j, at=place // count: (0, at, j))
            for array, place, count, _ in pieces
        ]
        + [pair],
        pair,
        jax.ShapeDtypeStruct((2, rows, hidden), BF16),
        [pltpu.VMEM((rows, depth), BF16)],
        vmem=56,
        flops=2 * rows * depth * hidden,
        nbytes=2 * depth * hidden + rows * (12 * hidden + 2 * depth),
        trans=rows * hidden,
    )(*blocks, *[array for array, _, _, _ in pieces], gate_and_up)


def hidden_back_kernel(x_ref, wg_ref, wu_ref, *outs):
    total = by_columns(x_ref[0], merged(wg_ref[...])) + by_columns(x_ref[1], merged(wu_ref[...]))
    store_rows(total, outs)


def hidden_back(grads, weights, owned, begin, rows, kind, parts=1):
    hidden, owners = grads.shape[2], weights.shape[0]
    group = max(1, (512 if rows <= 512 else 256) // owned)
    at = begin // rows
    outs = call(
        hidden_back_kernel,
        (owners // group,),
        [
            pl.BlockSpec((2, rows, hidden), lambda j: (0, at, 0)),
            pl.BlockSpec((group, owned, hidden), lambda j: (j, 0, 0)),
            pl.BlockSpec((group, owned, hidden), lambda j: (j, 1, 0)),
        ],
        *row_outputs(rows, owners * owned, group * owned, kind, parts),
        flops=4 * rows * owners * owned * hidden,
        nbytes=4 * owners * owned * hidden + rows * (4 * hidden + 4 * owners * owned),
    )(grads, weights, weights)
    return outs if parts > 1 else outs[0]


def total_of(refs):
    return functools.reduce(jnp.add, [ref[...].astype(F32) for ref in refs])


def norm_back(grad, gain, values, scale):
    weighted = grad * gain
    inner = jnp.sum(weighted * values, axis=1, keepdims=True)
    back = scale * weighted - values * scale**3 * inner / D
    return back, jnp.sum(grad * values * scale, axis=0, keepdims=True)


def result_of(counts, owners, refs):
    begin, parts = 0, []
    for count in counts:
        parts.append(total_of(refs[begin : begin + count]))
        begin += count
    result = parts[0]
    if len(parts) > 1:
        width = result.shape[1] // owners
        result = jnp.concatenate(
            [part[:, i * width : (i + 1) * width] for i in range(owners) for part in parts], axis=1
        )
    scale = lax.rsqrt(jnp.mean(result * result, axis=1, keepdims=True) + NORM_EPS)
    return result, scale, refs[begin:]


def result_kernel(counts, owners, *refs):
    result, scale, refs = result_of(counts, owners, refs)
    grad_ref, gain_ref, back_ref, gain_grad_ref = refs
    back, gain_grad = norm_back(grad_ref[...].astype(F32), gain_ref[...], result, scale)
    back_ref[...] = back.astype(BF16)
    gain_grad_ref[0] = gain_grad


def output_kernel(counts, owners, *refs):
    result, scale, (hidden_ref, gain_ref, out_ref) = result_of(counts, owners, refs)
    out_ref[...] = (hidden_ref[...] + result * scale * gain_ref[...]).astype(BF16)


def result_step(parts, owners, other, gain, begin, rows, forward):
    depth = other.shape[1]
    block = min(rows, 64)
    at = begin // block
    flat = [array for part in parts for array in part]
    back_specs = [pl.BlockSpec((1, 1, depth), lambda i: (i, 0, 0))]
    back_shapes = [jax.ShapeDtypeStruct((rows // block, 1, depth), F32)]
    return call(
        functools.partial(
            output_kernel if forward else result_kernel, [len(part) for part in parts], owners
        ),
        (rows // block,),
        [pl.BlockSpec((block, array.shape[1]), lambda i: (i + at, 0)) for array in flat + [other]]
        + [pl.BlockSpec((1, depth), lambda i: (0, 0))],
        [pl.BlockSpec((block, depth), lambda i: (i, 0))] + ([] if forward else back_specs),
        [jax.ShapeDtypeStruct((rows, depth), BF16)] + ([] if forward else back_shapes),
        flops=rows * depth * 20,
        nbytes=rows * depth * 20,
    )(*flat, other, gain[None])


def branch_back_kernel(count, *refs):
    branch_ref, grad_ref, gain_ref, hidden_ref, back_ref, gain_grad_ref = refs[count:]
    grad = grad_ref[...].astype(F32) + total_of(refs[:count])
    hidden_ref[...] = grad
    branch = branch_ref[...]
    scale = lax.rsqrt(jnp.mean(branch * branch, axis=1, keepdims=True) + NORM_EPS)
    back, gain_grad = norm_back(grad, gain_ref[...], branch, scale)
    back_ref[...] = back.astype(BF16)
    gain_grad_ref[0] = gain_grad


def branch_back(parts, branch, grad_out, gain):
    rows, depth = branch.shape
    block = min(rows, 64)
    mine = pl.BlockSpec((block, depth), lambda i: (i, 0))
    return call(
        functools.partial(branch_back_kernel, len(parts)),
        (rows // block,),
        [mine] * (len(parts) + 2) + [pl.BlockSpec((1, depth), lambda i: (0, 0))],
        [mine, mine, pl.BlockSpec((1, 1, depth), lambda i: (i, 0, 0))],
        [
            jax.ShapeDtypeStruct((rows, depth), F32),
            jax.ShapeDtypeStruct((rows, depth), BF16),
            jax.ShapeDtypeStruct((rows // block, 1, depth), F32),
        ],
        flops=rows * depth * 20,
        nbytes=rows * depth * 20,
    )(*parts, branch, grad_out, gain[None])


def input_back_kernel(places_ref, x_ref, w_ref, residual_ref, *outs):
    step, half = pl.program_id(1), pl.num_programs(1) // 2
    own = jnp.where(step == places_ref[0], residual_ref[...], 0.0)
    total = by_columns(x_ref[...], w_ref[...]) + own
    if len(outs) == 1:
        outs[0][...] = total.astype(outs[0].dtype)
        return

    @pl.when(step < half)
    def _():
        outs[0][...] = total.astype(outs[0].dtype)

    @pl.when(step >= half)
    def _():
        outs[1][...] = total.astype(outs[1].dtype)


def input_back(grads, weights, residual, mine, distances, kind, parts=1):
    rows, deep = grads.shape
    own = residual.shape[0]
    width = deep // 3
    blocks = rows // own
    half = blocks // 2
    places = jnp.stack([mine] + [mine ^ k for k in distances])
    specs = [pl.BlockSpec((own, width), lambda a, i, p: (a * blocks + i, 0))]
    if parts == 2:
        specs = [
            pl.BlockSpec((own, width), lambda a, i, p: (jnp.minimum(i, half - 1), 0)),
            pl.BlockSpec((own, width), lambda a, i, p: (jnp.maximum(i - half, 0), 0)),
        ]
    outs = call(
        input_back_kernel,
        (len(distances), blocks),
        [
            pl.BlockSpec((own, deep), lambda a, i, p: (i, 0)),
            pl.BlockSpec((width, deep), lambda a, i, p: (p[1 + a], 0)),
            pl.BlockSpec((own, width), lambda a, i, p: (0, p[1 + a])),
        ],
        specs,
        [jax.ShapeDtypeStruct((len(distances) * rows // parts, width), kind)] * parts,
        flops=2 * rows * deep * width * len(distances),
        nbytes=rows * deep * 2 * (len(distances) + 1),
        scalars=1,
    )(places, grads, weights, residual)
    return outs if parts > 1 else outs[0]


def body(
    inputs,
    cotangent,
    doc_lengths,
    attn_weights,
    mlp_weights,
    norm_gains,
    attn_first,
    attn_second,
    mlp_first,
    mlp_second,
    gain_first,
    gain_second,
):
    owners = ("dp", "ctx")
    n = lax.axis_size("tensor")
    mine = lax.axis_index("tensor")
    rows, width = inputs.shape
    own = rows // n
    hidden = mlp_weights.shape[2]

    low = attn_weights.astype(BF16)
    line = lax.axis_size("dp") == 4
    attn_shard = jnp.concatenate([low[0], low[1], low[2]] + ([] if line else [low[3]]), axis=1)
    out_shard = low[3]
    low = mlp_weights.astype(BF16)
    owned = low.shape[1]
    lead = owned // 2 if owned % 256 == 0 else 0
    up_shard = jnp.concatenate([low[0], low[1], low[2, :lead]], axis=0)
    attn_full = lax.all_gather(attn_shard, owners, axis=0, tiled=True)
    up_full = lax.all_gather(up_shard, owners, axis=0)
    down_full = lax.all_gather(low[2, lead:], owners, axis=0)
    down_pieces = [(down_full, 0, owned - lead, lead)]
    if lead:
        down_pieces = [(up_full, 2 * owned, lead, 0)] + down_pieces
    if line:
        w_qkv, place = attn_full, lax.axis_index("ctx")
        kept = line_gather(out_shard)
        w_out = jnp.zeros((4, 2) + out_shard.shape, BF16)
        for at, value in ((place, kept), (1 - place, other_core(kept))):
            w_out = lax.dynamic_update_slice(w_out, value[:, None], (0, at, 0, 0))
        w_out = w_out.reshape(-1, width)
    else:
        w_qkv, w_out = attn_full[:, : 3 * width], attn_full[:, 3 * width :]
    gains = lax.all_gather(
        norm_gains.astype(BF16), ("tensor",) + owners, axis=1, tiled=True
    ).astype(F32)
    gain_attn, gain_mlp = gains[2], gains[3]
    near = lax.dynamic_slice_in_dim(gains, mine * width, width, axis=1)
    gain_query, gain_key = near[0], near[1]

    gathered = jnp.zeros((rows, n * width), BF16)
    order = piece_order()
    for k, piece in zip(order, gather_pieces(inputs, True)):
        gathered = lax.dynamic_update_slice(gathered, piece, (0, (mine ^ k) * width))
    grad_out = jnp.zeros((own, n * width), BF16)
    for k in range(n):
        piece = lax.dynamic_slice_in_dim(cotangent, (mine ^ k) * own, own, axis=0)
        piece = swap(piece, k) if k else piece
        grad_out = lax.dynamic_update_slice(grad_out, piece, (0, (mine ^ k) * width))

    offset = lax.axis_index("ctx") * rows
    token_place = offset + jnp.arange(rows, dtype=jnp.int32)
    begins = doc_begins(doc_lengths[0], token_place)
    cosine, sine = turn_tables(token_place - begins)
    start = begins - offset

    qkv = matmul(gathered, w_qkv)
    queries, key_proj = qkv[:, :width], qkv[:, width : 2 * width]
    squares = axis_total(
        jnp.stack([jnp.sum(queries * queries, axis=1), jnp.sum(key_proj * key_proj, axis=1)]),
        "tensor",
    )
    qk_rs = lax.rsqrt(squares / D + NORM_EPS).T
    qk_rs = after(qk_rs, grad_out)
    query_low, key_low, value_low = rope(qkv, qk_rs, gain_query, gain_key, cosine, sine)
    all_keys = jnp.concatenate([passed_along(key_low, "ctx", 1), key_low], axis=0)
    all_values = jnp.concatenate([passed_along(value_low, "ctx", 1), value_low], axis=0)
    attn_low, log_total = attend(query_low, all_keys, all_values, start)

    parts = [
        by_columns(lax.dynamic_slice_in_dim(attn_low, (mine ^ k) * own, own, axis=0), w_out)
        for k in order
    ]
    branch = add_up(scatter_pieces(parts))
    branch_rs = lax.rsqrt(jnp.mean(branch * branch, axis=1, keepdims=True) + NORM_EPS)
    my_rows = lax.dynamic_slice_in_dim(gathered, mine * own, own, axis=0)
    hidden_in = my_rows.astype(F32) + branch * branch_rs * gain_attn
    hidden_low = jnp.concatenate(gather_pieces(hidden_in.astype(BF16), True), axis=0)
    gate_and_up, act_low = gate_up(hidden_low, up_full, owned)
    result = functools.partial(result_step, owners=down_full.shape[0], gain=gain_mlp)
    terms, done, near = [], (), []
    for array, place, count, _ in down_pieces:
        array = after(array, *done)
        piece = lambda x, *rest, array=array: down(x, array, place, count, *rest)
        if n != 4:
            parts = piece(act_low, 0, rows, F32)
            terms.append(scatter_pieces([parts[k * own : (k + 1) * own] for k in range(n)]))
            continue
        last = piece(act_low, own, own, BF16, 2)
        passing = send_far(last)
        pair = piece(after(act_low, *last, *near), 2 * own, 2 * own, F32)
        first = piece(after(act_low, pair), 0, own, F32)
        if len(terms) + 1 < len(down_pieces):
            sent, near = send_near(pair, passing)
            terms.append([first] + near)
            done = (first, sent)
    if n == 4:
        terms.append([first] + send_near(pair, passing)[1])
        half = own // 2
        steps = [
            result(terms, other=grad_out, begin=i * half, rows=half, forward=False) for i in range(2)
        ]
        halves = [gather_pieces(step[0]) for step in steps]
        result_blocks = [part[i] for group in ((0,), (1, 2), (3,), (4,)) for part in halves for i in group]
        gain_mlp_parts = steps[0][1] + steps[1][1]
    else:
        grad_result, gain_mlp_parts = result(
            terms, other=grad_out, begin=0, rows=own, forward=False
        )
        result_blocks = gather_pieces(grad_result)
    (output_low,) = result(terms, other=hidden_in, begin=0, rows=own, forward=True)
    grad_gain_mlp = jnp.sum(gain_mlp_parts, axis=(0, 1))
    down_sums = contract_rows(jnp.concatenate(result_blocks, axis=0), act_low).astype(BF16)
    owned_down = scatter_owned(down_sums, owners)
    grad_gate_up = act_back(result_blocks, down_pieces, after(gate_and_up, down_sums))
    ctx = lax.axis_index("ctx")
    if n == 4:
        last = hidden_back(grad_gate_up, up_full, owned, own, own, BF16, 2)
        passing = send_far(last)
        given = weight_half(hidden_low, after(grad_gate_up, *last), 1 - ctx)
        pair = hidden_back(after(grad_gate_up, given), up_full, owned, 2 * own, 2 * own, F32)
        sent, near = send_near(pair, passing)
        first = hidden_back(after(grad_gate_up, sent), up_full, owned, 0, own, F32)
        terms = [first] + near
    else:
        first = hidden_back(grad_gate_up, up_full, owned, 0, rows, F32)
        given = weight_half(hidden_low, after(grad_gate_up, first), 1 - ctx)
        terms = scatter_pieces([first[k * own : (k + 1) * own] for k in range(n)])
    up_sums = weight_half(hidden_low, grad_gate_up, ctx, other_core(given))
    grad_hidden, grad_branch, gain_attn_parts = branch_back(
        terms, after(branch, up_sums), grad_out, gain_attn
    )
    grad_gain_attn = jnp.sum(gain_attn_parts, axis=(0, 1))
    owned_up = scatter_owned(merged(after(up_sums, owned_down)))
    grad_branch_all = jnp.zeros((rows, n * width), BF16)
    for k, piece in zip(order, gather_pieces(grad_branch, True)):
        grad_branch_all = lax.dynamic_update_slice(grad_branch_all, piece, ((mine ^ k) * own, 0))
    down_new = adam(owned_down, mlp_weights, mlp_first, mlp_second, 2, 1)
    grad_mixed = matmul(after(grad_branch_all, down_new[0], output_low), w_out).astype(BF16)
    dq, dkp, dvp, dk, dv = attend_back(
        query_low, all_keys, all_values, grad_mixed, log_total.T, start
    )
    back_key = passed_along(dkp, "ctx", -1)
    back_value = passed_along(dvp, "ctx", -1)
    given = other_core(weight_half(after(grad_branch_all, dkp), attn_low, 1 - ctx))

    weighted_q, weighted_k, grad_v, inner, gain_parts = unrope(
        dq, dk, dv, back_key, back_value, qkv, qk_rs, gain_query, gain_key, cosine, sine
    )
    out_sums = weight_half(after(grad_branch_all, inner), attn_low, ctx, given)
    inner = after(axis_total(inner.T, "tensor").T, out_sums)
    grad_q = qk_rs[:, :1] * weighted_q - queries * qk_rs[:, :1] ** 3 * inner[:, :1] / D
    grad_k = qk_rs[:, 1:] * weighted_k - key_proj * qk_rs[:, 1:] ** 3 * inner[:, 1:] / D
    grad_qkv = jnp.concatenate([grad_q.astype(BF16), grad_k.astype(BF16), grad_v], axis=1)
    given = weight_half(gathered, grad_qkv, 1 - ctx)
    near_inputs = lambda source, distances, *rest: input_back(
        source, attn_full, grad_hidden, mine, distances, *rest
    )
    if n == 4:
        last = near_inputs(after(grad_qkv, given), order[1:2], BF16, 2)
        passing = send_far(last)
        attn_sums = weight_half(
            gathered, after(grad_qkv, *last), ctx, other_core(given), out_sums
        )
        pair = near_inputs(after(grad_qkv, attn_sums), order[2:], F32)
        sent, near = send_near(pair, passing)
    else:
        attn_sums = weight_half(gathered, grad_qkv, ctx, other_core(given), out_sums)
        parts = near_inputs(grad_qkv, order, F32)
        sent = parts
    owned_attn = scatter_owned(merged(after(attn_sums, owned_up)))
    new_mlp, mlp_one, mlp_two = adam(
        after(owned_up, sent), mlp_weights, mlp_first, mlp_second, 0, 2, down_new
    )
    output_low = after(output_low, new_mlp)
    output = jnp.zeros((rows, width), BF16)
    for k in range(n):
        piece = lax.dynamic_slice_in_dim(output_low, (mine ^ k) * width, width, axis=1)
        piece = swap(piece, k) if k else piece
        output = lax.dynamic_update_slice(output, piece, ((mine ^ k) * own, 0))
    if n == 4:
        grad_inputs = add_up([near_inputs(after(grad_qkv, new_mlp), order[:1], F32)] + near)
    else:
        grad_inputs = add_up(scatter_pieces([parts[k * rows : (k + 1) * rows] for k in range(n)]))

    wide = jnp.stack([grad_gain_attn, grad_gain_mlp])
    near = lax.dynamic_slice_in_dim(wide, mine * width, width, axis=1)
    for k in range(1, n):
        near = near + swap(lax.dynamic_slice_in_dim(wide, (mine ^ k) * width, width, axis=1), k)
    gain_sums = jnp.concatenate([jnp.sum(gain_parts, axis=0), near])
    gain_sums = axis_total(axis_total(after(gain_sums, sent), "ctx"), "dp")
    share = norm_gains.shape[1]
    place = (lax.axis_index("dp") * lax.axis_size("ctx") + lax.axis_index("ctx")) * share
    gain_grad = lax.dynamic_slice_in_dim(gain_sums, place, share, axis=1)

    new_attn, attn_one, attn_two = adam(owned_attn, attn_weights, attn_first, attn_second, 0, 4)
    new_gains, gain_one, gain_two = adam_step(
        norm_gains, gain_grad, gain_first, gain_second, GAIN_RATE, 0.0
    )
    return (
        output,
        grad_inputs,
        new_attn,
        attn_one,
        attn_two,
        new_mlp,
        mlp_one,
        mlp_two,
        new_gains,
        gain_one,
        gain_two,
    )


def solution(mesh):
    return jax.shard_map(
        body,
        mesh=mesh,
        in_specs=(
            P(("dp", "ctx"), "tensor"),
            P(("dp", "ctx"), "tensor"),
            P("dp", None),
            P(None, ("dp", "ctx"), "tensor"),
            P(None, ("dp", "ctx"), "tensor"),
            P(None, ("tensor", "dp", "ctx")),
            P(None, ("dp", "ctx"), "tensor"),
            P(None, ("dp", "ctx"), "tensor"),
            P(None, ("dp", "ctx"), "tensor"),
            P(None, ("dp", "ctx"), "tensor"),
            P(None, ("tensor", "dp", "ctx")),
            P(None, ("tensor", "dp", "ctx")),
        ),
        out_specs=(
            P(("dp", "ctx"), "tensor"),
            P(("dp", "ctx"), "tensor"),
            P(None, ("dp", "ctx"), "tensor"),
            P(None, ("dp", "ctx"), "tensor"),
            P(None, ("dp", "ctx"), "tensor"),
            P(None, ("dp", "ctx"), "tensor"),
            P(None, ("dp", "ctx"), "tensor"),
            P(None, ("dp", "ctx"), "tensor"),
            P(None, ("tensor", "dp", "ctx")),
            P(None, ("tensor", "dp", "ctx")),
            P(None, ("tensor", "dp", "ctx")),
        ),
        check_vma=False,
    )
```

```python
import functools

import jax
import jax.numpy as jnp
from jax import lax
from jax.experimental import pallas as pl
from jax.experimental.pallas import tpu as pltpu
from jax.sharding import PartitionSpec as P

D = 2048
HEAD_DIM = 128
STEP = 10


NORM_EPS = 1e-06
ROPE_THETA = 500000.0
BETA_ONE = 0.9
BETA_TWO = 0.95
ADAM_EPS = 1e-08
WEIGHT_DECAY = 0.1
LEARN_RATE = 0.02
GAIN_RATE = 1.0

SCORE_SCALE = HEAD_DIM ** (-0.5)
Q_BLOCK = 256
VMEM = 32
BF16 = jnp.bfloat16
F32 = jnp.float32


def passed_along(block, axis, distance):
    devices = range(lax.axis_size(axis))
    route = [(i - distance, i) for i in devices if i - distance in devices]
    return lax.ppermute(block, axis, route)


def swap(block, distance):
    return lax.ppermute(
        block, "tensor", [(i, i ^ distance) for i in range(lax.axis_size("tensor"))]
    )


def piece_order():
    n = lax.axis_size("tensor")
    return (0, 3, 1, 2) if n == 4 else tuple(range(n))


def gather_pieces(block, finely=False):
    n = lax.axis_size("tensor")
    if n != 4:
        return [block] + [swap(block, k) for k in range(1, n)]
    half = block.shape[0] // 2
    if not finely:
        one, two = swap(block, 1), swap(block, 2)
        return [block, swap(two[:half], 1), swap(one[half:], 2), one, two]
    upper, lower = block[:half], block[half:]
    two_upper, one_lower = swap(upper, 2), swap(lower, 1)
    one_upper, two_lower = swap(upper, 1), swap(lower, 2)
    far_upper, far_lower = swap(two_upper, 1), swap(one_lower, 2)
    return [
        jnp.concatenate(pair, axis=0)
        for pair in ((upper, lower), (far_upper, far_lower), (one_upper, one_lower), (two_upper, two_lower))
    ]


def send_far(last):
    upper, lower = last
    return jnp.concatenate([swap(lower, 2), swap(upper, 1)], axis=0)


def near_blocks(pair, passing):
    rows = pair.shape[0] // 2
    passing = jnp.pad(passing.astype(F32), ((rows // 2, rows // 2), (0, 0)))
    return (pair + passing).astype(BF16)


def send_near(pair, passing):
    rows = pair.shape[0] // 2
    pair = near_blocks(pair, passing)
    return pair, [swap(pair[:rows], 1), swap(pair[rows:], 2)]


def scatter_pieces(parts):
    if lax.axis_size("tensor") == 4:
        passing = send_far(jnp.split(parts[1].astype(BF16), 2, axis=0))
        return [parts[0]] + send_near(jnp.concatenate(parts[2:], axis=0), passing)[1]
    total = parts[0]
    for k in range(1, len(parts)):
        total = total + swap(parts[k].astype(BF16), k).astype(F32)
    return [total]


def add_up(terms):
    return functools.reduce(jnp.add, [term.astype(F32) for term in terms])


def axis_total(values, axis):
    n = lax.axis_size(axis)
    flat = values.reshape(-1, HEAD_DIM)
    others = [
        lax.ppermute(flat, axis, [(i, i ^ k if n in (2, 4, 8) else (i + k) % n) for i in range(n)])
        for k in range(1, n)
    ]
    return functools.reduce(jnp.add, others, flat).reshape(values.shape)


def doc_begins(doc_row, token_place):
    doc_ends = jnp.cumsum(doc_row)
    passed = token_place[:, None] >= doc_ends[None, :]
    return jnp.max(
        jnp.where(passed, doc_ends[None, :], jnp.zeros_like(doc_ends)[None, :]), axis=1
    )


def turn_tables(position):
    half_dim = HEAD_DIM // 2
    frequency = ROPE_THETA ** (-2.0 * jnp.arange(half_dim, dtype=F32) / HEAD_DIM)
    angles = position.astype(F32)[:, None] * frequency[None, :]
    cosine, sine = jnp.cos(angles), jnp.sin(angles)
    return jnp.concatenate([cosine, cosine], axis=1), jnp.concatenate([-sine, sine], axis=1)


def adam_step(weight, gradient, moment_one, moment_two, rate, decay):
    moment_one = BETA_ONE * moment_one + (1.0 - BETA_ONE) * gradient
    moment_two = BETA_TWO * moment_two + (1.0 - BETA_TWO) * gradient * gradient
    fix_one = 1.0 - BETA_ONE**STEP
    fix_two = 1.0 - BETA_TWO**STEP
    update = moment_one / fix_one / (jnp.sqrt(moment_two / fix_two) + ADAM_EPS)
    return (weight - rate * (update + decay * weight), moment_one, moment_two)


def adam_kernel(grad_ref, weight_ref, first_ref, second_ref, *rest):
    wide = weight_ref.shape[2]
    for i in range(weight_ref.shape[0]):
        grad = grad_ref[:, i * wide : (i + 1) * wide].astype(F32)
        new = adam_step(
            weight_ref[i], grad, first_ref[i], second_ref[i], LEARN_RATE, WEIGHT_DECAY
        )
        for ref, value in zip(rest[-3:], new):
            ref[i] = value


def adam(grad, weights, first, second, begin, count, earlier=()):
    _, rows, wide = weights.shape
    block = min(wide, 1024)
    group = max(1, min(count, 1024 // block))
    steps, at = wide // block, begin // group
    spec = pl.BlockSpec((group, rows, block), lambda k, j: (at + k, 0, j))
    return pl.pallas_call(
        adam_kernel,
        grid=(count // group, steps),
        in_specs=[
            pl.BlockSpec((rows, group * block), lambda k, j: (0, k * steps + j)), spec, spec, spec
        ]
        + [pl.BlockSpec(memory_space=pl.ANY)] * len(earlier),
        out_specs=[spec] * 3,
        out_shape=[jax.ShapeDtypeStruct(weights.shape, F32)] * 3,
        input_output_aliases={4 + i: i for i in range(len(earlier))},
        compiler_params=pltpu.CompilerParams(vmem_limit_bytes=60 * 1024 * 1024),
        cost_estimate=pl.CostEstimate(
            flops=0, bytes_accessed=count * rows * wide * 26, transcendentals=0
        ),
    )(grad, weights, first, second, *earlier)


def matmul(left, right):
    return jnp.dot(left, right, preferred_element_type=F32)


def contract_rows(left, right):
    return lax.dot_general(left, right, (((0,), (0,)), ((), ())), preferred_element_type=F32)


def by_columns(left, right):
    return lax.dot_general(left, right, (((1,), (1,)), ((), ())), preferred_element_type=F32)


def along_line(block, *hops):
    return lax.ppermute(block, "dp", list(hops))


def line_gather(block):
    place = lax.axis_index("dp")
    below = along_line(block, (0, 1), (1, 2), (2, 3))
    above = along_line(block, (1, 0), (2, 1), (3, 2))
    across = along_line(block, (0, 2), (1, 3), (2, 0), (3, 1))
    ends = along_line(across, (2, 3), (1, 0))
    found = [block, jnp.where(place == 3, ends, above), across, jnp.where(place == 0, ends, below)]
    whole = jnp.zeros((4,) + block.shape, block.dtype)
    for i, value in enumerate(found):
        at = (place + i) % 4
        whole = lax.dynamic_update_slice(whole, value[None], (at,) + (0,) * block.ndim)
    return whole


def line_scatter(blocks):
    place = lax.axis_index("dp")
    pick = lambda i: lax.dynamic_index_in_dim(blocks, i % 4, axis=0, keepdims=False)
    far = along_line(pick(jnp.where(place == 0, 3, 0)), (0, 1), (3, 2))
    above = along_line(pick(place + 1), (0, 1), (1, 2), (2, 3))
    below = along_line(pick(place + 3), (1, 0), (2, 1), (3, 2))
    across = (pick(place + 2).astype(F32) + far.astype(F32)).astype(BF16)
    across = along_line(across, (0, 2), (1, 3), (2, 0), (3, 1))
    return add_up([pick(place), above, below, across]).astype(BF16)


def after(value, *earlier):
    return lax.optimization_barrier((value,) + earlier)[0]


def other_core(values):
    return lax.ppermute(values, "ctx", [(0, 1), (1, 0)])


def scatter_owned(sums, axes=("dp",)):
    return lax.psum_scatter(sums, axes, scatter_dimension=0, tiled=True)


def call(
    kernel, grid, in_specs, out_specs, out_shape, scratch=(), flops=0, nbytes=0, trans=0, scalars=0,
    announced=0.25, vmem=VMEM,
):
    return pl.pallas_call(
        kernel,
        grid_spec=pltpu.PrefetchScalarGridSpec(
            num_scalar_prefetch=scalars,
            grid=grid,
            in_specs=in_specs,
            out_specs=out_specs,
            scratch_shapes=list(scratch),
        ),
        out_shape=out_shape,
        compiler_params=pltpu.CompilerParams(vmem_limit_bytes=vmem * 1024 * 1024),
        cost_estimate=pl.CostEstimate(
            flops=int(flops * announced),
            bytes_accessed=int(nbytes * announced),
            transcendentals=int(trans * announced),
        ),
    )


def weight_half_kernel(blocks, steps, ctx_ref, *refs):
    left, right_ref, (out_ref, turned) = refs[:blocks], refs[blocks], refs[-2:]
    given_ref = refs[blocks + 1] if len(refs) > blocks + 3 else None
    tail_ref = refs[blocks + 2] if len(refs) > blocks + 4 else None

    @pl.when(pl.program_id(0) == 0)
    def _():
        for i, ref in enumerate(left):
            turned[i] = ref[...].T

    @pl.when(pl.program_id(0) < steps)
    def _():
        right = right_ref[...]
        for i in range(blocks):
            total = matmul(turned[i], right)
            if given_ref is not None:
                total = total + given_ref[i].astype(F32)
            out_ref[i] = total.astype(BF16)

    if tail_ref is not None:

        @pl.when(pl.program_id(0) >= steps)
        def _():
            out_ref[...] = tail_ref[...]


def weight_half(left, right, ctx, given=None, tail=None):
    rows, depth = left.shape
    blocks = lax.axis_size("dp")
    owned = depth // (blocks * lax.axis_size("ctx"))
    n_ctx = lax.axis_size("ctx")
    wide = right.shape[-1]
    block = next(size for size in (512, 256, 128) if wide % size == 0)
    each = wide // block
    steps = each * (right.shape[0] if right.ndim == 3 else 1)
    last = steps - 1
    if right.ndim == 3:
        right_spec = pl.BlockSpec((None, rows, block), lambda j, c: (j // each, 0, j % each))
    else:
        right_spec = pl.BlockSpec((rows, block), lambda j, c: (0, jnp.minimum(j, last)))
    specs = [
        pl.BlockSpec((rows, owned), lambda j, c, i=i: (0, n_ctx * i + c[0])) for i in range(blocks)
    ]
    operands = [left] * blocks + [right]
    specs.append(right_spec)
    columns = steps * block
    more = 0
    if given is not None:
        operands.append(given)
        specs.append(
            pl.BlockSpec((blocks, owned, block), lambda j, c: (0, 0, jnp.minimum(j, last)))
        )
    if tail is not None:
        operands.append(tail)
        more = tail.shape[2] // block
        specs.append(
            pl.BlockSpec((blocks, owned, block), lambda j, c: (0, 0, jnp.maximum(j - steps, 0)))
        )
    return call(
        functools.partial(weight_half_kernel, blocks, steps),
        (steps + more,),
        specs,
        pl.BlockSpec((blocks, owned, block), lambda j, c: (0, 0, j)),
        jax.ShapeDtypeStruct((blocks, owned, columns + more * block), BF16),
        [pltpu.VMEM((blocks, owned, rows), BF16)],
        flops=2 * rows * blocks * owned * columns,
        nbytes=2 * (rows * blocks * owned + rows * columns + 2 * blocks * owned * columns),
        scalars=1,
    )(ctx[None], *operands)


def rope_kernel(q_ref, k_ref, v_ref, rs_ref, gq_ref, gk_ref, cos_ref, sin_ref, qo, ko, vo):
    cosine, sine = cos_ref[...], sin_ref[...]
    for place, (src, gain, dst) in enumerate(((q_ref, gq_ref, qo), (k_ref, gk_ref, ko))):
        scale = rs_ref[:, place : place + 1]
        for head in range(src.shape[1] // HEAD_DIM):
            cols = slice(head * HEAD_DIM, (head + 1) * HEAD_DIM)
            x = src[:, cols] * scale * gain[:, cols]
            dst[:, cols] = (x * cosine + pltpu.roll(x, HEAD_DIM // 2, 1) * sine).astype(BF16)
    vo[...] = v_ref[...].astype(BF16)


def rope(qkv, rs, gain_query, gain_key, cosine, sine):
    rows, width = qkv.shape[0], qkv.shape[1] // 3
    block = min(rows, 256)
    part = lambda j: pl.BlockSpec((block, width), lambda i, j=j: (i, j))
    gain = pl.BlockSpec((1, width), lambda i: (0, 0))
    table = pl.BlockSpec((block, HEAD_DIM), lambda i: (i, 0))
    out = jax.ShapeDtypeStruct((rows, width), BF16)
    return call(
        rope_kernel,
        (rows // block,),
        [part(0), part(1), part(2), pl.BlockSpec((block, 2), lambda i: (i, 0)), gain, gain]
        + [table, table],
        [part(0)] * 3,
        [out] * 3,
        flops=rows * width * 12,
        nbytes=rows * width * 18,
    )(qkv, qkv, qkv, rs, gain_query[None], gain_key[None], cosine, sine)


def attend_kernel(span, q_ref, k_ref, v_ref, start_ref, o_ref, lse_ref):
    rows = q_ref.shape[0]
    step = pl.program_id(0)
    first = pl.multiple_of(step * rows, rows)
    shape = (rows, span)
    row = lax.broadcasted_iota(jnp.int32, shape, 0)
    column = lax.broadcasted_iota(jnp.int32, shape, 1) - (span - rows)
    allowed = (column <= row) & (column >= start_ref[...] - step * rows)
    for head in range(q_ref.shape[1] // HEAD_DIM):
        cols = slice(head * HEAD_DIM, (head + 1) * HEAD_DIM)
        keys = k_ref[pl.ds(first, span), cols]
        values = v_ref[pl.ds(first, span), cols]
        scores = by_columns(q_ref[:, cols], keys) * SCORE_SCALE
        scores = jnp.where(allowed, scores, -1e30)
        top = jnp.max(scores, axis=1, keepdims=True)
        weights = jnp.exp(scores - top)
        total = jnp.sum(weights, axis=1, keepdims=True)
        low = (weights / total).astype(BF16)
        o_ref[:, cols] = matmul(low, values).astype(BF16)
        lse_ref[:, head : head + 1] = top + jnp.log(total)


def attend(query, keys, values, start):
    rows, width = query.shape
    heads = width // HEAD_DIM
    block = Q_BLOCK
    span = rows + block
    whole = pl.BlockSpec(keys.shape, lambda i: (0, 0))
    return call(
        functools.partial(attend_kernel, span),
        (rows // block,),
        [pl.BlockSpec((block, width), lambda i: (i, 0)), whole, whole]
        + [pl.BlockSpec((block, 1), lambda i: (i, 0))],
        [pl.BlockSpec((block, width), lambda i: (i, 0)), pl.BlockSpec((block, heads), lambda i: (i, 0))],
        [jax.ShapeDtypeStruct((rows, width), BF16), jax.ShapeDtypeStruct((rows, heads), F32)],
        flops=4 * rows * span * width,
        nbytes=rows * width * 12,
        trans=rows * span * heads,
    )(query, keys, values, start[:, None])


def attend_back_kernel(
    span, q_ref, k_ref, v_ref, do_ref, lse_ref, start_ref, dq_ref, dkp_ref, dvp_ref, dk_ref, dv_ref, ka, va
):
    rows = q_ref.shape[0]
    step = pl.program_id(0)
    first = pl.multiple_of(step * rows, rows)

    @pl.when(step == 0)
    def _():
        ka[...] = jnp.zeros_like(ka)
        va[...] = jnp.zeros_like(va)

    shape = (span, rows)
    column = lax.broadcasted_iota(jnp.int32, shape, 0) - (span - rows)
    row = lax.broadcasted_iota(jnp.int32, shape, 1)
    allowed = (column <= row) & (column >= start_ref[...] - step * rows)
    for head in range(q_ref.shape[1] // HEAD_DIM):
        cols = slice(head * HEAD_DIM, (head + 1) * HEAD_DIM)
        query, grad = q_ref[:, cols], do_ref[:, cols]
        keys = k_ref[pl.ds(first, span), cols]
        values = v_ref[pl.ds(first, span), cols]
        scores = by_columns(keys, query) * SCORE_SCALE
        weights = jnp.where(allowed, jnp.exp(scores - lse_ref[head : head + 1, :]), 0.0)
        grad_weights = by_columns(values, grad)
        mean = jnp.sum(weights * grad_weights, axis=0, keepdims=True)
        grad_scores = (weights * (grad_weights - mean)).astype(BF16)
        dq_ref[:, cols] = contract_rows(grad_scores, keys) * SCORE_SCALE
        va[pl.ds(first, span), cols] += matmul(weights.astype(BF16), grad)
        ka[pl.ds(first, span), cols] += matmul(grad_scores, query) * SCORE_SCALE

    @pl.when(step == pl.num_programs(0) - 1)
    def _():
        total = dk_ref.shape[0]
        dkp_ref[...] = ka[:total, :].astype(BF16)
        dvp_ref[...] = va[:total, :].astype(BF16)
        dk_ref[...] = ka[total:, :]
        dv_ref[...] = va[total:, :]


def attend_back(query, keys, values, grad, lse, start):
    rows, width = query.shape
    heads = width // HEAD_DIM
    block = Q_BLOCK
    span = rows + block
    whole = pl.BlockSpec(keys.shape, lambda i: (0, 0))
    mine = pl.BlockSpec((block, width), lambda i: (i, 0))
    full = pl.BlockSpec((rows, width), lambda i: (0, 0))
    return call(
        functools.partial(attend_back_kernel, span),
        (rows // block,),
        [mine, whole, whole, mine]
        + [pl.BlockSpec((heads, block), lambda i: (0, i)), pl.BlockSpec((1, block), lambda i: (0, i))],
        [mine, full, full, full, full],
        [jax.ShapeDtypeStruct((rows, width), t) for t in (F32, BF16, BF16, F32, F32)],
        [pltpu.VMEM(keys.shape, F32)] * 2,
        flops=10 * rows * span * width,
        nbytes=rows * width * 28,
        trans=rows * span * heads,
        announced=12,
    )(query, keys, values, grad, lse, start[None, :])


def unrope_kernel(
    dq_ref, dk_ref, dv_ref, bk_ref, bv_ref, q_ref, k_ref, rs_ref, gq_ref, gk_ref, cos_ref, sin_ref,
    wq_ref, wk_ref, dvo_ref, inner_ref, gain_ref,
):
    cosine, sine = cos_ref[...], -sin_ref[...]
    for place, (src, back, x_ref, gain, dst) in enumerate(
        ((dq_ref, None, q_ref, gq_ref, wq_ref), (dk_ref, bk_ref, k_ref, gk_ref, wk_ref))
    ):
        scale = rs_ref[:, place : place + 1]
        inner = 0.0
        for head in range(src.shape[1] // HEAD_DIM):
            cols = slice(head * HEAD_DIM, (head + 1) * HEAD_DIM)
            grad = src[:, cols]
            if back is not None:
                grad = grad + back[:, cols].astype(F32)
            grad = grad * cosine + pltpu.roll(grad, HEAD_DIM // 2, 1) * sine
            x = x_ref[:, cols]
            weighted = grad * gain[:, cols]
            dst[:, cols] = weighted
            inner = inner + jnp.sum(weighted * x, axis=1, keepdims=True)
            gain_ref[0, place : place + 1, cols] = jnp.sum(grad * x * scale, axis=0, keepdims=True)
        inner_ref[:, place : place + 1] = inner
    dvo_ref[...] = (dv_ref[...] + bv_ref[...].astype(F32)).astype(BF16)


def unrope(dq, dk, dv, back_k, back_v, qkv, rs, gain_query, gain_key, cosine, sine):
    rows, width = dq.shape
    block = min(rows, 256)
    part = lambda j: pl.BlockSpec((block, width), lambda i, j=j: (i, j))
    gain = pl.BlockSpec((1, width), lambda i: (0, 0))
    table = pl.BlockSpec((block, HEAD_DIM), lambda i: (i, 0))
    pair = pl.BlockSpec((block, 2), lambda i: (i, 0))
    return call(
        unrope_kernel,
        (rows // block,),
        [part(0)] * 5 + [part(0), part(1), pair, gain, gain, table, table],
        [part(0)] * 3 + [pair, pl.BlockSpec((1, 2, width), lambda i: (i, 0, 0))],
        [jax.ShapeDtypeStruct((rows, width), t) for t in (F32, F32, BF16)]
        + [jax.ShapeDtypeStruct((rows, 2), F32)]
        + [jax.ShapeDtypeStruct((rows // block, 2, width), F32)],
        flops=rows * width * 30,
        nbytes=rows * width * 34,
    )(dq, dk, dv, back_k, back_v, qkv, qkv, rs, gain_query[None], gain_key[None], cosine, sine)


def merged(block):
    return block.reshape(-1, block.shape[-1])


def gate_up_kernel(x_ref, wg_ref, wu_ref, gu_ref, act_ref):
    x = x_ref[...]
    gate, up = matmul(x, merged(wg_ref[...])), matmul(x, merged(wu_ref[...]))
    gu_ref[0], gu_ref[1] = gate, up
    act_ref[...] = (gate * jax.nn.sigmoid(gate) * up).astype(BF16)


def gate_up(x, weights, owned):
    rows, depth = x.shape
    owners, hidden = weights.shape[0], weights.shape[2]
    block = min(hidden, 256)
    return call(
        gate_up_kernel,
        (hidden // block,),
        [
            pl.BlockSpec((rows, depth), lambda j: (0, 0)),
            pl.BlockSpec((owners, owned, block), lambda j: (0, 0, j)),
            pl.BlockSpec((owners, owned, block), lambda j: (0, 1, j)),
        ],
        [
            pl.BlockSpec((2, rows, block), lambda j: (0, 0, j)),
            pl.BlockSpec((rows, block), lambda j: (0, j)),
        ],
        [
            jax.ShapeDtypeStruct((2, rows, hidden), F32),
            jax.ShapeDtypeStruct((rows, hidden), BF16),
        ],
        flops=4 * rows * depth * hidden,
        nbytes=4 * depth * hidden + rows * (10 * hidden + 2 * depth),
        trans=rows * hidden,
    )(x, weights, weights)


def store_rows(total, outs):
    rows = total.shape[0] // len(outs)
    for i, ref in enumerate(outs):
        ref[...] = total[i * rows : (i + 1) * rows].astype(ref.dtype)


def row_outputs(rows, columns, block, kind, parts):
    return (
        [pl.BlockSpec((rows // parts, block), lambda j: (0, j))] * parts,
        [jax.ShapeDtypeStruct((rows // parts, columns), kind)] * parts,
    )


def down_kernel(x_ref, w_ref, *outs):
    store_rows(by_columns(x_ref[...], merged(w_ref[...])), outs)


def down(x, weights, place, count, begin, rows, kind, parts=1):
    owners, hidden = weights.shape[0], weights.shape[2]
    group = max(1, min(owners, 512 // count))
    at, row = begin // rows, place // count
    outs = call(
        down_kernel,
        (owners // group,),
        [
            pl.BlockSpec((rows, hidden), lambda j: (at, 0)),
            pl.BlockSpec((group, count, hidden), lambda j: (j, row, 0)),
        ],
        *row_outputs(rows, owners * count, group * count, kind, parts),
        flops=2 * rows * owners * count * hidden,
        nbytes=2 * owners * count * hidden + rows * (2 * hidden + 4 * owners * count),
    )(x, weights)
    return outs if parts > 1 else outs[0]


def act_back_kernel(cuts, count_x, *refs):
    blocks, weights = refs[:count_x], refs[count_x : count_x + len(cuts)]
    gu_ref, out_ref, split = refs[count_x + len(cuts) :]
    owners = weights[0].shape[0]
    owned = split.shape[1] // owners

    @pl.when(pl.program_id(0) == 0)
    def _():
        row = 0
        for x_ref in blocks:
            rows, to = slice(row, row + x_ref.shape[0]), 0
            row += x_ref.shape[0]
            for begin, count in cuts:
                for i in range(owners):
                    at = i * owned + begin
                    split[rows, to : to + count] = x_ref[:, at : at + count]
                    to += count

    grad, at = 0.0, 0
    for (_, count), ref in zip(cuts, weights):
        grad = grad + matmul(split[:, at : at + owners * count], merged(ref[...]))
        at += owners * count
    gate, up = gu_ref[0], gu_ref[1]
    sig = jax.nn.sigmoid(gate)
    out_ref[0] = (grad * up * sig * (1.0 + gate * (1.0 - sig))).astype(BF16)
    out_ref[1] = (grad * gate * sig).astype(BF16)


def act_back(blocks, pieces, gate_and_up):
    _, rows, hidden = gate_and_up.shape
    depth = blocks[0].shape[1]
    block = min(hidden, 512)
    pair = pl.BlockSpec((2, rows, block), lambda j: (0, 0, j))
    return call(
        functools.partial(
            act_back_kernel, [(first, count) for _, _, count, first in pieces], len(blocks)
        ),
        (hidden // block,),
        [pl.BlockSpec(array.shape, lambda j: (0, 0)) for array in blocks]
        + [
            pl.BlockSpec((array.shape[0], count, block), lambda j, at=place // count: (0, at, j))
            for array, place, count, _ in pieces
        ]
        + [pair],
        pair,
        jax.ShapeDtypeStruct((2, rows, hidden), BF16),
        [pltpu.VMEM((rows, depth), BF16)],
        vmem=56,
        flops=2 * rows * depth * hidden,
        nbytes=2 * depth * hidden + rows * (12 * hidden + 2 * depth),
        trans=rows * hidden,
    )(*blocks, *[array for array, _, _, _ in pieces], gate_and_up)


def hidden_back_kernel(x_ref, wg_ref, wu_ref, *outs):
    total = by_columns(x_ref[0], merged(wg_ref[...])) + by_columns(x_ref[1], merged(wu_ref[...]))
    store_rows(total, outs)


def hidden_back(grads, weights, owned, begin, rows, kind, parts=1):
    hidden, owners = grads.shape[2], weights.shape[0]
    group = max(1, (512 if rows <= 512 else 256) // owned)
    at = begin // rows
    outs = call(
        hidden_back_kernel,
        (owners // group,),
        [
            pl.BlockSpec((2, rows, hidden), lambda j: (0, at, 0)),
            pl.BlockSpec((group, owned, hidden), lambda j: (j, 0, 0)),
            pl.BlockSpec((group, owned, hidden), lambda j: (j, 1, 0)),
        ],
        *row_outputs(rows, owners * owned, group * owned, kind, parts),
        flops=4 * rows * owners * owned * hidden,
        nbytes=4 * owners * owned * hidden + rows * (4 * hidden + 4 * owners * owned),
    )(grads, weights, weights)
    return outs if parts > 1 else outs[0]


def total_of(refs):
    return functools.reduce(jnp.add, [ref[...].astype(F32) for ref in refs])


def norm_back(grad, gain, values, scale):
    weighted = grad * gain
    inner = jnp.sum(weighted * values, axis=1, keepdims=True)
    back = scale * weighted - values * scale**3 * inner / D
    return back, jnp.sum(grad * values * scale, axis=0, keepdims=True)


def result_of(counts, owners, refs):
    begin, parts = 0, []
    for count in counts:
        parts.append(total_of(refs[begin : begin + count]))
        begin += count
    result = parts[0]
    if len(parts) > 1:
        width = result.shape[1] // owners
        result = jnp.concatenate(
            [part[:, i * width : (i + 1) * width] for i in range(owners) for part in parts], axis=1
        )
    scale = lax.rsqrt(jnp.mean(result * result, axis=1, keepdims=True) + NORM_EPS)
    return result, scale, refs[begin:]


def result_kernel(counts, owners, *refs):
    result, scale, refs = result_of(counts, owners, refs)
    grad_ref, gain_ref, back_ref, gain_grad_ref = refs
    back, gain_grad = norm_back(grad_ref[...].astype(F32), gain_ref[...], result, scale)
    back_ref[...] = back.astype(BF16)
    gain_grad_ref[0] = gain_grad


def output_kernel(counts, owners, *refs):
    result, scale, (hidden_ref, gain_ref, out_ref) = result_of(counts, owners, refs)
    out_ref[...] = (hidden_ref[...] + result * scale * gain_ref[...]).astype(BF16)


def result_step(parts, owners, other, gain, begin, rows, forward):
    depth = other.shape[1]
    block = min(rows, 64)
    at = begin // block
    flat = [array for part in parts for array in part]
    back_specs = [pl.BlockSpec((1, 1, depth), lambda i: (i, 0, 0))]
    back_shapes = [jax.ShapeDtypeStruct((rows // block, 1, depth), F32)]
    return call(
        functools.partial(
            output_kernel if forward else result_kernel, [len(part) for part in parts], owners
        ),
        (rows // block,),
        [pl.BlockSpec((block, array.shape[1]), lambda i: (i + at, 0)) for array in flat + [other]]
        + [pl.BlockSpec((1, depth), lambda i: (0, 0))],
        [pl.BlockSpec((block, depth), lambda i: (i, 0))] + ([] if forward else back_specs),
        [jax.ShapeDtypeStruct((rows, depth), BF16)] + ([] if forward else back_shapes),
        flops=rows * depth * 20,
        nbytes=rows * depth * 20,
    )(*flat, other, gain[None])


def branch_back_kernel(count, *refs):
    branch_ref, grad_ref, gain_ref, hidden_ref, back_ref, gain_grad_ref = refs[count:]
    grad = grad_ref[...].astype(F32) + total_of(refs[:count])
    hidden_ref[...] = grad
    branch = branch_ref[...]
    scale = lax.rsqrt(jnp.mean(branch * branch, axis=1, keepdims=True) + NORM_EPS)
    back, gain_grad = norm_back(grad, gain_ref[...], branch, scale)
    back_ref[...] = back.astype(BF16)
    gain_grad_ref[0] = gain_grad


def branch_back(parts, branch, grad_out, gain):
    rows, depth = branch.shape
    block = min(rows, 64)
    mine = pl.BlockSpec((block, depth), lambda i: (i, 0))
    return call(
        functools.partial(branch_back_kernel, len(parts)),
        (rows // block,),
        [mine] * (len(parts) + 2) + [pl.BlockSpec((1, depth), lambda i: (0, 0))],
        [mine, mine, pl.BlockSpec((1, 1, depth), lambda i: (i, 0, 0))],
        [
            jax.ShapeDtypeStruct((rows, depth), F32),
            jax.ShapeDtypeStruct((rows, depth), BF16),
            jax.ShapeDtypeStruct((rows // block, 1, depth), F32),
        ],
        flops=rows * depth * 20,
        nbytes=rows * depth * 20,
    )(*parts, branch, grad_out, gain[None])


def input_back_kernel(places_ref, x_ref, w_ref, residual_ref, *outs):
    step, half = pl.program_id(1), pl.num_programs(1) // 2
    own = jnp.where(step == places_ref[0], residual_ref[...], 0.0)
    total = by_columns(x_ref[...], w_ref[...]) + own
    if len(outs) == 1:
        outs[0][...] = total.astype(outs[0].dtype)
        return

    @pl.when(step < half)
    def _():
        outs[0][...] = total.astype(outs[0].dtype)

    @pl.when(step >= half)
    def _():
        outs[1][...] = total.astype(outs[1].dtype)


def input_back(grads, weights, residual, mine, distances, kind, parts=1):
    rows, deep = grads.shape
    own = residual.shape[0]
    width = deep // 3
    blocks = rows // own
    half = blocks // 2
    places = jnp.stack([mine] + [mine ^ k for k in distances])
    specs = [pl.BlockSpec((own, width), lambda a, i, p: (a * blocks + i, 0))]
    if parts == 2:
        specs = [
            pl.BlockSpec((own, width), lambda a, i, p: (jnp.minimum(i, half - 1), 0)),
            pl.BlockSpec((own, width), lambda a, i, p: (jnp.maximum(i - half, 0), 0)),
        ]
    outs = call(
        input_back_kernel,
        (len(distances), blocks),
        [
            pl.BlockSpec((own, deep), lambda a, i, p: (i, 0)),
            pl.BlockSpec((width, deep), lambda a, i, p: (p[1 + a], 0)),
            pl.BlockSpec((own, width), lambda a, i, p: (0, p[1 + a])),
        ],
        specs,
        [jax.ShapeDtypeStruct((len(distances) * rows // parts, width), kind)] * parts,
        announced=2,
        flops=2 * rows * deep * width * len(distances),
        nbytes=rows * deep * 2 * (len(distances) + 1),
        scalars=1,
    )(places, grads, weights, residual)
    return outs if parts > 1 else outs[0]


def body(
    inputs,
    cotangent,
    doc_lengths,
    attn_weights,
    mlp_weights,
    norm_gains,
    attn_first,
    attn_second,
    mlp_first,
    mlp_second,
    gain_first,
    gain_second,
):
    owners = ("dp", "ctx")
    n = lax.axis_size("tensor")
    mine = lax.axis_index("tensor")
    rows, width = inputs.shape
    own = rows // n
    hidden = mlp_weights.shape[2]

    low = attn_weights.astype(BF16)
    line = lax.axis_size("dp") == 4
    attn_shard = jnp.concatenate([low[0], low[1], low[2]] + ([] if line else [low[3]]), axis=1)
    out_shard = low[3]
    low = mlp_weights.astype(BF16)
    owned = low.shape[1]
    lead = owned // 2 if owned % 256 == 0 else 0
    up_shard = jnp.concatenate([low[0], low[1], low[2, :lead]], axis=0)
    attn_full = lax.all_gather(attn_shard, owners, axis=0, tiled=True)
    up_full = lax.all_gather(up_shard, owners, axis=0)
    down_full = lax.all_gather(low[2, lead:], owners, axis=0)
    down_pieces = [(down_full, 0, owned - lead, lead)]
    if lead:
        down_pieces = [(up_full, 2 * owned, lead, 0)] + down_pieces
    if line:
        w_qkv, place = attn_full, lax.axis_index("ctx")
        kept = line_gather(out_shard)
        w_out = jnp.zeros((4, 2) + out_shard.shape, BF16)
        for at, value in ((place, kept), (1 - place, other_core(kept))):
            w_out = lax.dynamic_update_slice(w_out, value[:, None], (0, at, 0, 0))
        w_out = w_out.reshape(-1, width)
    else:
        w_qkv, w_out = attn_full[:, : 3 * width], attn_full[:, 3 * width :]
    gains = lax.all_gather(
        norm_gains.astype(BF16), ("tensor",) + owners, axis=1, tiled=True
    ).astype(F32)
    gain_attn, gain_mlp = gains[2], gains[3]
    near = lax.dynamic_slice_in_dim(gains, mine * width, width, axis=1)
    gain_query, gain_key = near[0], near[1]

    gathered = jnp.zeros((rows, n * width), BF16)
    order = piece_order()
    for k, piece in zip(order, gather_pieces(inputs, True)):
        gathered = lax.dynamic_update_slice(gathered, piece, (0, (mine ^ k) * width))
    grad_out = jnp.zeros((own, n * width), BF16)
    for k in range(n):
        piece = lax.dynamic_slice_in_dim(cotangent, (mine ^ k) * own, own, axis=0)
        piece = swap(piece, k) if k else piece
        grad_out = lax.dynamic_update_slice(grad_out, piece, (0, (mine ^ k) * width))

    offset = lax.axis_index("ctx") * rows
    token_place = offset + jnp.arange(rows, dtype=jnp.int32)
    begins = doc_begins(doc_lengths[0], token_place)
    cosine, sine = turn_tables(token_place - begins)
    start = begins - offset

    qkv = matmul(gathered, w_qkv)
    queries, key_proj = qkv[:, :width], qkv[:, width : 2 * width]
    squares = axis_total(
        jnp.stack([jnp.sum(queries * queries, axis=1), jnp.sum(key_proj * key_proj, axis=1)]),
        "tensor",
    )
    qk_rs = lax.rsqrt(squares / D + NORM_EPS).T
    qk_rs = after(qk_rs, grad_out)
    query_low, key_low, value_low = rope(qkv, qk_rs, gain_query, gain_key, cosine, sine)
    all_keys = jnp.concatenate([passed_along(key_low, "ctx", 1), key_low], axis=0)
    all_values = jnp.concatenate([passed_along(value_low, "ctx", 1), value_low], axis=0)
    attn_low, log_total = attend(query_low, all_keys, all_values, start)

    parts = [
        by_columns(lax.dynamic_slice_in_dim(attn_low, (mine ^ k) * own, own, axis=0), w_out)
        for k in order
    ]
    branch = add_up(scatter_pieces(parts))
    branch_rs = lax.rsqrt(jnp.mean(branch * branch, axis=1, keepdims=True) + NORM_EPS)
    my_rows = lax.dynamic_slice_in_dim(gathered, mine * own, own, axis=0)
    hidden_in = my_rows.astype(F32) + branch * branch_rs * gain_attn
    hidden_low = jnp.concatenate(gather_pieces(hidden_in.astype(BF16), True), axis=0)
    gate_and_up, act_low = gate_up(hidden_low, up_full, owned)
    result = functools.partial(result_step, owners=down_full.shape[0], gain=gain_mlp)
    terms, done, near = [], (), []
    for array, place, count, _ in down_pieces:
        array = after(array, *done)
        piece = lambda x, *rest, array=array: down(x, array, place, count, *rest)
        if n != 4:
            parts = piece(act_low, 0, rows, F32)
            terms.append(scatter_pieces([parts[k * own : (k + 1) * own] for k in range(n)]))
            continue
        last = piece(act_low, own, own, BF16, 2)
        passing = send_far(last)
        pair = piece(after(act_low, *last, *near), 2 * own, 2 * own, F32)
        first = piece(after(act_low, pair), 0, own, F32)
        if len(terms) + 1 < len(down_pieces):
            sent, near = send_near(pair, passing)
            terms.append([first] + near)
            done = (first, sent)
    if n == 4:
        terms.append([first] + send_near(pair, passing)[1])
        half = own // 2
        steps = [
            result(terms, other=grad_out, begin=i * half, rows=half, forward=False) for i in range(2)
        ]
        halves = [gather_pieces(step[0]) for step in steps]
        result_blocks = [part[i] for group in ((0,), (1, 2), (3,), (4,)) for part in halves for i in group]
        gain_mlp_parts = steps[0][1] + steps[1][1]
    else:
        grad_result, gain_mlp_parts = result(
            terms, other=grad_out, begin=0, rows=own, forward=False
        )
        result_blocks = gather_pieces(grad_result)
    (output_low,) = result(terms, other=hidden_in, begin=0, rows=own, forward=True)
    grad_gain_mlp = jnp.sum(gain_mlp_parts, axis=(0, 1))
    down_sums = contract_rows(jnp.concatenate(result_blocks, axis=0), act_low).astype(BF16)
    owned_down = scatter_owned(down_sums, owners)
    grad_gate_up = act_back(result_blocks, down_pieces, after(gate_and_up, down_sums))
    ctx = lax.axis_index("ctx")
    if n == 4:
        last = hidden_back(grad_gate_up, up_full, owned, own, own, BF16, 2)
        passing = send_far(last)
        given = weight_half(hidden_low, after(grad_gate_up, *last), 1 - ctx)
        pair = hidden_back(after(grad_gate_up, given), up_full, owned, 2 * own, 2 * own, F32)
        sent, near = send_near(pair, passing)
        first = hidden_back(after(grad_gate_up, sent), up_full, owned, 0, own, F32)
        terms = [first] + near
    else:
        first = hidden_back(grad_gate_up, up_full, owned, 0, rows, F32)
        given = weight_half(hidden_low, after(grad_gate_up, first), 1 - ctx)
        terms = scatter_pieces([first[k * own : (k + 1) * own] for k in range(n)])
    up_sums = weight_half(hidden_low, grad_gate_up, ctx, other_core(given))
    grad_hidden, grad_branch, gain_attn_parts = branch_back(
        terms, after(branch, up_sums), grad_out, gain_attn
    )
    grad_gain_attn = jnp.sum(gain_attn_parts, axis=(0, 1))
    owned_up = scatter_owned(merged(after(up_sums, owned_down)))
    grad_branch_all = jnp.zeros((rows, n * width), BF16)
    for k, piece in zip(order, gather_pieces(grad_branch, True)):
        grad_branch_all = lax.dynamic_update_slice(grad_branch_all, piece, ((mine ^ k) * own, 0))
    down_new = adam(owned_down, mlp_weights, mlp_first, mlp_second, 2, 1)
    grad_mixed = matmul(after(grad_branch_all, down_new[0], output_low), w_out).astype(BF16)
    dq, dkp, dvp, dk, dv = attend_back(
        query_low, all_keys, all_values, grad_mixed, log_total.T, start
    )
    back_key = passed_along(dkp, "ctx", -1)
    back_value = passed_along(dvp, "ctx", -1)
    given = other_core(weight_half(after(grad_branch_all, dkp), attn_low, 1 - ctx))

    weighted_q, weighted_k, grad_v, inner, gain_parts = unrope(
        dq, dk, dv, back_key, back_value, qkv, qk_rs, gain_query, gain_key, cosine, sine
    )
    out_sums = weight_half(after(grad_branch_all, inner), attn_low, ctx, given)
    inner = after(axis_total(inner.T, "tensor").T, out_sums)
    grad_q = qk_rs[:, :1] * weighted_q - queries * qk_rs[:, :1] ** 3 * inner[:, :1] / D
    grad_k = qk_rs[:, 1:] * weighted_k - key_proj * qk_rs[:, 1:] ** 3 * inner[:, 1:] / D
    grad_qkv = jnp.concatenate([grad_q.astype(BF16), grad_k.astype(BF16), grad_v], axis=1)
    given = weight_half(gathered, grad_qkv, 1 - ctx)
    near_inputs = lambda source, distances, *rest: input_back(
        source, attn_full, grad_hidden, mine, distances, *rest
    )
    if n == 4:
        last = near_inputs(after(grad_qkv, given), order[1:2], BF16, 2)
        passing = send_far(last)
        attn_sums = weight_half(
            gathered, after(grad_qkv, *last), ctx, other_core(given), out_sums
        )
        pair = near_inputs(after(grad_qkv, attn_sums), order[2:], F32)
        sent, near = send_near(pair, passing)
    else:
        attn_sums = weight_half(gathered, grad_qkv, ctx, other_core(given), out_sums)
        parts = near_inputs(grad_qkv, order, F32)
        sent = parts
    owned_attn = scatter_owned(merged(after(attn_sums, owned_up)))
    new_mlp, mlp_one, mlp_two = adam(
        after(owned_up, sent), mlp_weights, mlp_first, mlp_second, 0, 2, down_new
    )
    output_low = after(output_low, new_mlp)
    output = jnp.zeros((rows, width), BF16)
    for k in range(n):
        piece = lax.dynamic_slice_in_dim(output_low, (mine ^ k) * width, width, axis=1)
        piece = swap(piece, k) if k else piece
        output = lax.dynamic_update_slice(output, piece, ((mine ^ k) * own, 0))
    if n == 4:
        grad_inputs = add_up([near_inputs(after(grad_qkv, new_mlp), order[:1], F32)] + near)
    else:
        grad_inputs = add_up(scatter_pieces([parts[k * rows : (k + 1) * rows] for k in range(n)]))

    wide = jnp.stack([grad_gain_attn, grad_gain_mlp])
    near = lax.dynamic_slice_in_dim(wide, mine * width, width, axis=1)
    for k in range(1, n):
        near = near + swap(lax.dynamic_slice_in_dim(wide, (mine ^ k) * width, width, axis=1), k)
    gain_sums = jnp.concatenate([jnp.sum(gain_parts, axis=0), near])
    gain_sums = axis_total(axis_total(after(gain_sums, sent), "ctx"), "dp")
    share = norm_gains.shape[1]
    place = (lax.axis_index("dp") * lax.axis_size("ctx") + lax.axis_index("ctx")) * share
    gain_grad = lax.dynamic_slice_in_dim(gain_sums, place, share, axis=1)

    new_attn, attn_one, attn_two = adam(owned_attn, attn_weights, attn_first, attn_second, 0, 4)
    new_gains, gain_one, gain_two = adam_step(
        norm_gains, gain_grad, gain_first, gain_second, GAIN_RATE, 0.0
    )
    return (
        output,
        grad_inputs,
        new_attn,
        attn_one,
        attn_two,
        new_mlp,
        mlp_one,
        mlp_two,
        new_gains,
        gain_one,
        gain_two,
    )


def solution(mesh):
    return jax.shard_map(
        body,
        mesh=mesh,
        in_specs=(
            P(("dp", "ctx"), "tensor"),
            P(("dp", "ctx"), "tensor"),
            P("dp", None),
            P(None, ("dp", "ctx"), "tensor"),
            P(None, ("dp", "ctx"), "tensor"),
            P(None, ("tensor", "dp", "ctx")),
            P(None, ("dp", "ctx"), "tensor"),
            P(None, ("dp", "ctx"), "tensor"),
            P(None, ("dp", "ctx"), "tensor"),
            P(None, ("dp", "ctx"), "tensor"),
            P(None, ("tensor", "dp", "ctx")),
            P(None, ("tensor", "dp", "ctx")),
        ),
        out_specs=(
            P(("dp", "ctx"), "tensor"),
            P(("dp", "ctx"), "tensor"),
            P(None, ("dp", "ctx"), "tensor"),
            P(None, ("dp", "ctx"), "tensor"),
            P(None, ("dp", "ctx"), "tensor"),
            P(None, ("dp", "ctx"), "tensor"),
            P(None, ("dp", "ctx"), "tensor"),
            P(None, ("dp", "ctx"), "tensor"),
            P(None, ("tensor", "dp", "ctx")),
            P(None, ("tensor", "dp", "ctx")),
            P(None, ("tensor", "dp", "ctx")),
        ),
        check_vma=False,
    )
```
